512 devices in a mesh: dp: 32 (over z, x_hi), seq: 16 (over y, x_lo, core).
Axes of the slice: x: 4 (x_hi: 2, x_lo: 2; x = x_hi * 2 + x_lo), y: 4, z: 16, core: 2. Of those that a mesh axis runs over, the one named last changes fastest.
Arguments:
- attn_queries: bfloat16 [32, 2048, 4096], P('dp', 'seq'), may hold values from -5 to 5
- attention_key_rows: bfloat16 [32, 2048, 512], P('dp', 'seq'), may hold values from -5 to 5
- attention_value_rows: bfloat16 [32, 2048, 512], P('dp', 'seq'), may hold values from -6 to 6
- score_gain: float32 [32], replicated, may hold values from 0.6 to 1.4
- attn_grad: bfloat16 [32, 2048, 4096], P('dp', 'seq'), may hold values from -15 to 15
- segment_ids: int32 [32, 2048], P('dp'), may hold values from 0 to 31, never falling along the last dimension, each value on 1 to 256 neighbouring positions
Outputs:
- grad_queries: bfloat16 [32, 2048, 4096], P('dp', 'seq')
- key_gradient_rows: bfloat16 [32, 2048, 512], P('dp', 'seq')
- value_gradient_rows: bfloat16 [32, 2048, 512], P('dp', 'seq')
- grad_gain: float32 [32], P('seq')
The draws below stay inside these ranges and needn't reach their ends.
Inputs may be any that keep to these rules, and one draw needn't show every extreme that they name: `segment_ids`: segment numbers never fall along a sequence; each document holds 1 to 256 positions, one exactly that many.
All inputs are finite; a program needn't handle non-finite values.
Results may differ from the reference program's by a relative error of at most 0.007.
Values may be sent and summed in bfloat16 or wider, within the bound.
A program may use at most 64 MiB of HBM per device.

```python
import math
import jax
import jax.numpy as jnp
import numpy as np
from jax import lax

QUERY_HEADS = 32
KEY_VALUE_HEADS = 4
HEAD_SIZE = 128
BATCH_SEQUENCES = 32
SEQUENCE_TOKENS = 2048


def row_factor(row_count, highest):
    return highest ** (jnp.arange(row_count, dtype=jnp.float32) / max(row_count - 1, 1))


def draw_attn_grad(key, part):
    key = jax.random.fold_in(key, 22)
    entry_items = jnp.clip(jax.random.normal(key, (BATCH_SEQUENCES, SEQUENCE_TOKENS, QUERY_HEADS * HEAD_SIZE), jnp.float32), -5.0, 5.0)
    factor = row_factor(BATCH_SEQUENCES, 3.0)
    return (entry_items * factor[:, None, None]).astype(jnp.bfloat16)


def draw_attn_queries(key, part):
    key = jax.random.fold_in(key, 31)
    random_seed_key = jax.random.fold_in(key, 0)
    entry_items = jnp.clip(jax.random.normal(random_seed_key, (BATCH_SEQUENCES, SEQUENCE_TOKENS, QUERY_HEADS * HEAD_SIZE), jnp.float32), -5.0, 5.0)
    return entry_items.astype(jnp.bfloat16)


def draw_attention_key_rows(key, part):
    key = jax.random.fold_in(key, 32)
    random_seed_key = jax.random.fold_in(key, 0)
    entry_items = jnp.clip(jax.random.normal(random_seed_key, (BATCH_SEQUENCES, SEQUENCE_TOKENS, KEY_VALUE_HEADS * HEAD_SIZE), jnp.float32), -5.0, 5.0)
    return entry_items.astype(jnp.bfloat16)


def steps_of(own_key, shape, shards, least, high):
    loudness = 1.0
    for dim, parts in shards:
        heights = jax.random.uniform(jax.random.fold_in(jax.random.fold_in(own_key, 6), dim), (parts,), jnp.float32, least / len(shards), high / len(shards))
        loudness = loudness * jnp.repeat(jnp.exp(heights), shape[dim] // parts).reshape((-1,) + (1,) * (len(shape) - 1 - dim))
    return loudness


def length_profile(amount, total, limit, skew):
    loads = [(1 << 20) // math.isqrt(standing ** skew) + 1 for standing in range(2, amount + 1)]
    rest, holding = total - limit - (amount - 1), [1] * (amount - 1)
    while rest > 0:
        movable = [i for i in range(amount - 1) if holding[i] < limit]
        pool, left = sum([loads[i] for i in movable]), rest
        for i in movable:
            extra = min(limit - holding[i], max(1, left * loads[i] // pool), rest)
            holding[i] = holding[i] + extra
            rest = rest - extra
    return np.array([limit] + holding)


def uneven(key, amount, total, limit, lean):
    if amount == 2:
        one = jax.random.randint(key, (), max(1, total - limit), min(limit, total - 1) + 1)
        return jnp.stack([one, total - one])
    tallies = jnp.asarray(length_profile(amount, total, limit, lean), jnp.int32)
    couples = (amount - 1) // 2
    giver, sink = tallies[1:1 + 2 * couples:2], tallies[2:2 + 2 * couples:2]
    room = jnp.minimum(giver - 1, limit - sink)
    moved = jax.random.randint(jax.random.fold_in(key, 1), (couples,), 0, 1 << 20) % (room + 1)
    tallies = tallies.at[1:1 + 2 * couples:2].set(giver - moved).at[2:2 + 2 * couples:2].set(sink + moved)
    return tallies[jax.random.permutation(jax.random.fold_in(key, 2), amount)]


def bell_draw(own_key, extent, scale, most, cuts=(), kind=jnp.bfloat16):
    factor_of = steps_of(own_key, extent, cuts, -0.22, 0.18) if cuts else 1.0
    array = jax.random.normal(own_key, extent, jnp.float32) * scale * factor_of
    return jnp.minimum(jnp.maximum(array, -most), most).astype(kind)


def setup_inputs(seed: int = 0) -> dict:
    key_of = jax.random.split(jax.random.key(seed), 7)
    attn_queries = draw_attn_queries(jax.random.fold_in(key_of[6], 71), 0)
    attention_key_rows = draw_attention_key_rows(jax.random.fold_in(key_of[6], 71), 0)
    attention_value_rows = bell_draw(key_of[2], (BATCH_SEQUENCES, SEQUENCE_TOKENS, KEY_VALUE_HEADS * HEAD_SIZE), 1.0, 6.0, ((0, 32), (1, 16)))
    score_gain = jnp.clip(jax.random.uniform(key_of[3], (QUERY_HEADS,), jnp.float32, 0.6, 1.4), 0.6, 1.4)
    attn_grad = draw_attn_grad(jax.random.fold_in(key_of[6], 71), 0)
    segment_ids = jax.vmap(lambda own: jnp.searchsorted(jnp.cumsum(uneven(own, max(4, SEQUENCE_TOKENS // 64), SEQUENCE_TOKENS, min(256, SEQUENCE_TOKENS // 2), 2)), jnp.arange(SEQUENCE_TOKENS), side="right"))(jax.random.split(key_of[5], BATCH_SEQUENCES)).reshape((BATCH_SEQUENCES, SEQUENCE_TOKENS)).astype(jnp.int32)
    return dict(attn_queries=attn_queries, attention_key_rows=attention_key_rows, attention_value_rows=attention_value_rows, score_gain=score_gain, attn_grad=attn_grad, segment_ids=segment_ids)


def head_backward(queries_one, keys_one, values_one, grad_one, gain_one, doc_ids):
    sequence_length, width = queries_one.shape
    block_rows = min(512, sequence_length)
    reach = min(256, sequence_length // 2)
    places = jnp.arange(sequence_length, dtype=jnp.int32)
    scale = width ** -0.5
    rows_dims = (((0,), (0,)), ((), ()))
    key_gradient_rows = jnp.zeros((sequence_length, width), jnp.float32)
    grad_vals = jnp.zeros((sequence_length, width), jnp.float32)
    gain_total = jnp.zeros((), jnp.float32)
    pieces = []
    for begin_row in range(0, sequence_length, block_rows):
        end_row = begin_row + block_rows
        low_row = max(0, begin_row - reach)
        rows_query = queries_one[begin_row:end_row]
        rows_grad = grad_one[begin_row:end_row]
        keys_part = keys_one[low_row:end_row]
        values_part = values_one[low_row:end_row]
        allowed = (doc_ids[begin_row:end_row, None] == doc_ids[None, low_row:end_row]) & (places[begin_row:end_row, None] >= places[None, low_row:end_row])
        raw = jnp.dot(rows_query, keys_part.T, preferred_element_type=jnp.float32) * scale
        dprob = jnp.dot(rows_grad, values_part.T, preferred_element_type=jnp.float32)
        masked = jnp.where(allowed, gain_one * raw, -1e30)
        highest = jnp.max(masked, axis=-1, keepdims=True)
        weights = jnp.exp(masked - highest) * allowed
        normed = weights / jnp.sum(weights, axis=-1, keepdims=True)
        normed_low = normed.astype(jnp.bfloat16)
        delta = jnp.sum(normed * dprob, axis=-1, keepdims=True)
        dscore = normed * (dprob - delta)
        gain_total = gain_total + jnp.sum(dscore * raw)
        dscaled = (dscore * (gain_one * scale)).astype(jnp.bfloat16)
        grad_vals = grad_vals.at[low_row:end_row].add(lax.dot_general(normed_low, rows_grad, rows_dims, preferred_element_type=jnp.float32))
        pieces.append(jnp.dot(dscaled, keys_part, preferred_element_type=jnp.float32))
        key_gradient_rows = key_gradient_rows.at[low_row:end_row].add(lax.dot_general(dscaled, rows_query, rows_dims, preferred_element_type=jnp.float32))
    return jnp.concatenate(pieces, axis=0), key_gradient_rows, grad_vals, gain_total


def reference(attn_queries, attention_key_rows, attention_value_rows, score_gain, attn_grad, segment_ids):
    query_head_cluster = QUERY_HEADS // KEY_VALUE_HEADS

    def one_sequence(item):
        queries, incoming_keys, incoming_values, grad_attn, doc_ids = item
        sequence_length = queries.shape[0]
        query_heads = jnp.transpose(queries.reshape(sequence_length, QUERY_HEADS, HEAD_SIZE), (1, 0, 2))
        grad_heads = jnp.transpose(grad_attn.reshape(sequence_length, QUERY_HEADS, HEAD_SIZE), (1, 0, 2))
        head_key_rows = jnp.transpose(incoming_keys.reshape(sequence_length, KEY_VALUE_HEADS, HEAD_SIZE), (1, 0, 2))
        head_value_rows = jnp.transpose(incoming_values.reshape(sequence_length, KEY_VALUE_HEADS, HEAD_SIZE), (1, 0, 2))
        group_of = jnp.arange(QUERY_HEADS, dtype=jnp.int32) // query_head_cluster

        def one_head(piece):
            single_query, single_grad, single_gain, group_index = piece
            return head_backward(single_query, head_key_rows[group_index], head_value_rows[group_index], single_grad, single_gain, doc_ids)

        grad_query, key_gradient_part, value_gradient_part, gain_part = lax.map(one_head, (query_heads, grad_heads, score_gain, group_of))
        key_gradient_total = jnp.sum(key_gradient_part.reshape(KEY_VALUE_HEADS, query_head_cluster, sequence_length, HEAD_SIZE), axis=1)
        value_gradient_total = jnp.sum(value_gradient_part.reshape(KEY_VALUE_HEADS, query_head_cluster, sequence_length, HEAD_SIZE), axis=1)
        return (
            jnp.transpose(grad_query, (1, 0, 2)).reshape(sequence_length, QUERY_HEADS * HEAD_SIZE).astype(jnp.bfloat16),
            jnp.transpose(key_gradient_total, (1, 0, 2)).reshape(sequence_length, KEY_VALUE_HEADS * HEAD_SIZE).astype(jnp.bfloat16),
            jnp.transpose(value_gradient_total, (1, 0, 2)).reshape(sequence_length, KEY_VALUE_HEADS * HEAD_SIZE).astype(jnp.bfloat16),
            gain_part)

    results = lax.map(one_sequence, (attn_queries, attention_key_rows, attention_value_rows, attn_grad, segment_ids))
    factor = 1.0 / (BATCH_SEQUENCES * SEQUENCE_TOKENS)
    return (results[0], results[1], results[2], jnp.sum(results[3], axis=0) * factor)
```

```python
import functools
import math

import jax
import jax.numpy as jnp
from jax import lax
from jax.experimental import pallas as pl
from jax.experimental.pallas import tpu as pltpu
from jax.sharding import PartitionSpec as P

QUERY_HEADS = 32
KEY_VALUE_HEADS = 4
HEAD_SIZE = 128
GROUP = QUERY_HEADS // KEY_VALUE_HEADS
BLOCK = 128
HALF = 64
WINDOW = 320
QUAD = 4
LANES = QUAD * HALF
CHUNK = 64
LOG2E = math.log2(math.e)
SCALE = HEAD_SIZE ** -0.5
BF16 = jnp.bfloat16
F32 = jnp.float32
NT = (((1,), (1,)), ((), ()))
TN = (((0,), (0,)), ((), ()))


def fold_rows(x):
    return jnp.sum(x.reshape(x.shape[0] // 8, 8, x.shape[1]), axis=0)


def kernel(
    seq_size, dp_size, factor,
    q_hbm, k_hbm, v_hbm, gain_ref, g_hbm, seg_ref,
    dq_hbm, dk_hbm, dv_hbm, gain_out,
    qg, kv, ret_send, ret, acc, dq_buf, dkv_buf, seg_rows, bias,
    s_buf, dp_buf, y_buf, p_buf, ds_buf,
    g_part, g_in1, g_sum, g_in2,
    in_sem, own_sem, halo_send, halo_recv, back_send, back_recv, dq_sem, dkv_sem, gain_sem,
):
    me = lax.axis_index("seq")
    row = lax.axis_index("dp")

    def seq_at(offset):
        return lax.rem(me + offset, seq_size)

    def load(j, carry):
        wide = pl.ds(pl.multiple_of(j * (GROUP * HEAD_SIZE), GROUP * HEAD_SIZE), GROUP * HEAD_SIZE)
        thin = pl.ds(pl.multiple_of(j * HEAD_SIZE, HEAD_SIZE), HEAD_SIZE)
        pltpu.make_async_copy(k_hbm.at[:, thin], kv.at[j, 0, pl.ds(2 * BLOCK, BLOCK)], own_sem.at[j]).start()
        pltpu.make_async_copy(v_hbm.at[:, thin], kv.at[j, 1, pl.ds(2 * BLOCK, BLOCK)], own_sem.at[j]).start()
        pltpu.make_async_copy(q_hbm.at[:, wide], qg.at[j, 0], in_sem.at[j]).start()
        pltpu.make_async_copy(g_hbm.at[:, wide], qg.at[j, 1], in_sem.at[j]).start()
        return carry

    barrier = pltpu.get_barrier_semaphore()

    def greet_seq(i, carry):
        pl.semaphore_signal(barrier, inc=1, device_id={"seq": seq_at(i)}, device_id_type=pl.DeviceIdType.MESH)
        return carry

    def greet_dp(i, carry):
        pl.semaphore_signal(
            barrier, inc=1, device_id={"dp": lax.rem(row + i, dp_size)}, device_id_type=pl.DeviceIdType.MESH
        )
        return carry

    lax.fori_loop(1, seq_size, greet_seq, 0)
    lax.fori_loop(1, dp_size, greet_dp, 0)
    lax.fori_loop(0, KEY_VALUE_HEADS, load, 0)
    pl.semaphore_wait(barrier, seq_size + dp_size - 2)

    def halo_start(j):
        thin = pl.ds(pl.multiple_of(j * HEAD_SIZE, HEAD_SIZE), HEAD_SIZE)
        for which, source in enumerate((k_hbm, v_hbm)):
            for hop in (1, 2):
                pltpu.make_async_remote_copy(
                    src_ref=source.at[:, thin],
                    dst_ref=kv.at[j, which, pl.ds((2 - hop) * BLOCK, BLOCK)],
                    send_sem=halo_send.at[j],
                    recv_sem=halo_recv.at[j],
                    device_id={"seq": seq_at(hop)},
                    device_id_type=pl.DeviceIdType.MESH,
                ).start()

    halo_start(0)

    for b in range(3):
        place = pl.multiple_of(seq_at(seq_size - 2 + b) * BLOCK, BLOCK)
        ids = seg_ref[:, pl.ds(place, BLOCK)].astype(F32)
        seg_rows[pl.ds(b * BLOCK, BLOCK)] = jnp.transpose(jnp.broadcast_to(ids, (BLOCK, BLOCK)))
    own_ids = jnp.broadcast_to(
        seg_ref[:, pl.ds(pl.multiple_of(me * BLOCK, BLOCK), BLOCK)].astype(F32), (8, BLOCK)
    )
    turned = pltpu.roll(own_ids, HALF, 1)
    lane8 = lax.broadcasted_iota(jnp.int32, (8, BLOCK), 1)
    key_place = lax.broadcasted_iota(jnp.int32, (WINDOW, BLOCK), 0)
    lane = lax.broadcasted_iota(jnp.int32, (WINDOW, BLOCK), 1)
    for half in range(2):
        ids = jnp.where((lane8 < HALF) == (half == 0), own_ids, turned)[0:1]
        s_at = (me - 2) * BLOCK + half * HALF + key_place
        t_at = me * BLOCK + half * HALF + jnp.where(lane < HALF, lane, lane - HALF)
        allowed = (seg_rows[pl.ds(half * HALF, WINDOW)] == ids) & (s_at <= t_at) & (s_at >= 0)
        bias[half] = jnp.where(allowed, 0.0, -1e30)

    lane_wide = lax.broadcasted_iota(jnp.int32, (1, LANES), 1)

    def back_copy(j, hop):
        return pltpu.make_async_remote_copy(
            src_ref=ret_send.at[j, 2 - hop],
            dst_ref=ret.at[j, 2 - hop],
            send_sem=back_send.at[j],
            recv_sem=back_recv.at[j],
            device_id={"seq": seq_at(seq_size - hop)},
            device_id_type=pl.DeviceIdType.MESH,
        )

    def whole_back(j):
        return pltpu.make_async_remote_copy(
            src_ref=ret_send.at[j],
            dst_ref=ret.at[j],
            send_sem=back_send.at[j],
            recv_sem=back_recv.at[j],
            device_id={"seq": seq_at(1)},
            device_id_type=pl.DeviceIdType.MESH,
        )

    def dkv_out(j, which, target):
        thin = pl.ds(pl.multiple_of(j * HEAD_SIZE, HEAD_SIZE), HEAD_SIZE)
        return pltpu.make_async_copy(dkv_buf.at[j, which], target.at[:, thin], dkv_sem.at[j, which])

    def finish(j):
        whole_back(j).wait_recv()
        for which, target in enumerate((dk_hbm, dv_hbm)):
            total = (
                acc[j, which, pl.ds(2 * BLOCK, BLOCK)]
                + ret[j, 1, which].astype(F32)
                + ret[j, 0, which].astype(F32)
            )
            dkv_buf[j, which] = total.astype(BF16)
            dkv_out(j, which, target).start()

    def dq_out(j):
        wide = pl.ds(pl.multiple_of(j * (GROUP * HEAD_SIZE), GROUP * HEAD_SIZE), GROUP * HEAD_SIZE)
        return pltpu.make_async_copy(dq_buf.at[j], dq_hbm.at[:, wide], dq_sem.at[j])

    def gain_copy1(target):
        return pltpu.make_async_remote_copy(
            src_ref=g_part.at[target],
            dst_ref=g_in1.at[lax.rem(me - target + seq_size, seq_size) - 1],
            send_sem=gain_sem.at[0],
            recv_sem=gain_sem.at[1],
            device_id={"seq": target},
            device_id_type=pl.DeviceIdType.MESH,
        )

    units = [(half, quad) for half in range(2) for quad in range(GROUP // QUAD)]

    def group(j, carry):
        pltpu.make_async_remote_copy(
            src_ref=kv.at[j, :, pl.ds(0, 2 * BLOCK)],
            dst_ref=kv.at[j, :, pl.ds(0, 2 * BLOCK)],
            send_sem=halo_send.at[j],
            recv_sem=halo_recv.at[j],
            device_id={"seq": seq_at(1)},
            device_id_type=pl.DeviceIdType.MESH,
        ).wait_recv()

        @pl.when(j < KEY_VALUE_HEADS - 1)
        def _():
            halo_start(j + 1)

        own = kv.at[j, :, pl.ds(2 * BLOCK, BLOCK)]
        pltpu.make_async_copy(own, own, own_sem.at[j]).wait()
        pltpu.make_async_copy(qg.at[j], qg.at[j], in_sem.at[j]).wait()

        def stack(which, half, quad):
            return jnp.concatenate(
                [
                    qg[j, which, pl.ds(half * HALF, HALF), pl.ds((quad * QUAD + h) * HEAD_SIZE, HEAD_SIZE)]
                    for h in range(QUAD)
                ],
                axis=0,
            )

        def first(u):
            half, quad = units[u]
            rows = pl.ds(half * HALF, WINDOW)
            s_buf[u] = lax.dot_general(kv[j, 0, rows], stack(0, half, quad), NT, preferred_element_type=F32)
            dp_buf[u] = lax.dot_general(kv[j, 1, rows], stack(1, half, quad), NT, preferred_element_type=F32)

        def middle(u):
            half, quad = units[u]
            gains = [gain_ref[j * GROUP + quad * QUAD + h] for h in range(QUAD)]
            gain = jnp.where(
                lane_wide < 2 * HALF,
                jnp.where(lane_wide < HALF, gains[0], gains[1]),
                jnp.where(lane_wide < 3 * HALF, gains[2], gains[3]),
            )
            to_score = gain * (SCALE * LOG2E)
            to_grad = gain * SCALE
            chunks = [pl.ds(c, CHUNK) for c in range(0, WINDOW, CHUNK)]
            top = jnp.full((8, LANES), -3e38, F32)
            for rows in chunks:
                shade = bias[half, rows]
                y = s_buf[u, rows] * to_score + jnp.concatenate([shade, shade], axis=1)
                y_buf[u, rows] = y
                top = jnp.maximum(top, jnp.max(y.reshape(CHUNK // 8, 8, LANES), axis=0))
            top = jnp.max(top, axis=0, keepdims=True)
            total = jnp.zeros((8, LANES), F32)
            dot = jnp.zeros((8, LANES), F32)
            for rows in chunks:
                e = jnp.exp2(y_buf[u, rows] - top)
                y_buf[u, rows] = e
                total = total + fold_rows(e)
                dot = dot + fold_rows(e * dp_buf[u, rows])
            inverse = 1.0 / jnp.sum(total, axis=0, keepdims=True)
            delta = jnp.sum(dot, axis=0, keepdims=True) * inverse
            spread = jnp.zeros((8, LANES), F32)
            for rows in chunks:
                p = y_buf[u, rows] * inverse
                dscore = p * (dp_buf[u, rows] - delta)
                spread = spread + fold_rows(dscore * s_buf[u, rows])
                p_buf[u, rows] = p.astype(BF16)
                ds_buf[u, rows] = (dscore * to_grad).astype(BF16)
            return jnp.sum(spread, axis=0, keepdims=True) * (SCALE * factor)

        def last(u):
            half, quad = units[u]
            rows = pl.ds(half * HALF, WINDOW)
            ds = ds_buf[u]
            dk_new = jnp.dot(ds, stack(0, half, quad), preferred_element_type=F32)
            dv_new = jnp.dot(p_buf[u], stack(1, half, quad), preferred_element_type=F32)
            acc[j, 0, rows] += dk_new
            acc[j, 1, rows] += dv_new
            dq = lax.dot_general(ds, kv[j, 0, rows], TN, preferred_element_type=F32).astype(BF16)
            for h in range(QUAD):
                dq_buf[
                    j, pl.ds(half * HALF, HALF), pl.ds((quad * QUAD + h) * HEAD_SIZE, HEAD_SIZE)
                ] = dq[h * HALF:(h + 1) * HALF]

        acc[j] = jnp.zeros((2, 3 * BLOCK, HEAD_SIZE), F32)
        first(0)
        terms = []
        for u in range(len(units)):
            if u + 1 < len(units):
                first(u + 1)
            terms.append(middle(u))
            last(u)

        for place in range(2):
            for which in range(2):
                ret_send[j, place, which] = acc[j, which, pl.ds(place * BLOCK, BLOCK)].astype(BF16)
            back_copy(j, 2 - place).start()
        dq_out(j).start()

        per = GROUP // QUAD
        for quad in range(per):
            both = terms[quad] + terms[per + quad]
            for side in range(2):
                target = j * (GROUP // 2) + quad * 2 + side
                g_part[target] = both[:, side * 2 * HALF:(side + 1) * 2 * HALF]

                @pl.when(target != me)
                def _():
                    gain_copy1(target).start()

        @pl.when(j > 0)
        def _():
            finish(j - 1)

        return carry

    lax.fori_loop(0, KEY_VALUE_HEADS, group, 0)

    def whole_gain(buf, at):
        return pltpu.make_async_remote_copy(
            src_ref=buf,
            dst_ref=buf,
            send_sem=gain_sem.at[at],
            recv_sem=gain_sem.at[at + 1],
            device_id={"seq": seq_at(1)},
            device_id_type=pl.DeviceIdType.MESH,
        )

    whole_gain(g_in1, 0).wait_recv()
    g_sum[0] = g_part[me] + jnp.sum(g_in1[...], axis=0)

    def gain_send2(i, carry):
        pltpu.make_async_remote_copy(
            src_ref=g_sum.at[0],
            dst_ref=g_in2.at[i - 1],
            send_sem=gain_sem.at[2],
            recv_sem=gain_sem.at[3],
            device_id={"dp": lax.rem(row + i, dp_size)},
            device_id_type=pl.DeviceIdType.MESH,
        ).start()
        return carry

    lax.fori_loop(1, dp_size, gain_send2, 0)
    finish(KEY_VALUE_HEADS - 1)
    whole_gain(g_in2, 2).wait_recv()
    lanes = g_sum[0] + jnp.sum(g_in2[...], axis=0)
    lane1 = lax.broadcasted_iota(jnp.int32, (1, 2 * HALF), 1)
    low = jnp.sum(jnp.where(lane1 < HALF, lanes, 0.0), axis=1, keepdims=True)
    high = jnp.sum(jnp.where(lane1 < HALF, 0.0, lanes), axis=1, keepdims=True)
    gain_out[...] = jnp.where(lane1 == 0, low, high)

    whole_gain(g_in1, 0).wait_send()
    whole_gain(g_in2, 2).wait_send()

    def drain(j, carry):
        pltpu.make_async_remote_copy(
            src_ref=kv.at[j, :, pl.ds(0, 2 * BLOCK)],
            dst_ref=kv.at[j, :, pl.ds(0, 2 * BLOCK)],
            send_sem=halo_send.at[j],
            recv_sem=halo_recv.at[j],
            device_id={"seq": seq_at(1)},
            device_id_type=pl.DeviceIdType.MESH,
        ).wait_send()
        whole_back(j).wait_send()
        dq_out(j).wait()
        dkv_out(j, 0, dk_hbm).wait()
        dkv_out(j, 1, dv_hbm).wait()
        return carry

    lax.fori_loop(0, KEY_VALUE_HEADS, drain, 0)


def body(queries, keys, values, score_gain, grad, segment_ids):
    seq_size = lax.axis_size("seq")
    dp_size = lax.axis_size("dp")
    tokens = queries.shape[1]
    factor = 1.0 / (dp_size * tokens * seq_size)
    any_space = pl.BlockSpec(memory_space=pl.ANY)
    heads = KEY_VALUE_HEADS
    units = 2 * GROUP // QUAD
    wide = GROUP * HEAD_SIZE
    dq, dk, dv, gain = pl.pallas_call(
        functools.partial(kernel, seq_size, dp_size, factor),
        out_shape=(
            jax.ShapeDtypeStruct((BLOCK, QUERY_HEADS * HEAD_SIZE), BF16),
            jax.ShapeDtypeStruct((BLOCK, heads * HEAD_SIZE), BF16),
            jax.ShapeDtypeStruct((BLOCK, heads * HEAD_SIZE), BF16),
            jax.ShapeDtypeStruct((1, 2 * HALF), F32),
        ),
        in_specs=[
            any_space,
            any_space,
            any_space,
            pl.BlockSpec(memory_space=pltpu.SMEM),
            any_space,
            pl.BlockSpec(memory_space=pltpu.VMEM),
        ],
        out_specs=(any_space, any_space, any_space, pl.BlockSpec(memory_space=pltpu.VMEM)),
        scratch_shapes=[
            pltpu.VMEM((heads, 2, BLOCK, wide), BF16),
            pltpu.VMEM((heads, 2, 3 * BLOCK, HEAD_SIZE), BF16),
            pltpu.VMEM((heads, 2, 2, BLOCK, HEAD_SIZE), BF16),
            pltpu.VMEM((heads, 2, 2, BLOCK, HEAD_SIZE), BF16),
            pltpu.VMEM((heads, 2, 3 * BLOCK, HEAD_SIZE), F32),
            pltpu.VMEM((heads, BLOCK, wide), BF16),
            pltpu.VMEM((heads, 2, BLOCK, HEAD_SIZE), BF16),
            pltpu.VMEM((3 * BLOCK, BLOCK), F32),
            pltpu.VMEM((2, WINDOW, BLOCK), F32),
            pltpu.VMEM((units, WINDOW, LANES), F32),
            pltpu.VMEM((units, WINDOW, LANES), F32),
            pltpu.VMEM((units, WINDOW, LANES), F32),
            pltpu.VMEM((units, WINDOW, LANES), BF16),
            pltpu.VMEM((units, WINDOW, LANES), BF16),
            pltpu.VMEM((seq_size, 1, 2 * HALF), F32),
            pltpu.VMEM((seq_size - 1, 1, 2 * HALF), F32),
            pltpu.VMEM((1, 1, 2 * HALF), F32),
            pltpu.VMEM((dp_size - 1, 1, 2 * HALF), F32),
            pltpu.SemaphoreType.DMA((heads,)),
            pltpu.SemaphoreType.DMA((heads,)),
            pltpu.SemaphoreType.DMA((heads,)),
            pltpu.SemaphoreType.DMA((heads,)),
            pltpu.SemaphoreType.DMA((heads,)),
            pltpu.SemaphoreType.DMA((heads,)),
            pltpu.SemaphoreType.DMA((heads,)),
            pltpu.SemaphoreType.DMA((heads, 2)),
            pltpu.SemaphoreType.DMA((4,)),
        ],
        compiler_params=pltpu.CompilerParams(
            collective_id=0, has_side_effects=True, vmem_limit_bytes=48 * 1024 * 1024
        ),
        cost_estimate=pl.CostEstimate(
            flops=2 * 5 * BLOCK * WINDOW * HEAD_SIZE * QUERY_HEADS,
            bytes_accessed=4 * 1024 * 1024,
            transcendentals=BLOCK * WINDOW * QUERY_HEADS,
        ),
    )(queries[0], keys[0], values[0], score_gain, grad[0], segment_ids)
    return dq[None], dk[None], dv[None], gain[0, :2]


def solution(mesh):
    return jax.shard_map(
        body,
        mesh=mesh,
        in_specs=(
            P("dp", "seq", None),
            P("dp", "seq", None),
            P("dp", "seq", None),
            P(),
            P("dp", "seq", None),
            P("dp", None),
        ),
        out_specs=(P("dp", "seq", None), P("dp", "seq", None), P("dp", "seq", None), P("seq")),
        check_vma=False,
    )
```

```python
import functools
import math

import jax
import jax.numpy as jnp
from jax import lax
from jax.experimental import pallas as pl
from jax.experimental.pallas import tpu as pltpu
from jax.sharding import PartitionSpec as P

QUERY_HEADS = 32
KEY_VALUE_HEADS = 4
HEAD_SIZE = 128
GROUP = QUERY_HEADS // KEY_VALUE_HEADS
BLOCK = 128
HALF = 64
WINDOW = 320
QUAD = 4
LANES = QUAD * HALF
CHUNK = 64
HAND_PARTS = 4
VMEM_BYTES = 64 * 1024 * 1024
LOG2E = math.log2(math.e)
SCALE = HEAD_SIZE ** -0.5
BF16 = jnp.bfloat16
F32 = jnp.float32
NT = (((1,), (1,)), ((), ()))
TN = (((0,), (0,)), ((), ()))


def fold_rows(x):
    return jnp.sum(x.reshape(x.shape[0] // 8, 8, x.shape[1]), axis=0)


def kernel(
    seq_size, dp_size, factor,
    q_hbm, k_hbm, v_hbm, gain_hbm, g_hbm, seg_hbm,
    dq_hbm, dk_hbm, dv_hbm, gain_out,
    qg, kv, ret_send, ret, acc, dq_buf, dkv_buf, seg_rows, bias,
    s_buf, dp_buf, y_buf, p_buf, ds_buf, seg_ref, gain_ref,
    g_part, g_in1, g_sum, g_in2,
    in_sem, own_sem, halo_send, halo_recv, back_send, back_recv, dq_sem, dkv_sem, gain_sem, small_sem,
):
    me = lax.axis_index("seq")
    row = lax.axis_index("dp")

    def seq_at(offset):
        return lax.rem(me + offset, seq_size)

    def load(j, carry):
        wide = pl.ds(pl.multiple_of(j * (GROUP * HEAD_SIZE), GROUP * HEAD_SIZE), GROUP * HEAD_SIZE)
        thin = pl.ds(pl.multiple_of(j * HEAD_SIZE, HEAD_SIZE), HEAD_SIZE)
        pltpu.make_async_copy(k_hbm.at[:, thin], kv.at[j, 0, pl.ds(2 * BLOCK, BLOCK)], own_sem.at[j]).start()
        pltpu.make_async_copy(v_hbm.at[:, thin], kv.at[j, 1, pl.ds(2 * BLOCK, BLOCK)], own_sem.at[j]).start()
        pltpu.make_async_copy(q_hbm.at[:, wide], qg.at[j, 0], in_sem.at[j]).start()
        pltpu.make_async_copy(g_hbm.at[:, wide], qg.at[j, 1], in_sem.at[j]).start()
        return carry

    barrier = pltpu.get_barrier_semaphore()

    def greet_seq(i, carry):
        pl.semaphore_signal(barrier, inc=1, device_id={"seq": seq_at(i)}, device_id_type=pl.DeviceIdType.MESH)
        return carry

    def greet_dp(i, carry):
        pl.semaphore_signal(
            barrier, inc=1, device_id={"dp": lax.rem(row + i, dp_size)}, device_id_type=pl.DeviceIdType.MESH
        )
        return carry

    lax.fori_loop(1, seq_size, greet_seq, 0)
    lax.fori_loop(1, dp_size, greet_dp, 0)
    seg_copy = pltpu.make_async_copy(seg_hbm, seg_ref, small_sem.at[0])
    gain_copy = pltpu.make_async_copy(gain_hbm, gain_ref, small_sem.at[1])
    seg_copy.start()
    gain_copy.start()
    lax.fori_loop(0, KEY_VALUE_HEADS, load, 0)
    pl.semaphore_wait(barrier, seq_size + dp_size - 2)

    def halo_start(j):
        thin = pl.ds(pl.multiple_of(j * HEAD_SIZE, HEAD_SIZE), HEAD_SIZE)
        for which, source in enumerate((k_hbm, v_hbm)):
            for hop in (1, 2):
                pltpu.make_async_remote_copy(
                    src_ref=source.at[:, thin],
                    dst_ref=kv.at[j, which, pl.ds((2 - hop) * BLOCK, BLOCK)],
                    send_sem=halo_send.at[j],
                    recv_sem=halo_recv.at[j],
                    device_id={"seq": seq_at(hop)},
                    device_id_type=pl.DeviceIdType.MESH,
                ).start()

    def halo_whole(j):
        return pltpu.make_async_remote_copy(
            src_ref=kv.at[j, :, pl.ds(0, 2 * BLOCK)],
            dst_ref=kv.at[j, :, pl.ds(0, 2 * BLOCK)],
            send_sem=halo_send.at[j],
            recv_sem=halo_recv.at[j],
            device_id={"seq": seq_at(1)},
            device_id_type=pl.DeviceIdType.MESH,
        )

    halo_start(0)
    seg_copy.wait()
    gain_copy.wait()

    for b in range(3):
        place = pl.multiple_of(seq_at(seq_size - 2 + b) * BLOCK, BLOCK)
        ids = seg_ref[:, pl.ds(place, BLOCK)].astype(F32)
        seg_rows[pl.ds(b * BLOCK, BLOCK)] = jnp.transpose(jnp.broadcast_to(ids, (BLOCK, BLOCK)))
    own_ids = jnp.broadcast_to(
        seg_ref[:, pl.ds(pl.multiple_of(me * BLOCK, BLOCK), BLOCK)].astype(F32), (8, BLOCK)
    )
    turned = pltpu.roll(own_ids, HALF, 1)
    lane8 = lax.broadcasted_iota(jnp.int32, (8, BLOCK), 1)
    key_place = lax.broadcasted_iota(jnp.int32, (WINDOW, BLOCK), 0)
    lane = lax.broadcasted_iota(jnp.int32, (WINDOW, BLOCK), 1)
    for half in range(2):
        ids = jnp.where((lane8 < HALF) == (half == 0), own_ids, turned)[0:1]
        s_at = (me - 2) * BLOCK + half * HALF + key_place
        t_at = me * BLOCK + half * HALF + jnp.where(lane < HALF, lane, lane - HALF)
        allowed = (seg_rows[pl.ds(half * HALF, WINDOW)] == ids) & (s_at <= t_at) & (s_at >= 0)
        bias[half] = jnp.where(allowed, 0.0, -1e30)

    lane_wide = lax.broadcasted_iota(jnp.int32, (1, LANES), 1)

    def back_copy(j, hop):
        return pltpu.make_async_remote_copy(
            src_ref=ret_send.at[j, 2 - hop],
            dst_ref=ret.at[j, 2 - hop],
            send_sem=back_send.at[j],
            recv_sem=back_recv.at[j],
            device_id={"seq": seq_at(seq_size - hop)},
            device_id_type=pl.DeviceIdType.MESH,
        )

    def whole_back(j):
        return pltpu.make_async_remote_copy(
            src_ref=ret_send.at[j],
            dst_ref=ret.at[j],
            send_sem=back_send.at[j],
            recv_sem=back_recv.at[j],
            device_id={"seq": seq_at(1)},
            device_id_type=pl.DeviceIdType.MESH,
        )

    def dkv_out(j, which, target):
        thin = pl.ds(pl.multiple_of(j * HEAD_SIZE, HEAD_SIZE), HEAD_SIZE)
        return pltpu.make_async_copy(dkv_buf.at[j, which], target.at[:, thin], dkv_sem.at[j, which])

    def finish(j):
        whole_back(j).wait_recv()
        for which, target in enumerate((dk_hbm, dv_hbm)):
            total = (
                acc[j, which, pl.ds(2 * BLOCK, BLOCK)]
                + ret[j, 1, which].astype(F32)
                + ret[j, 0, which].astype(F32)
            )
            dkv_buf[j, which] = total.astype(BF16)
            dkv_out(j, which, target).start()

    def dq_out(j):
        wide = pl.ds(pl.multiple_of(j * (GROUP * HEAD_SIZE), GROUP * HEAD_SIZE), GROUP * HEAD_SIZE)
        return pltpu.make_async_copy(dq_buf.at[j], dq_hbm.at[:, wide], dq_sem.at[j])

    def gain_copy1(target):
        return pltpu.make_async_remote_copy(
            src_ref=g_part.at[target],
            dst_ref=g_in1.at[lax.rem(me - target + seq_size, seq_size) - 1],
            send_sem=gain_sem.at[0],
            recv_sem=gain_sem.at[1],
            device_id={"seq": target},
            device_id_type=pl.DeviceIdType.MESH,
        )

    quads = GROUP // QUAD

    def group(j, carry):
        halo_whole(j).wait_recv()

        @pl.when(j < KEY_VALUE_HEADS - 1)
        def _():
            halo_start(j + 1)

        own = kv.at[j, :, pl.ds(2 * BLOCK, BLOCK)]
        pltpu.make_async_copy(own, own, own_sem.at[j]).wait()
        pltpu.make_async_copy(qg.at[j], qg.at[j], in_sem.at[j]).wait()

        def stack(which, half, heads):
            return jnp.concatenate(
                [
                    qg[j, which, pl.ds(half * HALF, HALF), pl.ds(h * HEAD_SIZE, HEAD_SIZE)]
                    for h in heads
                ],
                axis=0,
            )

        def first(half, quad):
            rows = pl.ds(half * HALF, WINDOW)
            heads = range(quad * QUAD, quad * QUAD + QUAD)
            s_buf[half, quad] = lax.dot_general(
                kv[j, 0, rows], stack(0, half, heads), NT, preferred_element_type=F32
            )
            dp_buf[half, quad] = lax.dot_general(
                kv[j, 1, rows], stack(1, half, heads), NT, preferred_element_type=F32
            )

        def middle(half, quad):
            gains = [gain_ref[j * GROUP + quad * QUAD + h] for h in range(QUAD)]
            gain = jnp.where(
                lane_wide < 2 * HALF,
                jnp.where(lane_wide < HALF, gains[0], gains[1]),
                jnp.where(lane_wide < 3 * HALF, gains[2], gains[3]),
            )
            to_score = gain * (SCALE * LOG2E)
            to_grad = gain * SCALE
            lanes = pl.ds(quad * LANES, LANES)
            chunks = [pl.ds(c, CHUNK) for c in range(0, WINDOW, CHUNK)]
            top = jnp.full((8, LANES), -3e38, F32)
            for rows in chunks:
                shade = bias[half, rows]
                y = s_buf[half, quad, rows] * to_score + jnp.concatenate([shade, shade], axis=1)
                y_buf[half, quad, rows] = y
                top = jnp.maximum(top, jnp.max(y.reshape(CHUNK // 8, 8, LANES), axis=0))
            top = jnp.max(top, axis=0, keepdims=True)
            total = jnp.zeros((8, LANES), F32)
            dot = jnp.zeros((8, LANES), F32)
            for rows in chunks:
                e = jnp.exp2(y_buf[half, quad, rows] - top)
                y_buf[half, quad, rows] = e
                total = total + fold_rows(e)
                dot = dot + fold_rows(e * dp_buf[half, quad, rows])
            inverse = 1.0 / jnp.sum(total, axis=0, keepdims=True)
            delta = jnp.sum(dot, axis=0, keepdims=True) * inverse
            spread = jnp.zeros((8, LANES), F32)
            for rows in chunks:
                p = y_buf[half, quad, rows] * inverse
                dscore = p * (dp_buf[half, quad, rows] - delta)
                spread = spread + fold_rows(dscore * s_buf[half, quad, rows])
                p_buf[half, rows, lanes] = p.astype(BF16)
                ds_buf[half, rows, lanes] = (dscore * to_grad).astype(BF16)
            return jnp.sum(spread, axis=0, keepdims=True) * (SCALE * factor)

        def last(half):
            rows = pl.ds(half * HALF, WINDOW)
            everyone = range(GROUP)
            turned_keys = jnp.transpose(kv[j, 0, rows])
            for quad in range(quads):
                ds = ds_buf[half, :, pl.ds(quad * LANES, LANES)]
                dq = jnp.dot(turned_keys, ds, preferred_element_type=F32).astype(BF16)
                dq = jnp.transpose(dq)
                for h in range(QUAD):
                    dq_buf[
                        j, pl.ds(half * HALF, HALF), pl.ds((quad * QUAD + h) * HEAD_SIZE, HEAD_SIZE)
                    ] = dq[h * HALF:(h + 1) * HALF]
            dk_new = jnp.dot(ds_buf[half], stack(0, half, everyone), preferred_element_type=F32)
            dv_new = jnp.dot(p_buf[half], stack(1, half, everyone), preferred_element_type=F32)
            if half == 0:
                acc[j, 0, rows] = dk_new
                acc[j, 1, rows] = dv_new
                acc[j, :, pl.ds(WINDOW, HALF)] = jnp.zeros((2, HALF, HEAD_SIZE), F32)
            else:
                acc[j, 0, rows] += dk_new
                acc[j, 1, rows] += dv_new

        first(0, 0)
        first(0, 1)
        term00 = middle(0, 0)
        first(1, 0)
        term01 = middle(0, 1)
        first(1, 1)
        last(0)
        term10 = middle(1, 0)
        term11 = middle(1, 1)
        last(1)
        terms = [term00 + term10, term01 + term11]

        for place in range(2):
            for which in range(2):
                ret_send[j, place, which] = acc[j, which, pl.ds(place * BLOCK, BLOCK)].astype(BF16)
            back_copy(j, 2 - place).start()
        dq_out(j).start()

        for quad in range(quads):
            both = terms[quad]
            for side in range(2):
                target = j * (GROUP // 2) + quad * 2 + side
                g_part[target] = both[:, side * 2 * HALF:(side + 1) * 2 * HALF]

                @pl.when(target != me)
                def _():
                    gain_copy1(target).start()

        @pl.when(j > 0)
        def _():
            finish(j - 1)

        return carry

    lax.fori_loop(0, KEY_VALUE_HEADS, group, 0)

    def whole_gain(buf, at):
        return pltpu.make_async_remote_copy(
            src_ref=buf,
            dst_ref=buf,
            send_sem=gain_sem.at[at],
            recv_sem=gain_sem.at[at + 1],
            device_id={"seq": seq_at(1)},
            device_id_type=pl.DeviceIdType.MESH,
        )

    whole_gain(g_in1, 0).wait_recv()
    g_sum[0] = g_part[me] + jnp.sum(g_in1[...], axis=0)

    def gain_send2(i, carry):
        pltpu.make_async_remote_copy(
            src_ref=g_sum.at[0],
            dst_ref=g_in2.at[i - 1],
            send_sem=gain_sem.at[2],
            recv_sem=gain_sem.at[3],
            device_id={"dp": lax.rem(row + i, dp_size)},
            device_id_type=pl.DeviceIdType.MESH,
        ).start()
        return carry

    lax.fori_loop(1, dp_size, gain_send2, 0)
    finish(KEY_VALUE_HEADS - 1)
    whole_gain(g_in2, 2).wait_recv()
    lanes = g_sum[0] + jnp.sum(g_in2[...], axis=0)
    lane1 = lax.broadcasted_iota(jnp.int32, (1, 2 * HALF), 1)
    gain_out[0] = jnp.sum(jnp.where(lane1 < HALF, lanes, 0.0))
    gain_out[1] = jnp.sum(jnp.where(lane1 < HALF, 0.0, lanes))

    whole_gain(g_in1, 0).wait_send()
    whole_gain(g_in2, 2).wait_send()

    def drain(j, carry):
        halo_whole(j).wait_send()
        whole_back(j).wait_send()
        dq_out(j).wait()
        dkv_out(j, 0, dk_hbm).wait()
        dkv_out(j, 1, dv_hbm).wait()
        return carry

    lax.fori_loop(0, KEY_VALUE_HEADS, drain, 0)


def hand_over(dq_in, dk_in, dv_in, gain_in, dq_out, dk_out, dv_out, gain_to, sems):
    copies = [
        pltpu.make_async_copy(dk_in, dk_out, sems.at[HAND_PARTS]),
        pltpu.make_async_copy(dv_in, dv_out, sems.at[HAND_PARTS + 1]),
        pltpu.make_async_copy(gain_in, gain_to, sems.at[HAND_PARTS + 2]),
    ]
    for i in range(HAND_PARTS):
        rows = pl.ds(i * (BLOCK // HAND_PARTS), BLOCK // HAND_PARTS)
        copies.append(pltpu.make_async_copy(dq_in.at[rows], dq_out.at[rows], sems.at[i]))
    for copy in copies:
        copy.start()
    for copy in copies:
        copy.wait()


def body(queries, keys, values, score_gain, grad, segment_ids):
    seq_size = lax.axis_size("seq")
    dp_size = lax.axis_size("dp")
    tokens = queries.shape[1]
    factor = 1.0 / (dp_size * tokens * seq_size)
    hbm = pl.BlockSpec(memory_space=pltpu.HBM)
    heads = KEY_VALUE_HEADS
    quads = GROUP // QUAD
    wide = GROUP * HEAD_SIZE
    dq, dk, dv, gain = pl.pallas_call(
        functools.partial(kernel, seq_size, dp_size, factor),
        out_shape=(
            jax.ShapeDtypeStruct((BLOCK, QUERY_HEADS * HEAD_SIZE), BF16),
            jax.ShapeDtypeStruct((BLOCK, heads * HEAD_SIZE), BF16),
            jax.ShapeDtypeStruct((BLOCK, heads * HEAD_SIZE), BF16),
            jax.ShapeDtypeStruct((2,), F32),
        ),
        in_specs=[hbm] * 6,
        out_specs=(hbm, hbm, hbm, pl.BlockSpec(memory_space=pltpu.SMEM)),
        scratch_shapes=[
            pltpu.VMEM((heads, 2, BLOCK, wide), BF16),
            pltpu.VMEM((heads, 2, 3 * BLOCK, HEAD_SIZE), BF16),
            pltpu.VMEM((heads, 2, 2, BLOCK, HEAD_SIZE), BF16),
            pltpu.VMEM((heads, 2, 2, BLOCK, HEAD_SIZE), BF16),
            pltpu.VMEM((heads, 2, 3 * BLOCK, HEAD_SIZE), F32),
            pltpu.VMEM((heads, BLOCK, wide), BF16),
            pltpu.VMEM((heads, 2, BLOCK, HEAD_SIZE), BF16),
            pltpu.VMEM((3 * BLOCK, BLOCK), F32),
            pltpu.VMEM((2, WINDOW, BLOCK), F32),
            pltpu.VMEM((2, quads, WINDOW, LANES), F32),
            pltpu.VMEM((2, quads, WINDOW, LANES), F32),
            pltpu.VMEM((2, quads, WINDOW, LANES), F32),
            pltpu.VMEM((2, WINDOW, quads * LANES), BF16),
            pltpu.VMEM((2, WINDOW, quads * LANES), BF16),
            pltpu.VMEM((1, tokens * seq_size), jnp.int32),
            pltpu.SMEM((QUERY_HEADS,), F32),
            pltpu.VMEM((seq_size, 1, 2 * HALF), F32),
            pltpu.VMEM((seq_size - 1, 1, 2 * HALF), F32),
            pltpu.VMEM((1, 1, 2 * HALF), F32),
            pltpu.VMEM((dp_size - 1, 1, 2 * HALF), F32),
            pltpu.SemaphoreType.DMA((heads,)),
            pltpu.SemaphoreType.DMA((heads,)),
            pltpu.SemaphoreType.DMA((heads,)),
            pltpu.SemaphoreType.DMA((heads,)),
            pltpu.SemaphoreType.DMA((heads,)),
            pltpu.SemaphoreType.DMA((heads,)),
            pltpu.SemaphoreType.DMA((heads,)),
            pltpu.SemaphoreType.DMA((heads, 2)),
            pltpu.SemaphoreType.DMA((4,)),
            pltpu.SemaphoreType.DMA((2,)),
        ],
        compiler_params=pltpu.CompilerParams(
            collective_id=0, has_side_effects=True, vmem_limit_bytes=VMEM_BYTES
        ),
        cost_estimate=pl.CostEstimate(
            flops=2 * 5 * BLOCK * WINDOW * HEAD_SIZE * QUERY_HEADS,
            bytes_accessed=4 * 1024 * 1024,
            transcendentals=BLOCK * WINDOW * QUERY_HEADS,
        ),
    )(queries[0], keys[0], values[0], score_gain, grad[0], segment_ids)
    results = (dq, dk, dv, gain)
    dq, dk, dv, gain = pl.pallas_call(
        hand_over,
        out_shape=tuple(jax.ShapeDtypeStruct(x.shape, x.dtype) for x in results),
        in_specs=[hbm] * 4,
        out_specs=(hbm,) * 4,
        scratch_shapes=[pltpu.SemaphoreType.DMA((HAND_PARTS + 3,))],
        compiler_params=pltpu.CompilerParams(vmem_limit_bytes=VMEM_BYTES),
    )(*results)
    return dq[None], dk[None], dv[None], gain


def solution(mesh):
    return jax.shard_map(
        body,
        mesh=mesh,
        in_specs=(
            P("dp", "seq", None),
            P("dp", "seq", None),
            P("dp", "seq", None),
            P(),
            P("dp", "seq", None),
            P("dp", None),
        ),
        out_specs=(P("dp", "seq", None), P("dp", "seq", None), P("dp", "seq", None), P("seq")),
        check_vma=False,
    )
```

```python
import functools
import math

import jax
import jax.numpy as jnp
from jax import lax
from jax.experimental import pallas as pl
from jax.experimental.pallas import tpu as pltpu
from jax.sharding import PartitionSpec as P

QUERY_HEADS = 32
KEY_VALUE_HEADS = 4
HEAD_SIZE = 128
GROUP = QUERY_HEADS // KEY_VALUE_HEADS
BLOCK = 128
HALF = 64
WINDOW = 320
QUAD = 4
LANES = QUAD * HALF
CHUNK = 64
HAND_PARTS = 4
VMEM_BYTES = 64 * 1024 * 1024
LOG2E = math.log2(math.e)
SCALE = HEAD_SIZE ** -0.5
BF16 = jnp.bfloat16
F32 = jnp.float32
NT = (((1,), (1,)), ((), ()))
TN = (((0,), (0,)), ((), ()))


def fold_rows(x):
    return jnp.sum(x.reshape(x.shape[0] // 8, 8, x.shape[1]), axis=0)


def kernel(
    seq_size, dp_size, factor,
    q_hbm, k_hbm, v_hbm, gain_hbm, g_hbm, seg_hbm,
    dq_hbm, dk_hbm, dv_hbm, gain_out,
    qg, kv, ret_send, ret, mate_send, mate_in, acc, dq_buf, dkv_buf, seg_rows, bias,
    s_buf, dp_buf, y_buf, p_buf, ds_buf, seg_ref, gain_ref,
    g_rows, g_part, g_in1, g_sum, g_in2,
    in_sem, own_sem, halo_send, halo_recv, mate_kv_send, mate_kv_recv, mate_qg_send, mate_qg_recv,
    back_send, back_recv, mate_back_send, mate_back_recv, dq_sem, mate_dq_send, mate_dq_recv,
    dkv_sem, gain1_send, gain1_recv, gain2_sem, small_sem,
):
    me = lax.axis_index("seq")
    row = lax.axis_index("dp")
    chips = seq_size // 2
    chip = lax.div(me, 2)
    core = me - 2 * chip
    other = 1 - core
    mate = 2 * chip + other
    next_chip = lax.rem(chip + 1, chips)
    last_chip = lax.rem(chip + chips - 1, chips)

    def thin(head):
        return pl.ds(pl.multiple_of(head * HEAD_SIZE, HEAD_SIZE), HEAD_SIZE)

    def wide(head):
        return pl.ds(pl.multiple_of(head * (GROUP * HEAD_SIZE), GROUP * HEAD_SIZE), GROUP * HEAD_SIZE)

    def block(index):
        return pl.ds(pl.multiple_of(index * BLOCK, BLOCK), BLOCK)

    def remote(source, target, send, recv, device):
        return pltpu.make_async_remote_copy(
            src_ref=source,
            dst_ref=target,
            send_sem=send,
            recv_sem=recv,
            device_id={"seq": device},
            device_id_type=pl.DeviceIdType.MESH,
        )

    barrier = pltpu.get_barrier_semaphore()

    def greet_seq(i, carry):
        pl.semaphore_signal(
            barrier, inc=1, device_id={"seq": lax.rem(me + i, seq_size)}, device_id_type=pl.DeviceIdType.MESH
        )
        return carry

    def greet_dp(i, carry):
        pl.semaphore_signal(
            barrier, inc=1, device_id={"dp": lax.rem(row + i, dp_size)}, device_id_type=pl.DeviceIdType.MESH
        )
        return carry

    lax.fori_loop(1, seq_size, greet_seq, 0)
    lax.fori_loop(1, dp_size, greet_dp, 0)

    for a in range(2):
        head = 2 * core + a
        pltpu.make_async_copy(k_hbm.at[:, thin(head)], kv.at[a, 0, block(2 + core)], own_sem.at[a]).start()
        pltpu.make_async_copy(v_hbm.at[:, thin(head)], kv.at[a, 1, block(2 + core)], own_sem.at[a]).start()
        pltpu.make_async_copy(q_hbm.at[:, wide(head)], qg.at[a, 0, block(core)], in_sem.at[a]).start()
        pltpu.make_async_copy(g_hbm.at[:, wide(head)], qg.at[a, 1, block(core)], in_sem.at[a]).start()
    seg_copy = pltpu.make_async_copy(seg_hbm, seg_ref, small_sem.at[0])
    gain_copy = pltpu.make_async_copy(gain_hbm, gain_ref, small_sem.at[1])
    seg_copy.start()
    gain_copy.start()
    pl.semaphore_wait(barrier, seq_size + dp_size - 2)

    def halo_start(a):
        for to_core in range(2):
            for which, source in enumerate((k_hbm, v_hbm)):
                remote(
                    source.at[:, thin(2 * to_core + a)],
                    kv.at[a, which, block(core)],
                    halo_send.at[a],
                    halo_recv.at[a],
                    2 * next_chip + to_core,
                ).start()

    def halo_whole(a):
        part = kv.at[a, :, pl.ds(0, 2 * BLOCK)]
        return remote(part, part, halo_send.at[a], halo_recv.at[a], 2 * next_chip)

    def mate_start(a):
        head = 2 * other + a
        for which, source in enumerate((k_hbm, v_hbm)):
            remote(
                source.at[:, thin(head)], kv.at[a, which, block(2 + core)],
                mate_kv_send.at[a], mate_kv_recv.at[a], mate,
            ).start()
        for which, source in enumerate((q_hbm, g_hbm)):
            remote(
                source.at[:, wide(head)], qg.at[a, which, block(core)],
                mate_qg_send.at[a], mate_qg_recv.at[a], mate,
            ).start()

    def mate_kv(a):
        part = kv.at[a, :, block(2 + other)]
        return remote(part, part, mate_kv_send.at[a], mate_kv_recv.at[a], mate)

    def mate_qg(a):
        part = qg.at[a, :, block(other)]
        return remote(part, part, mate_qg_send.at[a], mate_qg_recv.at[a], mate)

    halo_start(0)
    mate_start(0)
    mate_start(1)
    seg_copy.wait()
    gain_copy.wait()

    def ids_of(index):
        place = pl.multiple_of(lax.rem(2 * chip + index + seq_size, seq_size) * BLOCK, BLOCK)
        return seg_ref[:, pl.ds(place, BLOCK)].astype(F32)

    for b in range(4):
        seg_rows[pl.ds(b * BLOCK, BLOCK)] = jnp.transpose(
            jnp.broadcast_to(ids_of(b - 2), (BLOCK, BLOCK))
        )
    lane8 = lax.broadcasted_iota(jnp.int32, (8, BLOCK), 1)
    key_place = lax.broadcasted_iota(jnp.int32, (WINDOW, BLOCK), 0)
    lane = lax.broadcasted_iota(jnp.int32, (WINDOW, BLOCK), 1)
    causal = key_place <= 2 * BLOCK + jnp.where(lane < HALF, lane, lane - HALF)
    for x in range(2):
        query_ids = jnp.broadcast_to(ids_of(x), (8, BLOCK))
        turned = pltpu.roll(query_ids, HALF, 1)
        for half in range(2):
            start = x * BLOCK + half * HALF
            ids = jnp.where((lane8 < HALF) == (half == 0), query_ids, turned)[0:1]
            inside = (chip - 1) * (2 * BLOCK) + start + key_place >= 0
            allowed = (seg_rows[pl.ds(start, WINDOW)] == ids) & causal & inside
            bias[2 * x + half] = jnp.where(allowed, 0.0, -1e30)

    lane_wide = lax.broadcasted_iota(jnp.int32, (1, LANES), 1)
    quads = GROUP // QUAD

    def back_copy(a, place):
        return remote(
            ret_send.at[a, place], ret.at[2 * core + a],
            back_send.at[a], back_recv.at[2 * core + a], 2 * last_chip + place,
        )

    def back_whole(a):
        return remote(ret_send.at[a], ret_send.at[a], back_send.at[a], back_recv.at[a], 2 * last_chip)

    def back_from(head):
        return remote(ret.at[head], ret.at[head], back_send.at[0], back_recv.at[head], 2 * last_chip)

    def mate_back(a):
        return remote(
            mate_send.at[a], mate_in.at[a], mate_back_send.at[a], mate_back_recv.at[a], mate
        )

    def dkv_out(head, which):
        target = (dk_hbm, dv_hbm)[which]
        return pltpu.make_async_copy(
            dkv_buf.at[head, which], target.at[:, thin(head)], dkv_sem.at[head, which]
        )

    def finish(a):
        mine = 2 * core + a
        theirs = 2 * other + a
        back_from(mine).wait_recv()
        for which in range(2):
            total = acc[a, which, block(2 + core)] + ret[mine, which].astype(F32)
            dkv_buf[mine, which] = total.astype(BF16)
            dkv_out(mine, which).start()
        mate_back(a).wait_recv()
        back_from(theirs).wait_recv()
        for which in range(2):
            total = mate_in[a, which].astype(F32) + ret[theirs, which].astype(F32)
            dkv_buf[theirs, which] = total.astype(BF16)
            dkv_out(theirs, which).start()

    def dq_own(a):
        return pltpu.make_async_copy(dq_buf.at[a, 0], dq_hbm.at[:, wide(2 * core + a)], dq_sem.at[a])

    def dq_mate(a):
        return remote(
            dq_buf.at[a, 1], dq_hbm.at[:, wide(2 * core + a)], mate_dq_send.at[a], mate_dq_recv.at[a], mate
        )

    def dq_from(a):
        part = dq_hbm.at[:, wide(2 * other + a)]
        return remote(part, part, mate_dq_send.at[a], mate_dq_recv.at[a], mate)

    def gain_copy1(index):
        return remote(
            g_part.at[index], g_in1.at[chip], gain1_send.at[index], gain1_recv.at[chip], chips * core + index
        )

    def step(number, carry):
        a = lax.div(number, 2)
        late = number - 2 * a
        x = core + late - 2 * core * late
        base = x * BLOCK

        @pl.when(late == 0)
        def _():
            halo_whole(a).wait_recv()

            @pl.when(a == 0)
            def _():
                halo_start(1)

            own = kv.at[a, :, block(2 + core)]
            pltpu.make_async_copy(own, own, own_sem.at[a]).wait()
            held = qg.at[a, :, block(core)]
            pltpu.make_async_copy(held, held, in_sem.at[a]).wait()
            mate_kv(a).wait_recv()
            acc[a] = jnp.zeros((2, 4 * BLOCK, HEAD_SIZE), F32)

        @pl.when(late == 1)
        def _():
            mate_qg(a).wait_recv()

        def key_rows(half):
            return pl.ds(pl.multiple_of(base + half * HALF, HALF), WINDOW)

        def stack(which, half, heads):
            rows = pl.ds(pl.multiple_of(base + half * HALF, HALF), HALF)
            return jnp.concatenate(
                [qg[a, which, rows, pl.ds(h * HEAD_SIZE, HEAD_SIZE)] for h in heads], axis=0
            )

        def first(half, quad):
            rows = key_rows(half)
            heads = range(quad * QUAD, quad * QUAD + QUAD)
            s_buf[half, quad] = lax.dot_general(
                kv[a, 0, rows], stack(0, half, heads), NT, preferred_element_type=F32
            )
            dp_buf[half, quad] = lax.dot_general(
                kv[a, 1, rows], stack(1, half, heads), NT, preferred_element_type=F32
            )

        def middle(half, quad):
            gains = [gain_ref[(2 * core + a) * GROUP + quad * QUAD + h] for h in range(QUAD)]
            gain = jnp.where(
                lane_wide < 2 * HALF,
                jnp.where(lane_wide < HALF, gains[0], gains[1]),
                jnp.where(lane_wide < 3 * HALF, gains[2], gains[3]),
            )
            to_score = gain * (SCALE * LOG2E)
            to_grad = gain * SCALE
            lanes = pl.ds(quad * LANES, LANES)
            chunks = [pl.ds(i, CHUNK) for i in range(0, WINDOW, CHUNK)]
            top = jnp.full((8, LANES), -3e38, F32)
            for rows in chunks:
                shade = bias[2 * x + half, rows]
                y = s_buf[half, quad, rows] * to_score + jnp.concatenate([shade, shade], axis=1)
                y_buf[half, quad, rows] = y
                top = jnp.maximum(top, jnp.max(y.reshape(CHUNK // 8, 8, LANES), axis=0))
            top = jnp.max(top, axis=0, keepdims=True)
            total = jnp.zeros((8, LANES), F32)
            dot = jnp.zeros((8, LANES), F32)
            for rows in chunks:
                e = jnp.exp2(y_buf[half, quad, rows] - top)
                y_buf[half, quad, rows] = e
                total = total + fold_rows(e)
                dot = dot + fold_rows(e * dp_buf[half, quad, rows])
            inverse = 1.0 / jnp.sum(total, axis=0, keepdims=True)
            delta = jnp.sum(dot, axis=0, keepdims=True) * inverse
            spread = jnp.zeros((8, LANES), F32)
            for rows in chunks:
                p = y_buf[half, quad, rows] * inverse
                dscore = p * (dp_buf[half, quad, rows] - delta)
                spread = spread + fold_rows(dscore * s_buf[half, quad, rows])
                p_buf[half, rows, lanes] = p.astype(BF16)
                ds_buf[half, rows, lanes] = (dscore * to_grad).astype(BF16)
            return jnp.sum(spread, axis=0, keepdims=True) * (SCALE * factor)

        def last(half):
            rows = key_rows(half)
            everyone = range(GROUP)
            turned_keys = jnp.transpose(kv[a, 0, rows])
            for quad in range(quads):
                ds = ds_buf[half, :, pl.ds(quad * LANES, LANES)]
                dq = jnp.dot(turned_keys, ds, preferred_element_type=F32).astype(BF16)
                dq = jnp.transpose(dq)
                for h in range(QUAD):
                    dq_buf[
                        a, late, pl.ds(half * HALF, HALF),
                        pl.ds((quad * QUAD + h) * HEAD_SIZE, HEAD_SIZE),
                    ] = dq[h * HALF:(h + 1) * HALF]
            acc[a, 0, rows] += jnp.dot(
                ds_buf[half], stack(0, half, everyone), preferred_element_type=F32
            )
            acc[a, 1, rows] += jnp.dot(
                p_buf[half], stack(1, half, everyone), preferred_element_type=F32
            )

        first(0, 0)
        first(0, 1)
        term00 = middle(0, 0)
        first(1, 0)
        term01 = middle(0, 1)
        first(1, 1)
        last(0)
        term10 = middle(1, 0)
        term11 = middle(1, 1)
        last(1)
        terms = [term00 + term10, term01 + term11]

        @pl.when(late == 0)
        def _():
            dq_own(a).start()
            for quad in range(quads):
                g_rows[quad] = terms[quad]

        @pl.when(late == 1)
        def _():
            for place in range(2):
                for which in range(2):
                    ret_send[a, place, which] = acc[a, which, pl.ds(place * BLOCK, BLOCK)].astype(BF16)
                back_copy(a, place).start()
            for quad in range(quads):
                both = g_rows[quad] + terms[quad]
                for side in range(2):
                    index = a * (2 * quads) + quad * 2 + side
                    piece = both[:, side * 2 * HALF:(side + 1) * 2 * HALF]
                    target = chips * core + index

                    @pl.when(target == me)
                    def _():
                        g_in1[chip] = piece

                    @pl.when(target != me)
                    def _():
                        g_part[index] = piece
                        gain_copy1(index).start()

            for which in range(2):
                mate_send[a, which] = acc[a, which, block(2 + other)].astype(BF16)
            mate_back(a).start()
            dq_mate(a).start()

        return carry

    lax.fori_loop(0, 4, step, 0)
    finish(0)

    def gain_arrive(i, carry):
        @pl.when(2 * i + lax.div(me, chips) != me)
        def _():
            remote(g_in1.at[i], g_in1.at[i], gain1_send.at[0], gain1_recv.at[i], mate).wait_recv()

        return carry

    lax.fori_loop(0, chips, gain_arrive, 0)
    g_sum[0] = jnp.sum(g_in1[...], axis=0)

    def gain_send2(i, carry):
        pltpu.make_async_remote_copy(
            src_ref=g_sum.at[0],
            dst_ref=g_in2.at[i - 1],
            send_sem=gain2_sem.at[0],
            recv_sem=gain2_sem.at[1],
            device_id={"dp": lax.rem(row + i, dp_size)},
            device_id_type=pl.DeviceIdType.MESH,
        ).start()
        return carry

    lax.fori_loop(1, dp_size, gain_send2, 0)
    finish(1)
    gain2_whole = remote(g_in2, g_in2, gain2_sem.at[0], gain2_sem.at[1], mate)
    gain2_whole.wait_recv()
    lanes = g_sum[0] + jnp.sum(g_in2[...], axis=0)
    lane1 = lax.broadcasted_iota(jnp.int32, (1, 2 * HALF), 1)
    gain_out[0] = jnp.sum(jnp.where(lane1 < HALF, lanes, 0.0))
    gain_out[1] = jnp.sum(jnp.where(lane1 < HALF, 0.0, lanes))

    gain2_whole.wait_send()

    def gain_left(index, carry):
        @pl.when(chips * core + index != me)
        def _():
            gain_copy1(index).wait_send()

        return carry

    lax.fori_loop(0, chips, gain_left, 0)
    for a in range(2):
        halo_whole(a).wait_send()
        mate_kv(a).wait_send()
        mate_qg(a).wait_send()
        back_whole(a).wait_send()
        mate_back(a).wait_send()
        dq_own(a).wait()
        dq_mate(a).wait_send()
        dq_from(a).wait_recv()
    for head in range(KEY_VALUE_HEADS):
        for which in range(2):
            dkv_out(head, which).wait()


def hand_over(dq_in, dk_in, dv_in, gain_in, dq_out, dk_out, dv_out, gain_to, dq_buf, dk_buf, dv_buf, gain_buf, sems):
    trips = [
        (dk_in, dk_buf, dk_out),
        (dv_in, dv_buf, dv_out),
        (gain_in, gain_buf, gain_to),
    ]
    for i in range(HAND_PARTS):
        rows = pl.ds(i * (BLOCK // HAND_PARTS), BLOCK // HAND_PARTS)
        trips.append((dq_in.at[rows], dq_buf.at[rows], dq_out.at[rows]))
    there = [pltpu.make_async_copy(x, y, sems.at[0, i]) for i, (x, y, _) in enumerate(trips)]
    back = [pltpu.make_async_copy(y, z, sems.at[1, i]) for i, (_, y, z) in enumerate(trips)]
    for copy in there:
        copy.start()
    for arrive, leave in zip(there, back):
        arrive.wait()
        leave.start()
    for copy in back:
        copy.wait()


def body(queries, keys, values, score_gain, grad, segment_ids):
    seq_size = lax.axis_size("seq")
    dp_size = lax.axis_size("dp")
    tokens = queries.shape[1]
    factor = 1.0 / (dp_size * tokens * seq_size)
    hbm = pl.BlockSpec(memory_space=pltpu.HBM)
    heads = KEY_VALUE_HEADS
    quads = GROUP // QUAD
    pair = pltpu.SemaphoreType.DMA((2,))
    wide = GROUP * HEAD_SIZE
    dq, dk, dv, gain = pl.pallas_call(
        functools.partial(kernel, seq_size, dp_size, factor),
        out_shape=(
            jax.ShapeDtypeStruct((BLOCK, QUERY_HEADS * HEAD_SIZE), BF16),
            jax.ShapeDtypeStruct((BLOCK, heads * HEAD_SIZE), BF16),
            jax.ShapeDtypeStruct((BLOCK, heads * HEAD_SIZE), BF16),
            jax.ShapeDtypeStruct((2,), F32),
        ),
        in_specs=[hbm] * 6,
        out_specs=(hbm, hbm, hbm, pl.BlockSpec(memory_space=pltpu.SMEM)),
        scratch_shapes=[
            pltpu.VMEM((2, 2, 2 * BLOCK, wide), BF16),
            pltpu.VMEM((2, 2, 4 * BLOCK, HEAD_SIZE), BF16),
            pltpu.VMEM((2, 2, 2, BLOCK, HEAD_SIZE), BF16),
            pltpu.VMEM((heads, 2, BLOCK, HEAD_SIZE), BF16),
            pltpu.VMEM((2, 2, BLOCK, HEAD_SIZE), BF16),
            pltpu.VMEM((2, 2, BLOCK, HEAD_SIZE), BF16),
            pltpu.VMEM((2, 2, 4 * BLOCK, HEAD_SIZE), F32),
            pltpu.VMEM((2, 2, BLOCK, wide), BF16),
            pltpu.VMEM((heads, 2, BLOCK, HEAD_SIZE), BF16),
            pltpu.VMEM((4 * BLOCK, BLOCK), F32),
            pltpu.VMEM((4, WINDOW, BLOCK), F32),
            pltpu.VMEM((2, quads, WINDOW, LANES), F32),
            pltpu.VMEM((2, quads, WINDOW, LANES), F32),
            pltpu.VMEM((2, quads, WINDOW, LANES), F32),
            pltpu.VMEM((2, WINDOW, quads * LANES), BF16),
            pltpu.VMEM((2, WINDOW, quads * LANES), BF16),
            pltpu.VMEM((1, tokens * seq_size), jnp.int32),
            pltpu.SMEM((QUERY_HEADS,), F32),
            pltpu.VMEM((quads, 1, LANES), F32),
            pltpu.VMEM((seq_size // 2, 1, 2 * HALF), F32),
            pltpu.VMEM((seq_size // 2, 1, 2 * HALF), F32),
            pltpu.VMEM((1, 1, 2 * HALF), F32),
            pltpu.VMEM((dp_size - 1, 1, 2 * HALF), F32),
            pair, pair, pair, pair, pair, pair, pair, pair,
            pair,
            pltpu.SemaphoreType.DMA((heads,)),
            pair, pair, pair, pair, pair,
            pltpu.SemaphoreType.DMA((heads, 2)),
            pltpu.SemaphoreType.DMA((seq_size // 2,)),
            pltpu.SemaphoreType.DMA((seq_size // 2,)),
            pair, pair,
        ],
        compiler_params=pltpu.CompilerParams(
            collective_id=0, has_side_effects=True, vmem_limit_bytes=VMEM_BYTES
        ),
        cost_estimate=pl.CostEstimate(
            flops=2 * 5 * BLOCK * WINDOW * HEAD_SIZE * QUERY_HEADS,
            bytes_accessed=4 * 1024 * 1024,
            transcendentals=BLOCK * WINDOW * QUERY_HEADS,
        ),
    )(queries[0], keys[0], values[0], score_gain, grad[0], segment_ids)
    results = (dq, dk, dv, gain)
    dq, dk, dv, gain = pl.pallas_call(
        hand_over,
        out_shape=tuple(jax.ShapeDtypeStruct(x.shape, x.dtype) for x in results),
        in_specs=[hbm] * 4,
        out_specs=(hbm,) * 4,
        scratch_shapes=[
            *[pltpu.VMEM(x.shape, x.dtype) for x in results[:3]],
            pltpu.SMEM(gain.shape, gain.dtype),
            pltpu.SemaphoreType.DMA((2, HAND_PARTS + 3)),
        ],
        compiler_params=pltpu.CompilerParams(vmem_limit_bytes=VMEM_BYTES),
    )(*results)
    return dq[None], dk[None], dv[None], gain


def solution(mesh):
    return jax.shard_map(
        body,
        mesh=mesh,
        in_specs=(
            P("dp", "seq", None),
            P("dp", "seq", None),
            P("dp", "seq", None),
            P(),
            P("dp", "seq", None),
            P("dp", None),
        ),
        out_specs=(P("dp", "seq", None), P("dp", "seq", None), P("dp", "seq", None), P("seq")),
        check_vma=False,
    )
```

```python
import functools
import math

import jax
import jax.numpy as jnp
from jax import lax
from jax.experimental import pallas as pl
from jax.experimental.pallas import tpu as pltpu
from jax.sharding import PartitionSpec as P

QUERY_HEADS = 32
KEY_VALUE_HEADS = 4
HEAD_SIZE = 128
GROUP = QUERY_HEADS // KEY_VALUE_HEADS
BLOCK = 128
HALF = 64
WINDOW = 320
QUAD = 4
LANES = QUAD * HALF
CHUNK = 64
HAND_PARTS = 4
VMEM_BYTES = 64 * 1024 * 1024
LOG2E = math.log2(math.e)
SCALE = HEAD_SIZE ** -0.5
BF16 = jnp.bfloat16
F32 = jnp.float32
NT = (((1,), (1,)), ((), ()))
TN = (((0,), (0,)), ((), ()))


def fold_rows(x):
    return jnp.sum(x.reshape(x.shape[0] // 8, 8, x.shape[1]), axis=0)


def kernel(
    seq_size, dp_size, factor,
    q_hbm, k_hbm, v_hbm, gain_hbm, g_hbm, seg_hbm,
    dq_hbm, dk_hbm, dv_hbm, gain_out,
    qg, kv, ret_send, ret, mate_send, mate_in, acc, dq_buf, dkv_buf, seg_rows, bias,
    s_buf, dp_buf, y_buf, p_buf, ds_buf, seg_ref, gain_ref,
    g_rows, g_part, g_in1, g_sum, g_in2,
    in_sem, own_sem, halo_send, halo_recv, mate_kv_send, mate_kv_recv, mate_qg_send, mate_qg_recv,
    back_send, back_recv, mate_back_send, mate_back_recv, dq_sem, mate_dq_send, mate_dq_recv,
    dkv_sem, gain1_send, gain1_recv, gain2_sem, small_sem,
):
    me = lax.axis_index("seq")
    row = lax.axis_index("dp")
    chips = seq_size // 2
    chip = lax.div(me, 2)
    core = me - 2 * chip
    other = 1 - core
    mate = 2 * chip + other
    next_chip = lax.rem(chip + 1, chips)
    last_chip = lax.rem(chip + chips - 1, chips)

    def thin(head):
        return pl.ds(pl.multiple_of(head * HEAD_SIZE, HEAD_SIZE), HEAD_SIZE)

    def wide(head):
        return pl.ds(pl.multiple_of(head * (GROUP * HEAD_SIZE), GROUP * HEAD_SIZE), GROUP * HEAD_SIZE)

    def block(index):
        return pl.ds(pl.multiple_of(index * BLOCK, BLOCK), BLOCK)

    def remote(source, target, send, recv, device):
        return pltpu.make_async_remote_copy(
            src_ref=source,
            dst_ref=target,
            send_sem=send,
            recv_sem=recv,
            device_id={"seq": device},
            device_id_type=pl.DeviceIdType.MESH,
        )

    barrier = pltpu.get_barrier_semaphore()

    def greet_seq(i, carry):
        pl.semaphore_signal(
            barrier, inc=1, device_id={"seq": lax.rem(me - i + seq_size, seq_size)}, device_id_type=pl.DeviceIdType.MESH
        )
        return carry

    def greet_dp(i, carry):
        pl.semaphore_signal(
            barrier, inc=1, device_id={"dp": lax.rem(row + i, dp_size)}, device_id_type=pl.DeviceIdType.MESH
        )
        return carry

    lax.fori_loop(1, seq_size, greet_seq, 0)
    lax.fori_loop(1, dp_size, greet_dp, 0)

    for a in range(2):
        head = 2 * core + a
        pltpu.make_async_copy(k_hbm.at[:, thin(head)], kv.at[a, 0, block(2 + core)], own_sem.at[a]).start()
        pltpu.make_async_copy(v_hbm.at[:, thin(head)], kv.at[a, 1, block(2 + core)], own_sem.at[a]).start()
        pltpu.make_async_copy(q_hbm.at[:, wide(head)], qg.at[a, 0, block(core)], in_sem.at[a]).start()
        pltpu.make_async_copy(g_hbm.at[:, wide(head)], qg.at[a, 1, block(core)], in_sem.at[a]).start()
    seg_copy = pltpu.make_async_copy(seg_hbm, seg_ref, small_sem.at[0])
    gain_copy = pltpu.make_async_copy(gain_hbm, gain_ref, small_sem.at[1])
    seg_copy.start()
    gain_copy.start()
    pl.semaphore_wait(barrier, seq_size + dp_size - 2)

    def halo_start(a):
        for which, source in enumerate((k_hbm, v_hbm)):
            for to_core in range(2):
                remote(
                    source.at[:, thin(2 * to_core + a)],
                    kv.at[a, which, block(core)],
                    halo_send.at[a, which],
                    halo_recv.at[a, which],
                    2 * next_chip + to_core,
                ).start()

    def halo_whole(a, which):
        part = kv.at[a, which, pl.ds(0, 2 * BLOCK)]
        return remote(part, part, halo_send.at[a, which], halo_recv.at[a, which], 2 * next_chip)

    def mate_start(a):
        head = 2 * other + a
        for which, source in enumerate((k_hbm, v_hbm)):
            remote(
                source.at[:, thin(head)], kv.at[a, which, block(2 + core)],
                mate_kv_send.at[a, which], mate_kv_recv.at[a, which], mate,
            ).start()
        for which, source in enumerate((q_hbm, g_hbm)):
            remote(
                source.at[:, wide(head)], qg.at[a, which, block(core)],
                mate_qg_send.at[a], mate_qg_recv.at[a], mate,
            ).start()

    def mate_kv(a, which):
        part = kv.at[a, which, block(2 + other)]
        return remote(part, part, mate_kv_send.at[a, which], mate_kv_recv.at[a, which], mate)

    def mate_qg(a):
        part = qg.at[a, :, block(other)]
        return remote(part, part, mate_qg_send.at[a], mate_qg_recv.at[a], mate)

    halo_start(0)
    mate_start(0)
    mate_start(1)
    acc[...] = jnp.zeros(acc.shape, F32)
    seg_copy.wait()
    gain_copy.wait()

    def ids_of(index):
        place = pl.multiple_of(lax.rem(2 * chip + index + seq_size, seq_size) * BLOCK, BLOCK)
        return seg_ref[:, pl.ds(place, BLOCK)].astype(F32)

    for b in range(4):
        seg_rows[pl.ds(b * BLOCK, BLOCK)] = jnp.transpose(
            jnp.broadcast_to(ids_of(b - 2), (BLOCK, BLOCK))
        )
    lane8 = lax.broadcasted_iota(jnp.int32, (8, BLOCK), 1)
    key_place = lax.broadcasted_iota(jnp.int32, (WINDOW, BLOCK), 0)
    lane = lax.broadcasted_iota(jnp.int32, (WINDOW, BLOCK), 1)
    causal = key_place <= 2 * BLOCK + jnp.where(lane < HALF, lane, lane - HALF)
    for x in range(2):
        query_ids = jnp.broadcast_to(ids_of(x), (8, BLOCK))
        turned = pltpu.roll(query_ids, HALF, 1)
        for half in range(2):
            start = x * BLOCK + half * HALF
            ids = jnp.where((lane8 < HALF) == (half == 0), query_ids, turned)[0:1]
            inside = (chip - 1) * (2 * BLOCK) + start + key_place >= 0
            allowed = (seg_rows[pl.ds(start, WINDOW)] == ids) & causal & inside
            bias[2 * x + half] = jnp.where(allowed, 0.0, -1e30)

    lane_wide = lax.broadcasted_iota(jnp.int32, (1, LANES), 1)
    quads = GROUP // QUAD

    def back_copy(a, place):
        return remote(
            ret_send.at[a, place], ret.at[2 * core + a],
            back_send.at[a], back_recv.at[2 * core + a], 2 * last_chip + place,
        )

    def back_whole(a):
        return remote(ret_send.at[a], ret_send.at[a], back_send.at[a], back_recv.at[a], 2 * last_chip)

    def back_from(head):
        return remote(ret.at[head], ret.at[head], back_send.at[0], back_recv.at[head], 2 * last_chip)

    def mate_back(a):
        return remote(
            mate_send.at[a], mate_in.at[a], mate_back_send.at[a], mate_back_recv.at[a], mate
        )

    def dkv_out(head, which):
        target = (dk_hbm, dv_hbm)[which]
        return pltpu.make_async_copy(
            dkv_buf.at[head, which], target.at[:, thin(head)], dkv_sem.at[head, which]
        )

    def finish(a):
        mine = 2 * core + a
        theirs = 2 * other + a
        back_from(mine).wait_recv()
        for which in range(2):
            total = acc[a, which, block(2 + core)] + ret[mine, which].astype(F32)
            dkv_buf[mine, which] = total.astype(BF16)
            dkv_out(mine, which).start()
        mate_back(a).wait_recv()
        back_from(theirs).wait_recv()
        for which in range(2):
            total = mate_in[a, which].astype(F32) + ret[theirs, which].astype(F32)
            dkv_buf[theirs, which] = total.astype(BF16)
            dkv_out(theirs, which).start()

    def dq_own(a):
        return pltpu.make_async_copy(dq_buf.at[a, 0], dq_hbm.at[:, wide(2 * core + a)], dq_sem.at[a])

    def dq_mate(a):
        return remote(
            dq_buf.at[a, 1], dq_hbm.at[:, wide(2 * core + a)], mate_dq_send.at[a], mate_dq_recv.at[a], mate
        )

    def dq_from(a):
        part = dq_hbm.at[:, wide(2 * other + a)]
        return remote(part, part, mate_dq_send.at[a], mate_dq_recv.at[a], mate)

    def gain_copy1(index):
        return remote(
            g_part.at[index], g_in1.at[chip], gain1_send.at[index], gain1_recv.at[chip], chips * core + index
        )

    def block_of(late):
        return core + late - 2 * core * late

    def key_rows(x, half):
        return pl.ds(pl.multiple_of(x * BLOCK + half * HALF, HALF), WINDOW)

    def stack(a, x, which, half, heads):
        rows = pl.ds(pl.multiple_of(x * BLOCK + half * HALF, HALF), HALF)
        return jnp.concatenate(
            [qg[a, which, rows, pl.ds(h * HEAD_SIZE, HEAD_SIZE)] for h in heads], axis=0
        )

    def scores(number, carry):
        a = lax.div(number, 2)
        late = number - 2 * a
        x = block_of(late)

        @pl.when(late == 0)
        def _():
            own = kv.at[a, :, block(2 + core)]
            pltpu.make_async_copy(own, own, own_sem.at[a]).wait()
            held = qg.at[a, :, block(core)]
            pltpu.make_async_copy(held, held, in_sem.at[a]).wait()
            mate_kv(a, 0).wait_recv()
            halo_whole(a, 0).wait_recv()

        @pl.when(late == 1)
        def _():
            mate_qg(a).wait_recv()

        def product(target, which, half, quad):
            heads = range(quad * QUAD, quad * QUAD + QUAD)
            target[half, quad] = lax.dot_general(
                kv[a, which, key_rows(x, half)], stack(a, x, which, half, heads), NT,
                preferred_element_type=F32,
            )

        def middle(half, quad):
            gains = [gain_ref[(2 * core + a) * GROUP + quad * QUAD + h] for h in range(QUAD)]
            gain = jnp.where(
                lane_wide < 2 * HALF,
                jnp.where(lane_wide < HALF, gains[0], gains[1]),
                jnp.where(lane_wide < 3 * HALF, gains[2], gains[3]),
            )
            to_score = gain * (SCALE * LOG2E)
            to_grad = gain * SCALE
            lanes = pl.ds(quad * LANES, LANES)
            chunks = [pl.ds(i, CHUNK) for i in range(0, WINDOW, CHUNK)]
            top = jnp.full((8, LANES), -3e38, F32)
            for rows in chunks:
                shade = bias[2 * x + half, rows]
                y = s_buf[half, quad, rows] * to_score + jnp.concatenate([shade, shade], axis=1)
                y_buf[half, quad, rows] = y
                top = jnp.maximum(top, jnp.max(y.reshape(CHUNK // 8, 8, LANES), axis=0))
            top = jnp.max(top, axis=0, keepdims=True)
            total = jnp.zeros((8, LANES), F32)
            dot = jnp.zeros((8, LANES), F32)
            for rows in chunks:
                e = jnp.exp2(y_buf[half, quad, rows] - top)
                y_buf[half, quad, rows] = e
                total = total + fold_rows(e)
                dot = dot + fold_rows(e * dp_buf[half, quad, rows])
            inverse = 1.0 / jnp.sum(total, axis=0, keepdims=True)
            delta = jnp.sum(dot, axis=0, keepdims=True) * inverse
            spread = jnp.zeros((8, LANES), F32)
            for rows in chunks:
                p = y_buf[half, quad, rows] * inverse
                dscore = p * (dp_buf[half, quad, rows] - delta)
                spread = spread + fold_rows(dscore * s_buf[half, quad, rows])
                p_buf[number, half, rows, lanes] = p.astype(BF16)
                ds_buf[number, half, rows, lanes] = (dscore * to_grad).astype(BF16)
            return jnp.sum(spread, axis=0, keepdims=True) * (SCALE * factor)

        product(s_buf, 0, 0, 0)
        product(s_buf, 0, 0, 1)
        product(s_buf, 0, 1, 0)
        product(s_buf, 0, 1, 1)

        @pl.when(late == 0)
        def _():
            mate_kv(a, 1).wait_recv()
            halo_whole(a, 1).wait_recv()

            @pl.when(a == 0)
            def _():
                halo_start(1)

        product(dp_buf, 1, 0, 0)
        product(dp_buf, 1, 0, 1)
        term00 = middle(0, 0)
        product(dp_buf, 1, 1, 0)
        term01 = middle(0, 1)
        product(dp_buf, 1, 1, 1)
        term10 = middle(1, 0)
        term11 = middle(1, 1)
        terms = [term00 + term10, term01 + term11]

        @pl.when(late == 0)
        def _():
            for quad in range(quads):
                g_rows[quad] = terms[quad]

        @pl.when(late == 1)
        def _():
            for quad in range(quads):
                both = g_rows[quad] + terms[quad]
                for side in range(2):
                    index = a * (2 * quads) + quad * 2 + side
                    piece = both[:, side * 2 * HALF:(side + 1) * 2 * HALF]
                    target = chips * core + index

                    @pl.when(target == me)
                    def _():
                        g_in1[chip] = piece

                    @pl.when(target != me)
                    def _():
                        g_part[index] = piece
                        gain_copy1(index).start()

        return carry

    lax.fori_loop(0, 4, scores, 0)

    def gain_arrive(i, carry):
        @pl.when(2 * i + lax.div(me, chips) != me)
        def _():
            remote(g_in1.at[i], g_in1.at[i], gain1_send.at[0], gain1_recv.at[i], mate).wait_recv()

        return carry

    lax.fori_loop(0, chips, gain_arrive, 0)
    g_sum[0] = jnp.sum(g_in1[...], axis=0)

    def gain_send2(i, carry):
        pltpu.make_async_remote_copy(
            src_ref=g_sum.at[0],
            dst_ref=g_in2.at[i - 1],
            send_sem=gain2_sem.at[0],
            recv_sem=gain2_sem.at[1],
            device_id={"dp": lax.rem(row + i, dp_size)},
            device_id_type=pl.DeviceIdType.MESH,
        ).start()
        return carry

    lax.fori_loop(1, dp_size, gain_send2, 0)

    def key_side(a, carry):
        for late in range(2):
            x = block_of(late)
            for half in range(2):
                rows = key_rows(x, half)
                acc[a, 0, rows] += jnp.dot(
                    ds_buf[2 * a + late, half], stack(a, x, 0, half, range(GROUP)),
                    preferred_element_type=F32,
                )
                acc[a, 1, rows] += jnp.dot(
                    p_buf[2 * a + late, half], stack(a, x, 1, half, range(GROUP)),
                    preferred_element_type=F32,
                )
        for place in range(2):
            for which in range(2):
                ret_send[a, place, which] = acc[a, which, pl.ds(place * BLOCK, BLOCK)].astype(BF16)
            back_copy(a, place).start()
        for which in range(2):
            mate_send[a, which] = acc[a, which, block(2 + other)].astype(BF16)
        mate_back(a).start()
        return carry

    lax.fori_loop(0, 2, key_side, 0)

    def query_side(a, carry):
        for late in (1, 0):
            x = block_of(late)
            for half in range(2):
                turned_keys = jnp.transpose(kv[a, 0, key_rows(x, half)])
                for quad in range(quads):
                    ds = ds_buf[2 * a + late, half, :, pl.ds(quad * LANES, LANES)]
                    dq = jnp.dot(turned_keys, ds, preferred_element_type=F32).astype(BF16)
                    dq = jnp.transpose(dq)
                    for h in range(QUAD):
                        dq_buf[
                            a, late, pl.ds(half * HALF, HALF),
                            pl.ds((quad * QUAD + h) * HEAD_SIZE, HEAD_SIZE),
                        ] = dq[h * HALF:(h + 1) * HALF]
            if late:
                dq_mate(a).start()
            else:
                dq_own(a).start()
        return carry

    lax.fori_loop(0, 2, query_side, 0)
    finish(0)
    finish(1)
    gain2_whole = remote(g_in2, g_in2, gain2_sem.at[0], gain2_sem.at[1], mate)
    gain2_whole.wait_recv()
    lanes = g_sum[0] + jnp.sum(g_in2[...], axis=0)
    lane1 = lax.broadcasted_iota(jnp.int32, (1, 2 * HALF), 1)
    gain_out[0] = jnp.sum(jnp.where(lane1 < HALF, lanes, 0.0))
    gain_out[1] = jnp.sum(jnp.where(lane1 < HALF, 0.0, lanes))

    gain2_whole.wait_send()

    def gain_left(index, carry):
        @pl.when(chips * core + index != me)
        def _():
            gain_copy1(index).wait_send()

        return carry

    lax.fori_loop(0, chips, gain_left, 0)
    for a in range(2):
        for which in range(2):
            halo_whole(a, which).wait_send()
            mate_kv(a, which).wait_send()
        mate_qg(a).wait_send()
        back_whole(a).wait_send()
        mate_back(a).wait_send()
        dq_own(a).wait()
        dq_mate(a).wait_send()
        dq_from(a).wait_recv()
    for head in range(KEY_VALUE_HEADS):
        for which in range(2):
            dkv_out(head, which).wait()


def hand_over(dq_in, dk_in, dv_in, gain_in, dq_out, dk_out, dv_out, gain_to, dq_buf, dk_buf, dv_buf, gain_buf, sems):
    trips = [
        (dk_in, dk_buf, dk_out),
        (dv_in, dv_buf, dv_out),
        (gain_in, gain_buf, gain_to),
    ]
    for i in range(HAND_PARTS):
        rows = pl.ds(i * (BLOCK // HAND_PARTS), BLOCK // HAND_PARTS)
        trips.append((dq_in.at[rows], dq_buf.at[rows], dq_out.at[rows]))
    there = [pltpu.make_async_copy(x, y, sems.at[0, i]) for i, (x, y, _) in enumerate(trips)]
    back = [pltpu.make_async_copy(y, z, sems.at[1, i]) for i, (_, y, z) in enumerate(trips)]
    for copy in there:
        copy.start()
    for arrive, leave in zip(there, back):
        arrive.wait()
        leave.start()
    for copy in back:
        copy.wait()


def body(queries, keys, values, score_gain, grad, segment_ids):
    seq_size = lax.axis_size("seq")
    dp_size = lax.axis_size("dp")
    tokens = queries.shape[1]
    factor = 1.0 / (dp_size * tokens * seq_size)
    hbm = pl.BlockSpec(memory_space=pltpu.HBM)
    heads = KEY_VALUE_HEADS
    quads = GROUP // QUAD
    pair = pltpu.SemaphoreType.DMA((2,))
    four = pltpu.SemaphoreType.DMA((2, 2))
    wide = GROUP * HEAD_SIZE
    dq, dk, dv, gain = pl.pallas_call(
        functools.partial(kernel, seq_size, dp_size, factor),
        out_shape=(
            jax.ShapeDtypeStruct((BLOCK, QUERY_HEADS * HEAD_SIZE), BF16),
            jax.ShapeDtypeStruct((BLOCK, heads * HEAD_SIZE), BF16),
            jax.ShapeDtypeStruct((BLOCK, heads * HEAD_SIZE), BF16),
            jax.ShapeDtypeStruct((2,), F32),
        ),
        in_specs=[hbm] * 6,
        out_specs=(hbm, hbm, hbm, pl.BlockSpec(memory_space=pltpu.SMEM)),
        scratch_shapes=[
            pltpu.VMEM((2, 2, 2 * BLOCK, wide), BF16),
            pltpu.VMEM((2, 2, 4 * BLOCK, HEAD_SIZE), BF16),
            pltpu.VMEM((2, 2, 2, BLOCK, HEAD_SIZE), BF16),
            pltpu.VMEM((heads, 2, BLOCK, HEAD_SIZE), BF16),
            pltpu.VMEM((2, 2, BLOCK, HEAD_SIZE), BF16),
            pltpu.VMEM((2, 2, BLOCK, HEAD_SIZE), BF16),
            pltpu.VMEM((2, 2, 4 * BLOCK, HEAD_SIZE), F32),
            pltpu.VMEM((2, 2, BLOCK, wide), BF16),
            pltpu.VMEM((heads, 2, BLOCK, HEAD_SIZE), BF16),
            pltpu.VMEM((4 * BLOCK, BLOCK), F32),
            pltpu.VMEM((4, WINDOW, BLOCK), F32),
            pltpu.VMEM((2, quads, WINDOW, LANES), F32),
            pltpu.VMEM((2, quads, WINDOW, LANES), F32),
            pltpu.VMEM((2, quads, WINDOW, LANES), F32),
            pltpu.VMEM((4, 2, WINDOW, quads * LANES), BF16),
            pltpu.VMEM((4, 2, WINDOW, quads * LANES), BF16),
            pltpu.VMEM((1, tokens * seq_size), jnp.int32),
            pltpu.SMEM((QUERY_HEADS,), F32),
            pltpu.VMEM((quads, 1, LANES), F32),
            pltpu.VMEM((seq_size // 2, 1, 2 * HALF), F32),
            pltpu.VMEM((seq_size // 2, 1, 2 * HALF), F32),
            pltpu.VMEM((1, 1, 2 * HALF), F32),
            pltpu.VMEM((dp_size - 1, 1, 2 * HALF), F32),
            pair, pair, four, four, four, four, pair, pair,
            pair,
            pltpu.SemaphoreType.DMA((heads,)),
            pair, pair, pair, pair, pair,
            pltpu.SemaphoreType.DMA((heads, 2)),
            pltpu.SemaphoreType.DMA((seq_size // 2,)),
            pltpu.SemaphoreType.DMA((seq_size // 2,)),
            pair, pair,
        ],
        compiler_params=pltpu.CompilerParams(
            collective_id=0, has_side_effects=True, vmem_limit_bytes=VMEM_BYTES
        ),
        cost_estimate=pl.CostEstimate(
            flops=2 * 5 * BLOCK * WINDOW * HEAD_SIZE * QUERY_HEADS,
            bytes_accessed=4 * 1024 * 1024,
            transcendentals=BLOCK * WINDOW * QUERY_HEADS,
        ),
    )(queries[0], keys[0], values[0], score_gain, grad[0], segment_ids)
    results = (dq, dk, dv, gain)
    dq, dk, dv, gain = pl.pallas_call(
        hand_over,
        out_shape=tuple(jax.ShapeDtypeStruct(x.shape, x.dtype) for x in results),
        in_specs=[hbm] * 4,
        out_specs=(hbm,) * 4,
        scratch_shapes=[
            *[pltpu.VMEM(x.shape, x.dtype) for x in results[:3]],
            pltpu.SMEM(gain.shape, gain.dtype),
            pltpu.SemaphoreType.DMA((2, HAND_PARTS + 3)),
        ],
        compiler_params=pltpu.CompilerParams(vmem_limit_bytes=VMEM_BYTES),
    )(*results)
    return dq[None], dk[None], dv[None], gain


def solution(mesh):
    return jax.shard_map(
        body,
        mesh=mesh,
        in_specs=(
            P("dp", "seq", None),
            P("dp", "seq", None),
            P("dp", "seq", None),
            P(),
            P("dp", "seq", None),
            P("dp", None),
        ),
        out_specs=(P("dp", "seq", None), P("dp", "seq", None), P("dp", "seq", None), P("seq")),
        check_vma=False,
    )
```

```python
import functools
import math

import jax
import jax.numpy as jnp
from jax import lax
from jax.experimental import pallas as pl
from jax.experimental.pallas import tpu as pltpu
from jax.sharding import PartitionSpec as P

QUERY_HEADS = 32
KEY_VALUE_HEADS = 4
HEAD_SIZE = 128
GROUP = QUERY_HEADS // KEY_VALUE_HEADS
BLOCK = 128
HALF = 64
WINDOW = 320
QUAD = 4
LANES = QUAD * HALF
CHUNK = 64
HAND_PARTS = 4
LEADER = 7
VMEM_BYTES = 64 * 1024 * 1024
LOG2E = math.log2(math.e)
SCALE = HEAD_SIZE ** -0.5
BF16 = jnp.bfloat16
F32 = jnp.float32
NT = (((1,), (1,)), ((), ()))
TN = (((0,), (0,)), ((), ()))


def fold_rows(x):
    return jnp.sum(x.reshape(x.shape[0] // 8, 8, x.shape[1]), axis=0)


def kernel(
    seq_size, dp_size, factor,
    q_hbm, k_hbm, v_hbm, gain_hbm, g_hbm, seg_hbm,
    dq_hbm, dk_hbm, dv_hbm, gain_out,
    qg, kv, ret_send, ret, mate_send, mate_in, acc, dq_buf, dkv_buf, seg_rows, bias,
    s_buf, dp_buf, y_buf, p_buf, ds_buf, seg_ref, gain_ref,
    g_rows, g_part, g_in1, g_sum, g_in2, g_total,
    in_sem, own_sem, halo_send, halo_recv, mate_kv_send, mate_kv_recv, mate_qg_send, mate_qg_recv,
    back_send, back_recv, mate_back_send, mate_back_recv, dq_sem, mate_dq_send, mate_dq_recv,
    dkv_sem, gain1_send, gain1_recv, gain2_sem, gain3_sem, small_sem, ready,
):
    me = lax.axis_index("seq")
    row = lax.axis_index("dp")
    chips = seq_size // 2
    chip = lax.div(me, 2)
    core = me - 2 * chip
    other = 1 - core
    mate = 2 * chip + other
    next_chip = lax.rem(chip + 1, chips)
    last_chip = lax.rem(chip + chips - 1, chips)

    def thin(head):
        return pl.ds(pl.multiple_of(head * HEAD_SIZE, HEAD_SIZE), HEAD_SIZE)

    def wide(head):
        return pl.ds(pl.multiple_of(head * (GROUP * HEAD_SIZE), GROUP * HEAD_SIZE), GROUP * HEAD_SIZE)

    def block(index):
        return pl.ds(pl.multiple_of(index * BLOCK, BLOCK), BLOCK)

    def remote(source, target, send, recv, device):
        return pltpu.make_async_remote_copy(
            src_ref=source,
            dst_ref=target,
            send_sem=send,
            recv_sem=recv,
            device_id={"seq": device},
            device_id_type=pl.DeviceIdType.MESH,
        )

    barrier = pltpu.get_barrier_semaphore()

    def greet_seq(i, carry):
        there = lax.rem(me - i + seq_size, seq_size)

        @pl.when(there != LEADER)
        def _():
            pl.semaphore_signal(
                barrier, inc=1, device_id={"seq": there}, device_id_type=pl.DeviceIdType.MESH
            )

        return carry

    def greet_dp(i, carry):
        pl.semaphore_signal(
            barrier, inc=1, device_id={"dp": lax.rem(row + i, dp_size)}, device_id_type=pl.DeviceIdType.MESH
        )
        return carry

    lax.fori_loop(1, seq_size, greet_seq, 0)

    @pl.when(me == LEADER)
    def _():
        lax.fori_loop(1, dp_size, greet_dp, 0)

    for a in range(2):
        head = 2 * core + a
        pltpu.make_async_copy(k_hbm.at[:, thin(head)], kv.at[a, 0, block(2 + core)], own_sem.at[a]).start()
        pltpu.make_async_copy(v_hbm.at[:, thin(head)], kv.at[a, 1, block(2 + core)], own_sem.at[a]).start()
        pltpu.make_async_copy(q_hbm.at[:, wide(head)], qg.at[a, 0, block(core)], in_sem.at[a]).start()
        pltpu.make_async_copy(g_hbm.at[:, wide(head)], qg.at[a, 1, block(core)], in_sem.at[a]).start()
    seg_copy = pltpu.make_async_copy(seg_hbm, seg_ref, small_sem.at[0])
    gain_copy = pltpu.make_async_copy(gain_hbm, gain_ref, small_sem.at[1])
    seg_copy.start()
    gain_copy.start()

    @pl.when(me != LEADER)
    def _():
        pl.semaphore_wait(barrier, seq_size - 1)
        pl.semaphore_signal(
            ready, inc=1, device_id={"seq": LEADER}, device_id_type=pl.DeviceIdType.MESH
        )

    @pl.when(me == LEADER)
    def _():
        pl.semaphore_wait(ready, seq_size - 1)

    def halo_start(a):
        for which, source in enumerate((k_hbm, v_hbm)):
            for to_core in range(2):
                remote(
                    source.at[:, thin(2 * to_core + a)],
                    kv.at[a, which, block(core)],
                    halo_send.at[a, which],
                    halo_recv.at[a, which],
                    2 * next_chip + to_core,
                ).start()

    def halo_whole(a, which):
        part = kv.at[a, which, pl.ds(0, 2 * BLOCK)]
        return remote(part, part, halo_send.at[a, which], halo_recv.at[a, which], 2 * next_chip)

    def mate_start(a):
        head = 2 * other + a
        for which, source in enumerate((k_hbm, v_hbm)):
            remote(
                source.at[:, thin(head)], kv.at[a, which, block(2 + core)],
                mate_kv_send.at[a, which], mate_kv_recv.at[a, which], mate,
            ).start()
        for which, source in enumerate((q_hbm, g_hbm)):
            remote(
                source.at[:, wide(head)], qg.at[a, which, block(core)],
                mate_qg_send.at[a], mate_qg_recv.at[a], mate,
            ).start()

    def mate_kv(a, which):
        part = kv.at[a, which, block(2 + other)]
        return remote(part, part, mate_kv_send.at[a, which], mate_kv_recv.at[a, which], mate)

    def mate_qg(a):
        part = qg.at[a, :, block(other)]
        return remote(part, part, mate_qg_send.at[a], mate_qg_recv.at[a], mate)

    halo_start(0)
    mate_start(0)
    mate_start(1)
    acc[...] = jnp.zeros(acc.shape, F32)
    seg_copy.wait()
    gain_copy.wait()

    def ids_of(index):
        place = pl.multiple_of(lax.rem(2 * chip + index + seq_size, seq_size) * BLOCK, BLOCK)
        return seg_ref[:, pl.ds(place, BLOCK)].astype(F32)

    for b in range(4):
        seg_rows[pl.ds(b * BLOCK, BLOCK)] = jnp.transpose(
            jnp.broadcast_to(ids_of(b - 2), (BLOCK, BLOCK))
        )
    lane8 = lax.broadcasted_iota(jnp.int32, (8, BLOCK), 1)
    key_place = lax.broadcasted_iota(jnp.int32, (WINDOW, BLOCK), 0)
    lane = lax.broadcasted_iota(jnp.int32, (WINDOW, BLOCK), 1)
    causal = key_place <= 2 * BLOCK + jnp.where(lane < HALF, lane, lane - HALF)
    for x in range(2):
        query_ids = jnp.broadcast_to(ids_of(x), (8, BLOCK))
        turned = pltpu.roll(query_ids, HALF, 1)
        for half in range(2):
            start = x * BLOCK + half * HALF
            ids = jnp.where((lane8 < HALF) == (half == 0), query_ids, turned)[0:1]
            inside = (chip - 1) * (2 * BLOCK) + start + key_place >= 0
            allowed = (seg_rows[pl.ds(start, WINDOW)] == ids) & causal & inside
            bias[2 * x + half] = jnp.where(allowed, 0.0, -1e30)

    lane_wide = lax.broadcasted_iota(jnp.int32, (1, LANES), 1)
    quads = GROUP // QUAD

    def back_copy(a, place):
        return remote(
            ret_send.at[a, place], ret.at[2 * core + a],
            back_send.at[a], back_recv.at[2 * core + a], 2 * last_chip + place,
        )

    def back_whole(a):
        return remote(ret_send.at[a], ret_send.at[a], back_send.at[a], back_recv.at[a], 2 * last_chip)

    def back_from(head):
        return remote(ret.at[head], ret.at[head], back_send.at[0], back_recv.at[head], 2 * last_chip)

    def mate_back(a):
        return remote(
            mate_send.at[a], mate_in.at[a], mate_back_send.at[a], mate_back_recv.at[a], mate
        )

    def dkv_out(head, which):
        target = (dk_hbm, dv_hbm)[which]
        return pltpu.make_async_copy(
            dkv_buf.at[head, which], target.at[:, thin(head)], dkv_sem.at[head, which]
        )

    def finish(a):
        mine = 2 * core + a
        theirs = 2 * other + a
        back_from(mine).wait_recv()
        for which in range(2):
            total = acc[a, which, block(2 + core)] + ret[mine, which].astype(F32)
            dkv_buf[mine, which] = total.astype(BF16)
            dkv_out(mine, which).start()
        mate_back(a).wait_recv()
        back_from(theirs).wait_recv()
        for which in range(2):
            total = mate_in[a, which].astype(F32) + ret[theirs, which].astype(F32)
            dkv_buf[theirs, which] = total.astype(BF16)
            dkv_out(theirs, which).start()

    def dq_own(a):
        return pltpu.make_async_copy(dq_buf.at[a, 0], dq_hbm.at[:, wide(2 * core + a)], dq_sem.at[a])

    def dq_mate(a):
        return remote(
            dq_buf.at[a, 1], dq_hbm.at[:, wide(2 * core + a)], mate_dq_send.at[a], mate_dq_recv.at[a], mate
        )

    def dq_from(a):
        part = dq_hbm.at[:, wide(2 * other + a)]
        return remote(part, part, mate_dq_send.at[a], mate_dq_recv.at[a], mate)

    def gain_copy1(source):
        return remote(g_part, g_in1.at[source], gain1_send.at[0], gain1_recv.at[source], LEADER)

    def gain_copy3(target):
        return remote(g_total.at[0], g_total.at[1], gain3_sem.at[0], gain3_sem.at[1], target)

    def block_of(late):
        return core + late - 2 * core * late

    def key_rows(x, half):
        return pl.ds(pl.multiple_of(x * BLOCK + half * HALF, HALF), WINDOW)

    def stack(a, x, which, half, heads):
        rows = pl.ds(pl.multiple_of(x * BLOCK + half * HALF, HALF), HALF)
        return jnp.concatenate(
            [qg[a, which, rows, pl.ds(h * HEAD_SIZE, HEAD_SIZE)] for h in heads], axis=0
        )

    def scores(number, carry):
        a = lax.div(number, 2)
        late = number - 2 * a
        x = block_of(late)

        @pl.when(late == 0)
        def _():
            own = kv.at[a, :, block(2 + core)]
            pltpu.make_async_copy(own, own, own_sem.at[a]).wait()
            held = qg.at[a, :, block(core)]
            pltpu.make_async_copy(held, held, in_sem.at[a]).wait()
            mate_kv(a, 0).wait_recv()
            halo_whole(a, 0).wait_recv()

        @pl.when(late == 1)
        def _():
            mate_qg(a).wait_recv()

        def product(target, which, half, quad):
            heads = range(quad * QUAD, quad * QUAD + QUAD)
            target[half, quad] = lax.dot_general(
                kv[a, which, key_rows(x, half)], stack(a, x, which, half, heads), NT,
                preferred_element_type=F32,
            )

        def middle(half, quad):
            gains = [gain_ref[(2 * core + a) * GROUP + quad * QUAD + h] for h in range(QUAD)]
            gain = jnp.where(
                lane_wide < 2 * HALF,
                jnp.where(lane_wide < HALF, gains[0], gains[1]),
                jnp.where(lane_wide < 3 * HALF, gains[2], gains[3]),
            )
            to_score = gain * (SCALE * LOG2E)
            to_grad = gain * SCALE
            lanes = pl.ds(quad * LANES, LANES)
            chunks = [pl.ds(i, CHUNK) for i in range(0, WINDOW, CHUNK)]
            top = jnp.full((8, LANES), -3e38, F32)
            for rows in chunks:
                shade = bias[2 * x + half, rows]
                y = s_buf[half, quad, rows] * to_score + jnp.concatenate([shade, shade], axis=1)
                y_buf[half, quad, rows] = y
                top = jnp.maximum(top, jnp.max(y.reshape(CHUNK // 8, 8, LANES), axis=0))
            top = jnp.max(top, axis=0, keepdims=True)
            total = jnp.zeros((8, LANES), F32)
            dot = jnp.zeros((8, LANES), F32)
            for rows in chunks:
                e = jnp.exp2(y_buf[half, quad, rows] - top)
                y_buf[half, quad, rows] = e
                total = total + fold_rows(e)
                dot = dot + fold_rows(e * dp_buf[half, quad, rows])
            inverse = 1.0 / jnp.sum(total, axis=0, keepdims=True)
            delta = jnp.sum(dot, axis=0, keepdims=True) * inverse
            spread = jnp.zeros((8, LANES), F32)
            for rows in chunks:
                p = y_buf[half, quad, rows] * inverse
                dscore = p * (dp_buf[half, quad, rows] - delta)
                spread = spread + fold_rows(dscore * s_buf[half, quad, rows])
                p_buf[number, half, rows, lanes] = p.astype(BF16)
                ds_buf[number, half, rows, lanes] = (dscore * to_grad).astype(BF16)
            return jnp.sum(spread, axis=0, keepdims=True) * (SCALE * factor)

        product(s_buf, 0, 0, 0)
        product(s_buf, 0, 0, 1)
        product(s_buf, 0, 1, 0)
        product(s_buf, 0, 1, 1)

        @pl.when(late == 0)
        def _():
            mate_kv(a, 1).wait_recv()
            halo_whole(a, 1).wait_recv()

            @pl.when(a == 0)
            def _():
                halo_start(1)

        product(dp_buf, 1, 0, 0)
        product(dp_buf, 1, 0, 1)
        term00 = middle(0, 0)
        product(dp_buf, 1, 1, 0)
        term01 = middle(0, 1)
        product(dp_buf, 1, 1, 1)
        term10 = middle(1, 0)
        term11 = middle(1, 1)
        terms = [term00 + term10, term01 + term11]

        @pl.when(late == 0)
        def _():
            for quad in range(quads):
                g_rows[quad] = terms[quad]

        @pl.when(late == 1)
        def _():
            for quad in range(quads):
                both = g_rows[quad] + terms[quad]
                for side in range(2):
                    index = a * (2 * quads) + quad * 2 + side
                    g_part[pl.ds(index, 1), :] = both[:, side * 2 * HALF:(side + 1) * 2 * HALF]

        return carry

    lax.fori_loop(0, 4, scores, 0)

    @pl.when(me != LEADER)
    def _():
        gain_copy1(me).start()

    def gain_arrive(i, carry):
        @pl.when(i != LEADER)
        def _():
            gain_copy1(i).wait_recv()

        return carry

    def gain_send2(i, carry):
        pltpu.make_async_remote_copy(
            src_ref=g_sum.at[0],
            dst_ref=g_in2.at[i - 1],
            send_sem=gain2_sem.at[0],
            recv_sem=gain2_sem.at[1],
            device_id={"dp": lax.rem(row + i, dp_size)},
            device_id_type=pl.DeviceIdType.MESH,
        ).start()
        return carry

    @pl.when(me == LEADER)
    def _():
        g_in1[LEADER] = g_part[...]
        lax.fori_loop(0, seq_size, gain_arrive, 0)
        pairs = lax.broadcasted_iota(jnp.int32, (chips, 2 * HALF), 0)
        lanes = lax.broadcasted_iota(jnp.int32, (chips, 2 * HALF), 1)
        sums = jnp.zeros((chips, 2 * HALF), F32)
        for side in range(2):
            held = g_in1[side]
            for i in range(1, chips):
                held = held + g_in1[2 * i + side]
            low = jnp.sum(jnp.where(lanes < HALF, held, 0.0), axis=1, keepdims=True)
            high = jnp.sum(jnp.where(lanes < HALF, 0.0, held), axis=1, keepdims=True)
            place = 2 * (pairs + chips * side)
            sums = sums + jnp.where(lanes == place, low, 0.0) + jnp.where(lanes == place + 1, high, 0.0)
        g_sum[0] = jnp.sum(sums, axis=0, keepdims=True)
        pl.semaphore_wait(barrier, dp_size - 1)
        lax.fori_loop(1, dp_size, gain_send2, 0)

    def key_side(a, carry):
        for late in range(2):
            x = block_of(late)
            for half in range(2):
                rows = key_rows(x, half)
                acc[a, 0, rows] += jnp.dot(
                    ds_buf[2 * a + late, half], stack(a, x, 0, half, range(GROUP)),
                    preferred_element_type=F32,
                )
                acc[a, 1, rows] += jnp.dot(
                    p_buf[2 * a + late, half], stack(a, x, 1, half, range(GROUP)),
                    preferred_element_type=F32,
                )
        for place in range(2):
            for which in range(2):
                ret_send[a, place, which] = acc[a, which, pl.ds(place * BLOCK, BLOCK)].astype(BF16)
            back_copy(a, place).start()
        for which in range(2):
            mate_send[a, which] = acc[a, which, block(2 + other)].astype(BF16)
        mate_back(a).start()
        return carry

    lax.fori_loop(0, 2, key_side, 0)

    def query_side(a, carry):
        for late in (1, 0):
            x = block_of(late)
            for half in range(2):
                turned_keys = jnp.transpose(kv[a, 0, key_rows(x, half)])
                for quad in range(quads):
                    ds = ds_buf[2 * a + late, half, :, pl.ds(quad * LANES, LANES)]
                    dq = jnp.dot(turned_keys, ds, preferred_element_type=F32).astype(BF16)
                    dq = jnp.transpose(dq)
                    for h in range(QUAD):
                        dq_buf[
                            a, late, pl.ds(half * HALF, HALF),
                            pl.ds((quad * QUAD + h) * HEAD_SIZE, HEAD_SIZE),
                        ] = dq[h * HALF:(h + 1) * HALF]
            if late:
                dq_mate(a).start()
            else:
                dq_own(a).start()
        return carry

    lax.fori_loop(0, 2, query_side, 0)
    finish(0)
    finish(1)
    gain2_whole = remote(g_in2, g_in2, gain2_sem.at[0], gain2_sem.at[1], mate)

    def gain_send3(i, carry):
        gain_copy3(lax.rem(me + i, seq_size)).start()
        return carry

    @pl.when(me == LEADER)
    def _():
        gain2_whole.wait_recv()
        g_total[0] = g_sum[0] + jnp.sum(g_in2[...], axis=0)
        lax.fori_loop(1, seq_size, gain_send3, 0)
        g_total[1] = g_total[0]

    @pl.when(me != LEADER)
    def _():
        gain_copy3(mate).wait_recv()

    lane1 = lax.broadcasted_iota(jnp.int32, (1, 2 * HALF), 1)
    for side in range(2):
        gain_out[side] = jnp.sum(jnp.where(lane1 == 2 * me + side, g_total[1], 0.0))

    @pl.when(me == LEADER)
    def _():
        gain2_whole.wait_send()
        sent = g_in2.at[pl.ds(0, seq_size - 1)]
        remote(sent, sent, gain3_sem.at[0], gain3_sem.at[1], mate).wait_send()

    @pl.when(me != LEADER)
    def _():
        gain_copy1(me).wait_send()

    for a in range(2):
        for which in range(2):
            halo_whole(a, which).wait_send()
            mate_kv(a, which).wait_send()
        mate_qg(a).wait_send()
        back_whole(a).wait_send()
        mate_back(a).wait_send()
        dq_own(a).wait()
        dq_mate(a).wait_send()
        dq_from(a).wait_recv()
    for head in range(KEY_VALUE_HEADS):
        for which in range(2):
            dkv_out(head, which).wait()


def hand_over(dq_in, dk_in, dv_in, gain_in, dq_out, dk_out, dv_out, gain_to, dq_buf, dk_buf, dv_buf, gain_buf, sems):
    trips = [
        (dk_in, dk_buf, dk_out),
        (dv_in, dv_buf, dv_out),
        (gain_in, gain_buf, gain_to),
    ]
    for i in range(HAND_PARTS):
        rows = pl.ds(i * (BLOCK // HAND_PARTS), BLOCK // HAND_PARTS)
        trips.append((dq_in.at[rows], dq_buf.at[rows], dq_out.at[rows]))
    there = [pltpu.make_async_copy(x, y, sems.at[0, i]) for i, (x, y, _) in enumerate(trips)]
    back = [pltpu.make_async_copy(y, z, sems.at[1, i]) for i, (_, y, z) in enumerate(trips)]
    for copy in there:
        copy.start()
    for arrive, leave in zip(there, back):
        arrive.wait()
        leave.start()
    for copy in back:
        copy.wait()


def body(queries, keys, values, score_gain, grad, segment_ids):
    seq_size = lax.axis_size("seq")
    dp_size = lax.axis_size("dp")
    tokens = queries.shape[1]
    factor = 1.0 / (dp_size * tokens * seq_size)
    hbm = pl.BlockSpec(memory_space=pltpu.HBM)
    heads = KEY_VALUE_HEADS
    quads = GROUP // QUAD
    pair = pltpu.SemaphoreType.DMA((2,))
    four = pltpu.SemaphoreType.DMA((2, 2))
    wide = GROUP * HEAD_SIZE
    dq, dk, dv, gain = pl.pallas_call(
        functools.partial(kernel, seq_size, dp_size, factor),
        out_shape=(
            jax.ShapeDtypeStruct((BLOCK, QUERY_HEADS * HEAD_SIZE), BF16),
            jax.ShapeDtypeStruct((BLOCK, heads * HEAD_SIZE), BF16),
            jax.ShapeDtypeStruct((BLOCK, heads * HEAD_SIZE), BF16),
            jax.ShapeDtypeStruct((2,), F32),
        ),
        in_specs=[hbm] * 6,
        out_specs=(hbm, hbm, hbm, pl.BlockSpec(memory_space=pltpu.SMEM)),
        scratch_shapes=[
            pltpu.VMEM((2, 2, 2 * BLOCK, wide), BF16),
            pltpu.VMEM((2, 2, 4 * BLOCK, HEAD_SIZE), BF16),
            pltpu.VMEM((2, 2, 2, BLOCK, HEAD_SIZE), BF16),
            pltpu.VMEM((heads, 2, BLOCK, HEAD_SIZE), BF16),
            pltpu.VMEM((2, 2, BLOCK, HEAD_SIZE), BF16),
            pltpu.VMEM((2, 2, BLOCK, HEAD_SIZE), BF16),
            pltpu.VMEM((2, 2, 4 * BLOCK, HEAD_SIZE), F32),
            pltpu.VMEM((2, 2, BLOCK, wide), BF16),
            pltpu.VMEM((heads, 2, BLOCK, HEAD_SIZE), BF16),
            pltpu.VMEM((4 * BLOCK, BLOCK), F32),
            pltpu.VMEM((4, WINDOW, BLOCK), F32),
            pltpu.VMEM((2, quads, WINDOW, LANES), F32),
            pltpu.VMEM((2, quads, WINDOW, LANES), F32),
            pltpu.VMEM((2, quads, WINDOW, LANES), F32),
            pltpu.VMEM((4, 2, WINDOW, quads * LANES), BF16),
            pltpu.VMEM((4, 2, WINDOW, quads * LANES), BF16),
            pltpu.VMEM((1, tokens * seq_size), jnp.int32),
            pltpu.SMEM((QUERY_HEADS,), F32),
            pltpu.VMEM((quads, 1, LANES), F32),
            pltpu.VMEM((seq_size // 2, 2 * HALF), F32),
            pltpu.VMEM((seq_size, seq_size // 2, 2 * HALF), F32),
            pltpu.VMEM((1, 1, 2 * HALF), F32),
            pltpu.VMEM((dp_size - 1, 1, 2 * HALF), F32),
            pltpu.VMEM((2, 1, 2 * HALF), F32),
            pair, pair, four, four, four, four, pair, pair,
            pair,
            pltpu.SemaphoreType.DMA((heads,)),
            pair, pair, pair, pair, pair,
            pltpu.SemaphoreType.DMA((heads, 2)),
            pair,
            pltpu.SemaphoreType.DMA((seq_size,)),
            pair, pair, pair,
            pltpu.SemaphoreType.REGULAR,
        ],
        compiler_params=pltpu.CompilerParams(
            collective_id=0, has_side_effects=True, vmem_limit_bytes=VMEM_BYTES
        ),
        cost_estimate=pl.CostEstimate(
            flops=2 * 5 * BLOCK * WINDOW * HEAD_SIZE * QUERY_HEADS,
            bytes_accessed=4 * 1024 * 1024,
            transcendentals=BLOCK * WINDOW * QUERY_HEADS,
        ),
    )(queries[0], keys[0], values[0], score_gain, grad[0], segment_ids)
    results = (dq, dk, dv, gain)
    dq, dk, dv, gain = pl.pallas_call(
        hand_over,
        out_shape=tuple(jax.ShapeDtypeStruct(x.shape, x.dtype) for x in results),
        in_specs=[hbm] * 4,
        out_specs=(hbm,) * 4,
        scratch_shapes=[
            *[pltpu.VMEM(x.shape, x.dtype) for x in results[:3]],
            pltpu.SMEM(gain.shape, gain.dtype),
            pltpu.SemaphoreType.DMA((2, HAND_PARTS + 3)),
        ],
        compiler_params=pltpu.CompilerParams(vmem_limit_bytes=VMEM_BYTES),
    )(*results)
    return dq[None], dk[None], dv[None], gain


def solution(mesh):
    return jax.shard_map(
        body,
        mesh=mesh,
        in_specs=(
            P("dp", "seq", None),
            P("dp", "seq", None),
            P("dp", "seq", None),
            P(),
            P("dp", "seq", None),
            P("dp", None),
        ),
        out_specs=(P("dp", "seq", None), P("dp", "seq", None), P("dp", "seq", None), P("seq")),
        check_vma=False,
    )
```

```python
import functools
import math

import jax
import jax.numpy as jnp
from jax import lax
from jax.experimental import pallas as pl
from jax.experimental.pallas import tpu as pltpu
from jax.sharding import PartitionSpec as P

QUERY_HEADS = 32
KEY_VALUE_HEADS = 4
HEAD_SIZE = 128
GROUP = QUERY_HEADS // KEY_VALUE_HEADS
BLOCK = 128
PART = 32
PARTS = BLOCK // PART
WINDOW = 288
LANES = GROUP * PART
SIDE = 128
CHUNK = 32
HAND_PARTS = 4
LEADER = 7
VMEM_BYTES = 64 * 1024 * 1024
LOG2E = math.log2(math.e)
SCALE = HEAD_SIZE ** -0.5
BF16 = jnp.bfloat16
F32 = jnp.float32
NT = (((1,), (1,)), ((), ()))
TN = (((0,), (0,)), ((), ()))


def fold_rows(x):
    return jnp.sum(x.reshape(x.shape[0] // 8, 8, x.shape[1]), axis=0)


def kernel(
    seq_size, dp_size, factor,
    q_hbm, k_hbm, v_hbm, gain_hbm, g_hbm, seg_hbm,
    dq_hbm, dk_hbm, dv_hbm, gain_out,
    qg, kv, ret_send, ret, mate_send, mate_in, acc, dq_buf, dkv_buf, seg_rows, bias,
    s_buf, dp_buf, y_buf, p_buf, ds_buf, seg_ref, gain_ref,
    g_part, g_in1, g_sum, g_in2, g_total,
    in_sem, own_sem, halo_send, halo_recv, mate_kv_send, mate_kv_recv, mate_qg_send, mate_qg_recv,
    back_send, back_recv, mate_back_send, mate_back_recv, dq_sem, mate_dq_send, mate_dq_recv,
    dkv_sem, gain1_send, gain1_recv, gain2_sem, gain3_sem, small_sem, ready,
):
    me = lax.axis_index("seq")
    row = lax.axis_index("dp")
    chips = seq_size // 2
    chip = lax.div(me, 2)
    core = me - 2 * chip
    other = 1 - core
    mate = 2 * chip + other
    next_chip = lax.rem(chip + 1, chips)
    last_chip = lax.rem(chip + chips - 1, chips)

    def thin(head):
        return pl.ds(pl.multiple_of(head * HEAD_SIZE, HEAD_SIZE), HEAD_SIZE)

    def wide(head):
        return pl.ds(pl.multiple_of(head * (GROUP * HEAD_SIZE), GROUP * HEAD_SIZE), GROUP * HEAD_SIZE)

    def block(index):
        return pl.ds(pl.multiple_of(index * BLOCK, BLOCK), BLOCK)

    def remote(source, target, send, recv, device):
        return pltpu.make_async_remote_copy(
            src_ref=source,
            dst_ref=target,
            send_sem=send,
            recv_sem=recv,
            device_id={"seq": device},
            device_id_type=pl.DeviceIdType.MESH,
        )

    barrier = pltpu.get_barrier_semaphore()

    def greet_seq(i, carry):
        there = lax.rem(me - i + seq_size, seq_size)

        @pl.when(there != LEADER)
        def _():
            pl.semaphore_signal(
                barrier, inc=1, device_id={"seq": there}, device_id_type=pl.DeviceIdType.MESH
            )

        return carry

    def greet_dp(i, carry):
        pl.semaphore_signal(
            barrier, inc=1, device_id={"dp": lax.rem(row + i, dp_size)}, device_id_type=pl.DeviceIdType.MESH
        )
        return carry

    lax.fori_loop(1, seq_size, greet_seq, 0)

    @pl.when(me == LEADER)
    def _():
        lax.fori_loop(1, dp_size, greet_dp, 0)

    for a in range(2):
        head = 2 * core + a
        pltpu.make_async_copy(k_hbm.at[:, thin(head)], kv.at[a, 0, block(2 + core)], own_sem.at[a]).start()
        pltpu.make_async_copy(v_hbm.at[:, thin(head)], kv.at[a, 1, block(2 + core)], own_sem.at[a]).start()
        pltpu.make_async_copy(q_hbm.at[:, wide(head)], qg.at[a, 0, pl.ds(0, BLOCK)], in_sem.at[a]).start()
        pltpu.make_async_copy(g_hbm.at[:, wide(head)], qg.at[a, 1, pl.ds(0, BLOCK)], in_sem.at[a]).start()
    seg_copy = pltpu.make_async_copy(seg_hbm, seg_ref, small_sem.at[0])
    gain_copy = pltpu.make_async_copy(gain_hbm, gain_ref, small_sem.at[1])
    seg_copy.start()
    gain_copy.start()

    @pl.when(me != LEADER)
    def _():
        pl.semaphore_wait(barrier, seq_size - 1)
        pl.semaphore_signal(
            ready, inc=1, device_id={"seq": LEADER}, device_id_type=pl.DeviceIdType.MESH
        )

    @pl.when(me == LEADER)
    def _():
        pl.semaphore_wait(ready, seq_size - 1)

    def halo_start(a):
        for which, source in enumerate((k_hbm, v_hbm)):
            for to_core in range(2):
                remote(
                    source.at[:, thin(2 * to_core + a)],
                    kv.at[a, which, block(core)],
                    halo_send.at[a, which],
                    halo_recv.at[a, which],
                    2 * next_chip + to_core,
                ).start()

    def halo_whole(a, which):
        part = kv.at[a, which, pl.ds(0, 2 * BLOCK)]
        return remote(part, part, halo_send.at[a, which], halo_recv.at[a, which], 2 * next_chip)

    def mate_start(a):
        head = 2 * other + a
        for which, source in enumerate((k_hbm, v_hbm)):
            remote(
                source.at[:, thin(head)], kv.at[a, which, block(2 + core)],
                mate_kv_send.at[a, which], mate_kv_recv.at[a, which], mate,
            ).start()
        for which, source in enumerate((q_hbm, g_hbm)):
            remote(
                source.at[:, wide(head)], qg.at[a, which, pl.ds(BLOCK, BLOCK)],
                mate_qg_send.at[a], mate_qg_recv.at[a], mate,
            ).start()

    def mate_kv(a, which):
        part = kv.at[a, which, block(2 + other)]
        return remote(part, part, mate_kv_send.at[a, which], mate_kv_recv.at[a, which], mate)

    def mate_qg(a):
        part = qg.at[a, :, pl.ds(BLOCK, BLOCK)]
        return remote(part, part, mate_qg_send.at[a], mate_qg_recv.at[a], mate)

    halo_start(0)
    mate_start(0)
    mate_start(1)
    acc[...] = jnp.zeros(acc.shape, F32)
    seg_copy.wait()
    gain_copy.wait()

    def ids_of(index):
        place = pl.multiple_of(lax.rem(2 * chip + index + seq_size, seq_size) * BLOCK, BLOCK)
        return seg_ref[:, pl.ds(place, BLOCK)].astype(F32)

    for b in range(4):
        seg_rows[pl.ds(b * BLOCK, BLOCK)] = jnp.transpose(
            jnp.broadcast_to(ids_of(b - 2), (BLOCK, BLOCK))
        )
    def block_of(late):
        return other if late else core

    group8 = lax.broadcasted_iota(jnp.int32, (8, BLOCK), 1) // PART
    key_place = lax.broadcasted_iota(jnp.int32, (WINDOW, BLOCK), 0)
    lane = lax.broadcasted_iota(jnp.int32, (WINDOW, BLOCK), 1)
    causal = key_place <= 2 * BLOCK + lane % PART
    for late in range(2):
        x = block_of(late)
        query_ids = jnp.broadcast_to(ids_of(x), (8, BLOCK))
        rolled = [query_ids] + [pltpu.roll(query_ids, PART * k, 1) for k in range(1, PARTS)]
        for part in range(PARTS):
            start = x * BLOCK + part * PART
            ids = rolled[-part % PARTS]
            for j in range(1, PARTS):
                ids = jnp.where(group8 == j, rolled[(j - part) % PARTS], ids)
            inside = (chip - 1) * (2 * BLOCK) + start + key_place >= 0
            keys_ids = seg_rows[pl.ds(pl.multiple_of(start, PART), WINDOW)]
            allowed = (keys_ids == ids[0:1]) & causal & inside
            bias[late * PARTS + part] = jnp.where(allowed, 0.0, -1e30)

    lane_wide = lax.broadcasted_iota(jnp.int32, (1, LANES), 1)

    def back_copy(a, place):
        return remote(
            ret_send.at[a, place], ret.at[2 * core + a],
            back_send.at[a], back_recv.at[2 * core + a], 2 * last_chip + place,
        )

    def back_whole(a):
        return remote(ret_send.at[a], ret_send.at[a], back_send.at[a], back_recv.at[a], 2 * last_chip)

    def back_from(head):
        return remote(ret.at[head], ret.at[head], back_send.at[0], back_recv.at[head], 2 * last_chip)

    def mate_back(a):
        return remote(
            mate_send.at[a], mate_in.at[a], mate_back_send.at[a], mate_back_recv.at[a], mate
        )

    def dkv_out(head, which):
        target = (dk_hbm, dv_hbm)[which]
        return pltpu.make_async_copy(
            dkv_buf.at[head, which], target.at[:, thin(head)], dkv_sem.at[head, which]
        )

    def finish(a):
        mine = 2 * core + a
        theirs = 2 * other + a
        back_from(mine).wait_recv()
        for which in range(2):
            total = acc[a, which, block(2 + core)] + ret[mine, which].astype(F32)
            dkv_buf[mine, which] = total.astype(BF16)
            dkv_out(mine, which).start()
        mate_back(a).wait_recv()
        back_from(theirs).wait_recv()
        for which in range(2):
            total = mate_in[a, which].astype(F32) + ret[theirs, which].astype(F32)
            dkv_buf[theirs, which] = total.astype(BF16)
            dkv_out(theirs, which).start()

    def dq_own(a):
        return pltpu.make_async_copy(dq_buf.at[a, 0], dq_hbm.at[:, wide(2 * core + a)], dq_sem.at[a])

    def dq_mate(a):
        return remote(
            dq_buf.at[a, 1], dq_hbm.at[:, wide(2 * core + a)], mate_dq_send.at[a], mate_dq_recv.at[a], mate
        )

    def dq_from(a):
        part = dq_hbm.at[:, wide(2 * other + a)]
        return remote(part, part, mate_dq_send.at[a], mate_dq_recv.at[a], mate)

    def gain_copy1(source):
        return remote(g_part, g_in1.at[source], gain1_send.at[0], gain1_recv.at[source], LEADER)

    def gain_copy3(target):
        return remote(g_total.at[0], g_total.at[1], gain3_sem.at[0], gain3_sem.at[1], target)

    def key_rows(late, part):
        return pl.ds(pl.multiple_of(block_of(late) * BLOCK + part * PART, PART), WINDOW)

    def stack(a, late, which, part):
        rows = pl.ds(late * BLOCK + part * PART, PART)
        return jnp.concatenate(
            [qg[a, which, rows, pl.ds(h * HEAD_SIZE, HEAD_SIZE)] for h in range(GROUP)], axis=0
        )

    units = [(late, part) for late in range(2) for part in range(PARTS)]

    def scores(a, carry):
        gain = jnp.full((1, LANES), gain_ref[(2 * core + a) * GROUP], F32)
        for h in range(1, GROUP):
            gain = jnp.where(lane_wide >= h * PART, gain_ref[(2 * core + a) * GROUP + h], gain)
        to_score = gain * (SCALE * LOG2E)
        to_grad = gain * SCALE

        def product(target, which, u):
            late, part = units[u]
            target[u] = lax.dot_general(
                kv[a, which, key_rows(late, part)], stack(a, late, which, part), NT,
                preferred_element_type=F32,
            )

        def middle(u):
            late, part = units[u]
            chunks = [pl.ds(i, CHUNK) for i in range(0, WINDOW, CHUNK)]
            top = jnp.full((8, LANES), -3e38, F32)
            for rows in chunks:
                shade = bias[u, rows]
                y = s_buf[u, rows] * to_score + jnp.concatenate([shade, shade], axis=1)
                y_buf[u, rows] = y
                top = jnp.maximum(top, jnp.max(y.reshape(CHUNK // 8, 8, LANES), axis=0))
            top = jnp.max(top, axis=0, keepdims=True)
            total = jnp.zeros((8, LANES), F32)
            dot = jnp.zeros((8, LANES), F32)
            for rows in chunks:
                e = jnp.exp2(y_buf[u, rows] - top)
                y_buf[u, rows] = e
                total = total + fold_rows(e)
                dot = dot + fold_rows(e * dp_buf[u, rows])
            inverse = 1.0 / jnp.sum(total, axis=0, keepdims=True)
            delta = jnp.sum(dot, axis=0, keepdims=True) * inverse
            spread = jnp.zeros((8, LANES), F32)
            for rows in chunks:
                p = y_buf[u, rows] * inverse
                dscore = p * (dp_buf[u, rows] - delta)
                spread = spread + fold_rows(dscore * s_buf[u, rows])
                p_buf[2 * a + late, part, rows] = p.astype(BF16)
                ds_buf[2 * a + late, part, rows] = (dscore * to_grad).astype(BF16)
            return jnp.sum(spread, axis=0, keepdims=True) * (SCALE * factor)

        own = kv.at[a, :, block(2 + core)]
        pltpu.make_async_copy(own, own, own_sem.at[a]).wait()
        held = qg.at[a, :, pl.ds(0, BLOCK)]
        pltpu.make_async_copy(held, held, in_sem.at[a]).wait()
        mate_kv(a, 0).wait_recv()
        halo_whole(a, 0).wait_recv()
        for u in range(PARTS):
            product(s_buf, 0, u)
        mate_kv(a, 1).wait_recv()
        halo_whole(a, 1).wait_recv()
        mate_qg(a).wait_recv()

        @pl.when(a == 0)
        def _():
            halo_start(1)

        product(dp_buf, 1, 0)
        terms = jnp.zeros((1, LANES), F32)
        for u in range(len(units)):
            if u + 1 < len(units):
                product(dp_buf, 1, u + 1)
            if u + PARTS < len(units):
                product(s_buf, 0, u + PARTS)
            terms = terms + middle(u)
        for side in range(2):
            g_part[pl.ds(2 * a + side, 1), :] = terms[:, side * SIDE:(side + 1) * SIDE]
        return carry

    g_part[...] = jnp.zeros(g_part.shape, F32)
    lax.fori_loop(0, 2, scores, 0)

    @pl.when(me != LEADER)
    def _():
        gain_copy1(me).start()

    def gain_arrive(i, carry):
        @pl.when(i != LEADER)
        def _():
            gain_copy1(i).wait_recv()

        return carry

    def gain_send2(i, carry):
        pltpu.make_async_remote_copy(
            src_ref=g_sum.at[0],
            dst_ref=g_in2.at[i - 1],
            send_sem=gain2_sem.at[0],
            recv_sem=gain2_sem.at[1],
            device_id={"dp": lax.rem(row + i, dp_size)},
            device_id_type=pl.DeviceIdType.MESH,
        ).start()
        return carry

    @pl.when(me == LEADER)
    def _():
        g_in1[LEADER] = g_part[...]
        lax.fori_loop(0, seq_size, gain_arrive, 0)
        row_of = lax.broadcasted_iota(jnp.int32, (chips, SIDE), 0)
        lanes = lax.broadcasted_iota(jnp.int32, (chips, SIDE), 1)
        sums = jnp.zeros((chips, SIDE), F32)
        for side in range(2):
            held = g_in1[side]
            for i in range(1, chips):
                held = held + g_in1[2 * i + side]
            for h in range(PARTS):
                head_sum = jnp.sum(jnp.where(lanes // PART == h, held, 0.0), axis=1, keepdims=True)
                place = (QUERY_HEADS // 2) * side + PARTS * row_of + h
                sums = sums + jnp.where((lanes == place) & (row_of < PARTS), head_sum, 0.0)
        g_sum[0] = jnp.sum(sums, axis=0, keepdims=True)
        pl.semaphore_wait(barrier, dp_size - 1)
        lax.fori_loop(1, dp_size, gain_send2, 0)

    def key_side(a, carry):
        for late in range(2):
            for part in range(PARTS):
                rows = key_rows(late, part)
                acc[a, 0, rows] += jnp.dot(
                    ds_buf[2 * a + late, part], stack(a, late, 0, part), preferred_element_type=F32
                )
                acc[a, 1, rows] += jnp.dot(
                    p_buf[2 * a + late, part], stack(a, late, 1, part), preferred_element_type=F32
                )
        for place in range(2):
            for which in range(2):
                ret_send[a, place, which] = acc[a, which, pl.ds(place * BLOCK, BLOCK)].astype(BF16)
            back_copy(a, place).start()
        for which in range(2):
            mate_send[a, which] = acc[a, which, block(2 + other)].astype(BF16)
        mate_back(a).start()
        return carry

    lax.fori_loop(0, 2, key_side, 0)

    def query_side(a, carry):
        for late in (1, 0):
            for part in range(PARTS):
                turned_keys = jnp.transpose(kv[a, 0, key_rows(late, part)])
                dq = jnp.dot(turned_keys, ds_buf[2 * a + late, part], preferred_element_type=F32)
                dq = jnp.transpose(dq.astype(BF16))
                for h in range(GROUP):
                    dq_buf[
                        a, late, pl.ds(part * PART, PART), pl.ds(h * HEAD_SIZE, HEAD_SIZE)
                    ] = dq[h * PART:(h + 1) * PART]
            if late:
                dq_mate(a).start()
            else:
                dq_own(a).start()
        return carry

    lax.fori_loop(0, 2, query_side, 0)
    finish(0)
    finish(1)
    gain2_whole = remote(g_in2, g_in2, gain2_sem.at[0], gain2_sem.at[1], mate)

    def gain_send3(i, carry):
        gain_copy3(lax.rem(me + i, seq_size)).start()
        return carry

    @pl.when(me == LEADER)
    def _():
        gain2_whole.wait_recv()
        g_total[0] = g_sum[0] + jnp.sum(g_in2[...], axis=0)
        lax.fori_loop(1, seq_size, gain_send3, 0)
        g_total[1] = g_total[0]

    @pl.when(me != LEADER)
    def _():
        gain_copy3(mate).wait_recv()

    lane1 = lax.broadcasted_iota(jnp.int32, (1, SIDE), 1)
    for side in range(2):
        gain_out[side] = jnp.sum(jnp.where(lane1 == 2 * me + side, g_total[1], 0.0))

    @pl.when(me == LEADER)
    def _():
        gain2_whole.wait_send()
        sent = g_in2.at[pl.ds(0, seq_size - 1)]
        remote(sent, sent, gain3_sem.at[0], gain3_sem.at[1], mate).wait_send()

    @pl.when(me != LEADER)
    def _():
        gain_copy1(me).wait_send()

    for a in range(2):
        for which in range(2):
            halo_whole(a, which).wait_send()
            mate_kv(a, which).wait_send()
        mate_qg(a).wait_send()
        back_whole(a).wait_send()
        mate_back(a).wait_send()
        dq_own(a).wait()
        dq_mate(a).wait_send()
        dq_from(a).wait_recv()
    for head in range(KEY_VALUE_HEADS):
        for which in range(2):
            dkv_out(head, which).wait()


def hand_over(dq_in, dk_in, dv_in, gain_in, dq_out, dk_out, dv_out, gain_to, dq_buf, dk_buf, dv_buf, gain_buf, sems):
    trips = [
        (dk_in, dk_buf, dk_out),
        (dv_in, dv_buf, dv_out),
        (gain_in, gain_buf, gain_to),
    ]
    for i in range(HAND_PARTS):
        rows = pl.ds(i * (BLOCK // HAND_PARTS), BLOCK // HAND_PARTS)
        trips.append((dq_in.at[rows], dq_buf.at[rows], dq_out.at[rows]))
    there = [pltpu.make_async_copy(x, y, sems.at[0, i]) for i, (x, y, _) in enumerate(trips)]
    back = [pltpu.make_async_copy(y, z, sems.at[1, i]) for i, (_, y, z) in enumerate(trips)]
    for copy in there:
        copy.start()
    for arrive, leave in zip(there, back):
        arrive.wait()
        leave.start()
    for copy in back:
        copy.wait()


def body(queries, keys, values, score_gain, grad, segment_ids):
    seq_size = lax.axis_size("seq")
    dp_size = lax.axis_size("dp")
    tokens = queries.shape[1]
    factor = 1.0 / (dp_size * tokens * seq_size)
    hbm = pl.BlockSpec(memory_space=pltpu.HBM)
    heads = KEY_VALUE_HEADS
    pair = pltpu.SemaphoreType.DMA((2,))
    four = pltpu.SemaphoreType.DMA((2, 2))
    wide = GROUP * HEAD_SIZE
    dq, dk, dv, gain = pl.pallas_call(
        functools.partial(kernel, seq_size, dp_size, factor),
        out_shape=(
            jax.ShapeDtypeStruct((BLOCK, QUERY_HEADS * HEAD_SIZE), BF16),
            jax.ShapeDtypeStruct((BLOCK, heads * HEAD_SIZE), BF16),
            jax.ShapeDtypeStruct((BLOCK, heads * HEAD_SIZE), BF16),
            jax.ShapeDtypeStruct((2,), F32),
        ),
        in_specs=[hbm] * 6,
        out_specs=(hbm, hbm, hbm, pl.BlockSpec(memory_space=pltpu.SMEM)),
        scratch_shapes=[
            pltpu.VMEM((2, 2, 2 * BLOCK, wide), BF16),
            pltpu.VMEM((2, 2, 4 * BLOCK, HEAD_SIZE), BF16),
            pltpu.VMEM((2, 2, 2, BLOCK, HEAD_SIZE), BF16),
            pltpu.VMEM((heads, 2, BLOCK, HEAD_SIZE), BF16),
            pltpu.VMEM((2, 2, BLOCK, HEAD_SIZE), BF16),
            pltpu.VMEM((2, 2, BLOCK, HEAD_SIZE), BF16),
            pltpu.VMEM((2, 2, 4 * BLOCK, HEAD_SIZE), F32),
            pltpu.VMEM((2, 2, BLOCK, wide), BF16),
            pltpu.VMEM((heads, 2, BLOCK, HEAD_SIZE), BF16),
            pltpu.VMEM((4 * BLOCK, BLOCK), F32),
            pltpu.VMEM((2 * PARTS, WINDOW, BLOCK), F32),
            pltpu.VMEM((2 * PARTS, WINDOW, LANES), F32),
            pltpu.VMEM((2 * PARTS, WINDOW, LANES), F32),
            pltpu.VMEM((2 * PARTS, WINDOW, LANES), F32),
            pltpu.VMEM((4, PARTS, WINDOW, LANES), BF16),
            pltpu.VMEM((4, PARTS, WINDOW, LANES), BF16),
            pltpu.VMEM((1, tokens * seq_size), jnp.int32),
            pltpu.SMEM((QUERY_HEADS,), F32),
            pltpu.VMEM((seq_size // 2, SIDE), F32),
            pltpu.VMEM((seq_size, seq_size // 2, SIDE), F32),
            pltpu.VMEM((1, 1, SIDE), F32),
            pltpu.VMEM((dp_size - 1, 1, SIDE), F32),
            pltpu.VMEM((2, 1, SIDE), F32),
            pair, pair, four, four, four, four, pair, pair,
            pair,
            pltpu.SemaphoreType.DMA((heads,)),
            pair, pair, pair, pair, pair,
            pltpu.SemaphoreType.DMA((heads, 2)),
            pair,
            pltpu.SemaphoreType.DMA((seq_size,)),
            pair, pair, pair,
            pltpu.SemaphoreType.REGULAR,
        ],
        compiler_params=pltpu.CompilerParams(
            collective_id=0, has_side_effects=True, vmem_limit_bytes=VMEM_BYTES
        ),
        cost_estimate=pl.CostEstimate(
            flops=2 * 5 * BLOCK * WINDOW * HEAD_SIZE * QUERY_HEADS,
            bytes_accessed=4 * 1024 * 1024,
            transcendentals=BLOCK * WINDOW * QUERY_HEADS,
        ),
    )(queries[0], keys[0], values[0], score_gain, grad[0], segment_ids)
    results = (dq, dk, dv, gain)
    dq, dk, dv, gain = pl.pallas_call(
        hand_over,
        out_shape=tuple(jax.ShapeDtypeStruct(x.shape, x.dtype) for x in results),
        in_specs=[hbm] * 4,
        out_specs=(hbm,) * 4,
        scratch_shapes=[
            *[pltpu.VMEM(x.shape, x.dtype) for x in results[:3]],
            pltpu.SMEM(gain.shape, gain.dtype),
            pltpu.SemaphoreType.DMA((2, HAND_PARTS + 3)),
        ],
        compiler_params=pltpu.CompilerParams(vmem_limit_bytes=VMEM_BYTES),
    )(*results)
    return dq[None], dk[None], dv[None], gain


def solution(mesh):
    return jax.shard_map(
        body,
        mesh=mesh,
        in_specs=(
            P("dp", "seq", None),
            P("dp", "seq", None),
            P("dp", "seq", None),
            P(),
            P("dp", "seq", None),
            P("dp", None),
        ),
        out_specs=(P("dp", "seq", None), P("dp", "seq", None), P("dp", "seq", None), P("seq")),
        check_vma=False,
    )
```

```python
import functools
import math

import jax
import jax.numpy as jnp
from jax import lax
from jax.experimental import pallas as pl
from jax.experimental.pallas import tpu as pltpu
from jax.sharding import PartitionSpec as P

QUERY_HEADS = 32
KEY_VALUE_HEADS = 4
HEAD_SIZE = 128
GROUP = QUERY_HEADS // KEY_VALUE_HEADS
BLOCK = 128
PART = 32
PARTS = BLOCK // PART
WINDOW = 288
LANES = GROUP * PART
SIDE = 128
CHUNK = 32
HAND_PARTS = 4
LEADER = 7
VMEM_BYTES = 64 * 1024 * 1024
LOG2E = math.log2(math.e)
SCALE = HEAD_SIZE ** -0.5
BF16 = jnp.bfloat16
F32 = jnp.float32
NT = (((1,), (1,)), ((), ()))
TN = (((0,), (0,)), ((), ()))


def fold_rows(x):
    return jnp.sum(x.reshape(x.shape[0] // 8, 8, x.shape[1]), axis=0)


def kernel(
    seq_size, dp_size, factor,
    q_hbm, k_hbm, v_hbm, gain_hbm, g_hbm, seg_hbm,
    dq_hbm, dk_hbm, dv_hbm, gain_out,
    qg, kv, ret_send, ret, mate_send, mate_in, acc, dq_buf, dkv_buf, seg_rows, bias,
    s_buf, dp_buf, y_buf, p_buf, ds_buf, seg_ref, gain_ref,
    g_part, g_in1, g_sum, g_in2, g_total,
    in_sem, own_sem, halo_send, halo_recv, mate_kv_send, mate_kv_recv, mate_qg_send, mate_qg_recv,
    back_send, back_recv, mate_back_send, mate_back_recv, dq_sem, mate_dq_send, mate_dq_recv,
    dkv_sem, gain1_send, gain1_recv, gain2_sem, gain3_sem, small_sem, ready,
):
    me = lax.axis_index("seq")
    row = lax.axis_index("dp")
    chips = seq_size // 2
    chip = lax.div(me, 2)
    core = me - 2 * chip
    other = 1 - core
    mate = 2 * chip + other
    next_chip = lax.rem(chip + 1, chips)
    last_chip = lax.rem(chip + chips - 1, chips)

    def thin(head):
        return pl.ds(pl.multiple_of(head * HEAD_SIZE, HEAD_SIZE), HEAD_SIZE)

    def wide(head):
        return pl.ds(pl.multiple_of(head * (GROUP * HEAD_SIZE), GROUP * HEAD_SIZE), GROUP * HEAD_SIZE)

    def block(index):
        return pl.ds(pl.multiple_of(index * BLOCK, BLOCK), BLOCK)

    def remote(source, target, send, recv, device):
        return pltpu.make_async_remote_copy(
            src_ref=source,
            dst_ref=target,
            send_sem=send,
            recv_sem=recv,
            device_id={"seq": device},
            device_id_type=pl.DeviceIdType.MESH,
        )

    barrier = pltpu.get_barrier_semaphore()

    def greet_seq(i, carry):
        there = lax.rem(me - i + seq_size, seq_size)

        @pl.when(there != LEADER)
        def _():
            pl.semaphore_signal(
                barrier, inc=1, device_id={"seq": there}, device_id_type=pl.DeviceIdType.MESH
            )

        return carry

    def greet_dp(i, carry):
        pl.semaphore_signal(
            barrier, inc=1, device_id={"dp": lax.rem(row + i, dp_size)}, device_id_type=pl.DeviceIdType.MESH
        )
        return carry

    lax.fori_loop(1, seq_size, greet_seq, 0)

    @pl.when(me == LEADER)
    def _():
        lax.fori_loop(1, dp_size, greet_dp, 0)

    for a in range(2):
        head = 2 * core + a
        pltpu.make_async_copy(k_hbm.at[:, thin(head)], kv.at[a, 0, block(2 + core)], own_sem.at[a]).start()
        pltpu.make_async_copy(v_hbm.at[:, thin(head)], kv.at[a, 1, block(2 + core)], own_sem.at[a]).start()
        pltpu.make_async_copy(q_hbm.at[:, wide(head)], qg.at[a, 0, pl.ds(0, BLOCK)], in_sem.at[a]).start()
        pltpu.make_async_copy(g_hbm.at[:, wide(head)], qg.at[a, 1, pl.ds(0, BLOCK)], in_sem.at[a]).start()
    seg_copy = pltpu.make_async_copy(seg_hbm, seg_ref, small_sem.at[0])
    gain_copy = pltpu.make_async_copy(gain_hbm, gain_ref, small_sem.at[1])
    seg_copy.start()
    gain_copy.start()

    @pl.when(me != LEADER)
    def _():
        pl.semaphore_wait(barrier, seq_size - 1)
        pl.semaphore_signal(
            ready, inc=1, device_id={"seq": LEADER}, device_id_type=pl.DeviceIdType.MESH
        )

    @pl.when(me == LEADER)
    def _():
        pl.semaphore_wait(ready, seq_size - 1)

    def halo_start(a):
        for which, source in enumerate((k_hbm, v_hbm)):
            for to_core in range(2):
                remote(
                    source.at[:, thin(2 * to_core + a)],
                    kv.at[a, which, block(core)],
                    halo_send.at[a, which],
                    halo_recv.at[a, which],
                    2 * next_chip + to_core,
                ).start()

    def halo_whole(a, which):
        part = kv.at[a, which, pl.ds(0, 2 * BLOCK)]
        return remote(part, part, halo_send.at[a, which], halo_recv.at[a, which], 2 * next_chip)

    def mate_start(a):
        head = 2 * other + a
        for which, source in enumerate((k_hbm, v_hbm)):
            remote(
                source.at[:, thin(head)], kv.at[a, which, block(2 + core)],
                mate_kv_send.at[a, which], mate_kv_recv.at[a, which], mate,
            ).start()

    def mate_queries_start(a):
        head = 2 * other + a
        for which, source in enumerate((q_hbm, g_hbm)):
            remote(
                source.at[:, wide(head)], qg.at[a, which, pl.ds(BLOCK, BLOCK)],
                mate_qg_send.at[a], mate_qg_recv.at[a], mate,
            ).start()

    def mate_kv(a, which):
        part = kv.at[a, which, block(2 + other)]
        return remote(part, part, mate_kv_send.at[a, which], mate_kv_recv.at[a, which], mate)

    def mate_qg(a):
        part = qg.at[a, :, pl.ds(BLOCK, BLOCK)]
        return remote(part, part, mate_qg_send.at[a], mate_qg_recv.at[a], mate)

    halo_start(0)
    mate_start(0)
    mate_queries_start(0)
    halo_start(1)
    mate_start(1)
    acc[...] = jnp.zeros(acc.shape, F32)
    seg_copy.wait()
    gain_copy.wait()

    def ids_of(index):
        place = pl.multiple_of(lax.rem(2 * chip + index + seq_size, seq_size) * BLOCK, BLOCK)
        return seg_ref[:, pl.ds(place, BLOCK)].astype(F32)

    for b in range(4):
        seg_rows[pl.ds(b * BLOCK, BLOCK)] = jnp.transpose(
            jnp.broadcast_to(ids_of(b - 2), (BLOCK, BLOCK))
        )
    def block_of(late):
        return other if late else core

    group8 = lax.broadcasted_iota(jnp.int32, (8, BLOCK), 1) // PART
    key_place = lax.broadcasted_iota(jnp.int32, (WINDOW, BLOCK), 0)
    lane = lax.broadcasted_iota(jnp.int32, (WINDOW, BLOCK), 1)
    causal = key_place <= 2 * BLOCK + lane % PART
    for late in range(2):
        x = block_of(late)
        query_ids = jnp.broadcast_to(ids_of(x), (8, BLOCK))
        rolled = [query_ids] + [pltpu.roll(query_ids, PART * k, 1) for k in range(1, PARTS)]
        for part in range(PARTS):
            start = x * BLOCK + part * PART
            ids = rolled[-part % PARTS]
            for j in range(1, PARTS):
                ids = jnp.where(group8 == j, rolled[(j - part) % PARTS], ids)
            inside = (chip - 1) * (2 * BLOCK) + start + key_place >= 0
            keys_ids = seg_rows[pl.ds(pl.multiple_of(start, PART), WINDOW)]
            allowed = (keys_ids == ids[0:1]) & causal & inside
            bias[late * PARTS + part] = jnp.where(allowed, 0.0, -1e30)

    lane_wide = lax.broadcasted_iota(jnp.int32, (1, LANES), 1)

    def back_copy(a, place):
        return remote(
            ret_send.at[a, place], ret.at[2 * core + a],
            back_send.at[a], back_recv.at[2 * core + a], 2 * last_chip + place,
        )

    def back_whole(a):
        return remote(ret_send.at[a], ret_send.at[a], back_send.at[a], back_recv.at[a], 2 * last_chip)

    def back_from(head):
        return remote(ret.at[head], ret.at[head], back_send.at[0], back_recv.at[head], 2 * last_chip)

    def mate_back(a):
        return remote(
            mate_send.at[a], mate_in.at[a], mate_back_send.at[a], mate_back_recv.at[a], mate
        )

    def dkv_out(head, which):
        target = (dk_hbm, dv_hbm)[which]
        return pltpu.make_async_copy(
            dkv_buf.at[head, which], target.at[:, thin(head)], dkv_sem.at[head, which]
        )

    def finish(a):
        mine = 2 * core + a
        theirs = 2 * other + a
        back_from(mine).wait_recv()
        for which in range(2):
            total = acc[a, which, block(2 + core)] + ret[mine, which].astype(F32)
            dkv_buf[mine, which] = total.astype(BF16)
            dkv_out(mine, which).start()
        mate_back(a).wait_recv()
        back_from(theirs).wait_recv()
        for which in range(2):
            total = mate_in[a, which].astype(F32) + ret[theirs, which].astype(F32)
            dkv_buf[theirs, which] = total.astype(BF16)
            dkv_out(theirs, which).start()

    def dq_own(a):
        return pltpu.make_async_copy(dq_buf.at[a, 0], dq_hbm.at[:, wide(2 * core + a)], dq_sem.at[a])

    def dq_mate(a):
        return remote(
            dq_buf.at[a, 1], dq_hbm.at[:, wide(2 * core + a)], mate_dq_send.at[a], mate_dq_recv.at[a], mate
        )

    def dq_from(a):
        part = dq_hbm.at[:, wide(2 * other + a)]
        return remote(part, part, mate_dq_send.at[a], mate_dq_recv.at[a], mate)

    def gain_copy1(source):
        return remote(g_part, g_in1.at[source], gain1_send.at[0], gain1_recv.at[source], LEADER)

    def gain_copy3(target):
        return remote(g_total.at[0], g_total.at[1], gain3_sem.at[0], gain3_sem.at[1], target)

    def key_rows(late, part):
        return pl.ds(pl.multiple_of(block_of(late) * BLOCK + part * PART, PART), WINDOW)

    def stack(a, late, which, part):
        rows = pl.ds(late * BLOCK + part * PART, PART)
        return jnp.concatenate(
            [qg[a, which, rows, pl.ds(h * HEAD_SIZE, HEAD_SIZE)] for h in range(GROUP)], axis=0
        )

    def scores(late, a):
        gain = jnp.full((1, LANES), gain_ref[(2 * core + a) * GROUP], F32)
        for h in range(1, GROUP):
            gain = jnp.where(lane_wide >= h * PART, gain_ref[(2 * core + a) * GROUP + h], gain)
        to_score = gain * (SCALE * LOG2E)
        to_grad = gain * SCALE

        def product(target, which, u):
            target[u] = lax.dot_general(
                kv[a, which, key_rows(late, u)], stack(a, late, which, u), NT,
                preferred_element_type=F32,
            )

        def middle(u):
            chunks = [pl.ds(i, CHUNK) for i in range(0, WINDOW, CHUNK)]
            top = jnp.full((8, LANES), -3e38, F32)
            for rows in chunks:
                shade = bias[late * PARTS + u, rows]
                y = s_buf[u, rows] * to_score + jnp.concatenate([shade, shade], axis=1)
                y_buf[u, rows] = y
                top = jnp.maximum(top, jnp.max(y.reshape(CHUNK // 8, 8, LANES), axis=0))
            top = jnp.max(top, axis=0, keepdims=True)
            total = jnp.zeros((8, LANES), F32)
            dot = jnp.zeros((8, LANES), F32)
            for rows in chunks:
                e = jnp.exp2(y_buf[u, rows] - top)
                y_buf[u, rows] = e
                total = total + fold_rows(e)
                dot = dot + fold_rows(e * dp_buf[u, rows])
            inverse = 1.0 / jnp.sum(total, axis=0, keepdims=True)
            delta = jnp.sum(dot, axis=0, keepdims=True) * inverse
            spread = jnp.zeros((8, LANES), F32)
            for rows in chunks:
                p = y_buf[u, rows] * inverse
                dscore = p * (dp_buf[u, rows] - delta)
                spread = spread + fold_rows(dscore * s_buf[u, rows])
                p_buf[2 * a + late, u, rows] = p.astype(BF16)
                ds_buf[2 * a + late, u, rows] = (dscore * to_grad).astype(BF16)
            return jnp.sum(spread, axis=0, keepdims=True) * (SCALE * factor)

        if late:
            mate_qg(a).wait_recv()
        else:
            own = kv.at[a, :, block(2 + core)]
            pltpu.make_async_copy(own, own, own_sem.at[a]).wait()
            held = qg.at[a, :, pl.ds(0, BLOCK)]
            pltpu.make_async_copy(held, held, in_sem.at[a]).wait()
            mate_kv(a, 0).wait_recv()
            halo_whole(a, 0).wait_recv()
        for u in range(PARTS):
            product(s_buf, 0, u)
        if not late:
            mate_kv(a, 1).wait_recv()
            halo_whole(a, 1).wait_recv()
        product(dp_buf, 1, 0)
        terms = jnp.zeros((1, LANES), F32)
        for u in range(PARTS):
            if u + 1 < PARTS:
                product(dp_buf, 1, u + 1)
            terms = terms + middle(u)
        for side in range(2):
            g_part[pl.ds(2 * a + side, 1), :] += terms[:, side * SIDE:(side + 1) * SIDE]

    def own_scores(a, carry):
        scores(0, a)

        @pl.when(a == 0)
        def _():
            mate_queries_start(1)

        return carry

    def mate_scores(a, carry):
        scores(1, a)
        return carry

    g_part[...] = jnp.zeros(g_part.shape, F32)
    lax.fori_loop(0, 2, own_scores, 0)
    lax.fori_loop(0, 2, mate_scores, 0)

    @pl.when(me != LEADER)
    def _():
        gain_copy1(me).start()

    def gain_arrive(i, carry):
        @pl.when(i != LEADER)
        def _():
            gain_copy1(i).wait_recv()

        return carry

    def gain_send2(i, carry):
        pltpu.make_async_remote_copy(
            src_ref=g_sum.at[0],
            dst_ref=g_in2.at[i - 1],
            send_sem=gain2_sem.at[0],
            recv_sem=gain2_sem.at[1],
            device_id={"dp": lax.rem(row + i, dp_size)},
            device_id_type=pl.DeviceIdType.MESH,
        ).start()
        return carry

    @pl.when(me == LEADER)
    def _():
        g_in1[LEADER] = g_part[...]
        lax.fori_loop(0, seq_size, gain_arrive, 0)
        row_of = lax.broadcasted_iota(jnp.int32, (chips, SIDE), 0)
        lanes = lax.broadcasted_iota(jnp.int32, (chips, SIDE), 1)
        sums = jnp.zeros((chips, SIDE), F32)
        for side in range(2):
            held = g_in1[side]
            for i in range(1, chips):
                held = held + g_in1[2 * i + side]
            for h in range(PARTS):
                head_sum = jnp.sum(jnp.where(lanes // PART == h, held, 0.0), axis=1, keepdims=True)
                place = (QUERY_HEADS // 2) * side + PARTS * row_of + h
                sums = sums + jnp.where((lanes == place) & (row_of < PARTS), head_sum, 0.0)
        g_sum[0] = jnp.sum(sums, axis=0, keepdims=True)
        pl.semaphore_wait(barrier, dp_size - 1)
        lax.fori_loop(1, dp_size, gain_send2, 0)

    def key_side(a, carry):
        for late in range(2):
            for part in range(PARTS):
                rows = key_rows(late, part)
                acc[a, 0, rows] += jnp.dot(
                    ds_buf[2 * a + late, part], stack(a, late, 0, part), preferred_element_type=F32
                )
                acc[a, 1, rows] += jnp.dot(
                    p_buf[2 * a + late, part], stack(a, late, 1, part), preferred_element_type=F32
                )
        for place in range(2):
            for which in range(2):
                ret_send[a, place, which] = acc[a, which, pl.ds(place * BLOCK, BLOCK)].astype(BF16)
            back_copy(a, place).start()
        for which in range(2):
            mate_send[a, which] = acc[a, which, block(2 + other)].astype(BF16)
        mate_back(a).start()
        return carry

    lax.fori_loop(0, 2, key_side, 0)

    def query_side(a, carry):
        for late in (1, 0):
            for part in range(PARTS):
                turned_keys = jnp.transpose(kv[a, 0, key_rows(late, part)])
                dq = jnp.dot(turned_keys, ds_buf[2 * a + late, part], preferred_element_type=F32)
                dq = jnp.transpose(dq.astype(BF16))
                for h in range(GROUP):
                    dq_buf[
                        a, late, pl.ds(part * PART, PART), pl.ds(h * HEAD_SIZE, HEAD_SIZE)
                    ] = dq[h * PART:(h + 1) * PART]
            if late:
                dq_mate(a).start()
            else:
                dq_own(a).start()
        return carry

    lax.fori_loop(0, 2, query_side, 0)
    finish(0)
    finish(1)
    gain2_whole = remote(g_in2, g_in2, gain2_sem.at[0], gain2_sem.at[1], mate)

    def gain_send3(i, carry):
        gain_copy3(lax.rem(me + i, seq_size)).start()
        return carry

    @pl.when(me == LEADER)
    def _():
        gain2_whole.wait_recv()
        g_total[0] = g_sum[0] + jnp.sum(g_in2[...], axis=0)
        lax.fori_loop(1, seq_size, gain_send3, 0)
        g_total[1] = g_total[0]

    @pl.when(me != LEADER)
    def _():
        gain_copy3(mate).wait_recv()

    lane1 = lax.broadcasted_iota(jnp.int32, (1, SIDE), 1)
    for side in range(2):
        gain_out[side] = jnp.sum(jnp.where(lane1 == 2 * me + side, g_total[1], 0.0))

    @pl.when(me == LEADER)
    def _():
        gain2_whole.wait_send()
        sent = g_in2.at[pl.ds(0, seq_size - 1)]
        remote(sent, sent, gain3_sem.at[0], gain3_sem.at[1], mate).wait_send()

    @pl.when(me != LEADER)
    def _():
        gain_copy1(me).wait_send()

    for a in range(2):
        for which in range(2):
            halo_whole(a, which).wait_send()
            mate_kv(a, which).wait_send()
        mate_qg(a).wait_send()
        back_whole(a).wait_send()
        mate_back(a).wait_send()
        dq_own(a).wait()
        dq_mate(a).wait_send()
        dq_from(a).wait_recv()
    for head in range(KEY_VALUE_HEADS):
        for which in range(2):
            dkv_out(head, which).wait()


def hand_over(dq_in, dk_in, dv_in, gain_in, dq_out, dk_out, dv_out, gain_to, dq_buf, dk_buf, dv_buf, gain_buf, sems):
    trips = [
        (dk_in, dk_buf, dk_out),
        (dv_in, dv_buf, dv_out),
        (gain_in, gain_buf, gain_to),
    ]
    for i in range(HAND_PARTS):
        rows = pl.ds(i * (BLOCK // HAND_PARTS), BLOCK // HAND_PARTS)
        trips.append((dq_in.at[rows], dq_buf.at[rows], dq_out.at[rows]))
    there = [pltpu.make_async_copy(x, y, sems.at[0, i]) for i, (x, y, _) in enumerate(trips)]
    back = [pltpu.make_async_copy(y, z, sems.at[1, i]) for i, (_, y, z) in enumerate(trips)]
    for copy in there:
        copy.start()
    for arrive, leave in zip(there, back):
        arrive.wait()
        leave.start()
    for copy in back:
        copy.wait()


def body(queries, keys, values, score_gain, grad, segment_ids):
    seq_size = lax.axis_size("seq")
    dp_size = lax.axis_size("dp")
    tokens = queries.shape[1]
    factor = 1.0 / (dp_size * tokens * seq_size)
    hbm = pl.BlockSpec(memory_space=pltpu.HBM)
    heads = KEY_VALUE_HEADS
    pair = pltpu.SemaphoreType.DMA((2,))
    four = pltpu.SemaphoreType.DMA((2, 2))
    wide = GROUP * HEAD_SIZE
    dq, dk, dv, gain = pl.pallas_call(
        functools.partial(kernel, seq_size, dp_size, factor),
        out_shape=(
            jax.ShapeDtypeStruct((BLOCK, QUERY_HEADS * HEAD_SIZE), BF16),
            jax.ShapeDtypeStruct((BLOCK, heads * HEAD_SIZE), BF16),
            jax.ShapeDtypeStruct((BLOCK, heads * HEAD_SIZE), BF16),
            jax.ShapeDtypeStruct((2,), F32),
        ),
        in_specs=[hbm] * 6,
        out_specs=(hbm, hbm, hbm, pl.BlockSpec(memory_space=pltpu.SMEM)),
        scratch_shapes=[
            pltpu.VMEM((2, 2, 2 * BLOCK, wide), BF16),
            pltpu.VMEM((2, 2, 4 * BLOCK, HEAD_SIZE), BF16),
            pltpu.VMEM((2, 2, 2, BLOCK, HEAD_SIZE), BF16),
            pltpu.VMEM((heads, 2, BLOCK, HEAD_SIZE), BF16),
            pltpu.VMEM((2, 2, BLOCK, HEAD_SIZE), BF16),
            pltpu.VMEM((2, 2, BLOCK, HEAD_SIZE), BF16),
            pltpu.VMEM((2, 2, 4 * BLOCK, HEAD_SIZE), F32),
            pltpu.VMEM((2, 2, BLOCK, wide), BF16),
            pltpu.VMEM((heads, 2, BLOCK, HEAD_SIZE), BF16),
            pltpu.VMEM((4 * BLOCK, BLOCK), F32),
            pltpu.VMEM((2 * PARTS, WINDOW, BLOCK), F32),
            pltpu.VMEM((PARTS, WINDOW, LANES), F32),
            pltpu.VMEM((PARTS, WINDOW, LANES), F32),
            pltpu.VMEM((PARTS, WINDOW, LANES), F32),
            pltpu.VMEM((4, PARTS, WINDOW, LANES), BF16),
            pltpu.VMEM((4, PARTS, WINDOW, LANES), BF16),
            pltpu.VMEM((1, tokens * seq_size), jnp.int32),
            pltpu.SMEM((QUERY_HEADS,), F32),
            pltpu.VMEM((seq_size // 2, SIDE), F32),
            pltpu.VMEM((seq_size, seq_size // 2, SIDE), F32),
            pltpu.VMEM((1, 1, SIDE), F32),
            pltpu.VMEM((dp_size - 1, 1, SIDE), F32),
            pltpu.VMEM((2, 1, SIDE), F32),
            pair, pair, four, four, four, four, pair, pair,
            pair,
            pltpu.SemaphoreType.DMA((heads,)),
            pair, pair, pair, pair, pair,
            pltpu.SemaphoreType.DMA((heads, 2)),
            pair,
            pltpu.SemaphoreType.DMA((seq_size,)),
            pair, pair, pair,
            pltpu.SemaphoreType.REGULAR,
        ],
        compiler_params=pltpu.CompilerParams(
            collective_id=0, has_side_effects=True, vmem_limit_bytes=VMEM_BYTES
        ),
        cost_estimate=pl.CostEstimate(
            flops=2 * 5 * BLOCK * WINDOW * HEAD_SIZE * QUERY_HEADS,
            bytes_accessed=4 * 1024 * 1024,
            transcendentals=BLOCK * WINDOW * QUERY_HEADS,
        ),
    )(queries[0], keys[0], values[0], score_gain, grad[0], segment_ids)
    results = (dq, dk, dv, gain)
    dq, dk, dv, gain = pl.pallas_call(
        hand_over,
        out_shape=tuple(jax.ShapeDtypeStruct(x.shape, x.dtype) for x in results),
        in_specs=[hbm] * 4,
        out_specs=(hbm,) * 4,
        scratch_shapes=[
            *[pltpu.VMEM(x.shape, x.dtype) for x in results[:3]],
            pltpu.SMEM(gain.shape, gain.dtype),
            pltpu.SemaphoreType.DMA((2, HAND_PARTS + 3)),
        ],
        compiler_params=pltpu.CompilerParams(vmem_limit_bytes=VMEM_BYTES),
    )(*results)
    return dq[None], dk[None], dv[None], gain


def solution(mesh):
    return jax.shard_map(
        body,
        mesh=mesh,
        in_specs=(
            P("dp", "seq", None),
            P("dp", "seq", None),
            P("dp", "seq", None),
            P(),
            P("dp", "seq", None),
            P("dp", None),
        ),
        out_specs=(P("dp", "seq", None), P("dp", "seq", None), P("dp", "seq", None), P("seq")),
        check_vma=False,
    )
```

```python
import functools
import math

import jax
import jax.numpy as jnp
from jax import lax
from jax.experimental import pallas as pl
from jax.experimental.pallas import tpu as pltpu
from jax.sharding import PartitionSpec as P

QUERY_HEADS = 32
KEY_VALUE_HEADS = 4
HEAD_SIZE = 128
GROUP = QUERY_HEADS // KEY_VALUE_HEADS
BLOCK = 128
PART = 32
PARTS = BLOCK // PART
WINDOW = 288
LANES = GROUP * PART
SIDE = 128
CHUNK = 32
HAND_PARTS = 8
LEADER = 7
VMEM_BYTES = 64 * 1024 * 1024
LOG2E = math.log2(math.e)
SCALE = HEAD_SIZE ** -0.5
BF16 = jnp.bfloat16
F32 = jnp.float32
NT = (((1,), (1,)), ((), ()))
TN = (((0,), (0,)), ((), ()))


def fold_rows(x):
    return jnp.sum(x.reshape(x.shape[0] // 8, 8, x.shape[1]), axis=0)


def kernel(
    seq_size, dp_size, factor,
    q_hbm, k_hbm, v_hbm, gain_hbm, g_hbm, seg_hbm,
    dq_hbm, dk_hbm, dv_hbm, gain_out,
    qg, kv, ret_send, ret, mate_send, mate_in, acc, dq_buf, dkv_buf, seg_rows, bias,
    s_buf, dp_buf, y_buf, p_buf, ds_buf, seg_ref, gain_ref,
    g_part, g_in1, g_sum, g_in2, g_total,
    in_sem, own_sem, halo_send, halo_recv, mate_kv_send, mate_kv_recv, mate_qg_send, mate_qg_recv,
    back_send, back_recv, mate_back_send, mate_back_recv, dq_sem, mate_dq_send, mate_dq_recv,
    dkv_sem, gain1_send, gain1_recv, gain2_sem, gain3_sem, small_sem, ready,
):
    me = lax.axis_index("seq")
    row = lax.axis_index("dp")
    chips = seq_size // 2
    chip = lax.div(me, 2)
    core = me - 2 * chip
    other = 1 - core
    mate = 2 * chip + other
    next_chip = lax.rem(chip + 1, chips)
    last_chip = lax.rem(chip + chips - 1, chips)

    def thin(head):
        return pl.ds(pl.multiple_of(head * HEAD_SIZE, HEAD_SIZE), HEAD_SIZE)

    def wide(head):
        return pl.ds(pl.multiple_of(head * (GROUP * HEAD_SIZE), GROUP * HEAD_SIZE), GROUP * HEAD_SIZE)

    def block(index):
        return pl.ds(pl.multiple_of(index * BLOCK, BLOCK), BLOCK)

    def remote(source, target, send, recv, device):
        return pltpu.make_async_remote_copy(
            src_ref=source,
            dst_ref=target,
            send_sem=send,
            recv_sem=recv,
            device_id={"seq": device},
            device_id_type=pl.DeviceIdType.MESH,
        )

    barrier = pltpu.get_barrier_semaphore()

    def greet_seq(i, carry):
        there = lax.rem(me - i + seq_size, seq_size)

        @pl.when(there != LEADER)
        def _():
            pl.semaphore_signal(
                barrier, inc=1, device_id={"seq": there}, device_id_type=pl.DeviceIdType.MESH
            )

        return carry

    def greet_dp(i, carry):
        pl.semaphore_signal(
            barrier, inc=1, device_id={"dp": lax.rem(row + i, dp_size)}, device_id_type=pl.DeviceIdType.MESH
        )
        return carry

    lax.fori_loop(1, seq_size, greet_seq, 0)

    @pl.when(me == LEADER)
    def _():
        lax.fori_loop(1, dp_size, greet_dp, 0)

    for a in range(2):
        head = 2 * core + a
        pltpu.make_async_copy(k_hbm.at[:, thin(head)], kv.at[a, 0, block(2 + core)], own_sem.at[a]).start()
        pltpu.make_async_copy(v_hbm.at[:, thin(head)], kv.at[a, 1, block(2 + core)], own_sem.at[a]).start()
        pltpu.make_async_copy(q_hbm.at[:, wide(head)], qg.at[a, 0, pl.ds(0, BLOCK)], in_sem.at[a]).start()
        pltpu.make_async_copy(g_hbm.at[:, wide(head)], qg.at[a, 1, pl.ds(0, BLOCK)], in_sem.at[a]).start()
    seg_copy = pltpu.make_async_copy(seg_hbm, seg_ref, small_sem.at[0])
    gain_copy = pltpu.make_async_copy(gain_hbm, gain_ref, small_sem.at[1])
    seg_copy.start()
    gain_copy.start()

    @pl.when(me != LEADER)
    def _():
        pl.semaphore_wait(barrier, seq_size - 1)
        pl.semaphore_signal(
            ready, inc=1, device_id={"seq": LEADER}, device_id_type=pl.DeviceIdType.MESH
        )

    @pl.when(me == LEADER)
    def _():
        pl.semaphore_wait(ready, seq_size - 1)

    def halo_start(a):
        for which, source in enumerate((k_hbm, v_hbm)):
            for to_core in range(2):
                remote(
                    source.at[:, thin(2 * to_core + a)],
                    kv.at[a, which, block(core)],
                    halo_send.at[a, which],
                    halo_recv.at[a, which],
                    2 * next_chip + to_core,
                ).start()

    def halo_whole(a, which):
        part = kv.at[a, which, pl.ds(0, 2 * BLOCK)]
        return remote(part, part, halo_send.at[a, which], halo_recv.at[a, which], 2 * next_chip)

    def mate_start(a):
        head = 2 * other + a
        for which, source in enumerate((k_hbm, v_hbm)):
            remote(
                source.at[:, thin(head)], kv.at[a, which, block(2 + core)],
                mate_kv_send.at[a, which], mate_kv_recv.at[a, which], mate,
            ).start()

    def mate_queries_start(a):
        head = 2 * other + a
        for which, source in enumerate((q_hbm, g_hbm)):
            remote(
                source.at[:, wide(head)], qg.at[a, which, pl.ds(BLOCK, BLOCK)],
                mate_qg_send.at[a], mate_qg_recv.at[a], mate,
            ).start()

    def mate_kv(a, which):
        part = kv.at[a, which, block(2 + other)]
        return remote(part, part, mate_kv_send.at[a, which], mate_kv_recv.at[a, which], mate)

    def mate_qg(a):
        part = qg.at[a, :, pl.ds(BLOCK, BLOCK)]
        return remote(part, part, mate_qg_send.at[a], mate_qg_recv.at[a], mate)

    halo_start(0)
    mate_start(0)
    mate_queries_start(0)
    halo_start(1)
    mate_start(1)
    acc[...] = jnp.zeros(acc.shape, F32)
    seg_copy.wait()
    gain_copy.wait()

    def ids_of(index):
        place = pl.multiple_of(lax.rem(2 * chip + index + seq_size, seq_size) * BLOCK, BLOCK)
        return seg_ref[:, pl.ds(place, BLOCK)].astype(F32)

    for b in range(4):
        seg_rows[pl.ds(b * BLOCK, BLOCK)] = jnp.transpose(
            jnp.broadcast_to(ids_of(b - 2), (BLOCK, BLOCK))
        )
    def block_of(late):
        return other if late else core

    group8 = lax.broadcasted_iota(jnp.int32, (8, BLOCK), 1) // PART
    key_place = lax.broadcasted_iota(jnp.int32, (WINDOW, BLOCK), 0)
    lane = lax.broadcasted_iota(jnp.int32, (WINDOW, BLOCK), 1)
    causal = key_place <= 2 * BLOCK + lane % PART
    for late in range(2):
        x = block_of(late)
        query_ids = jnp.broadcast_to(ids_of(x), (8, BLOCK))
        rolled = [query_ids] + [pltpu.roll(query_ids, PART * k, 1) for k in range(1, PARTS)]
        for part in range(PARTS):
            start = x * BLOCK + part * PART
            ids = rolled[-part % PARTS]
            for j in range(1, PARTS):
                ids = jnp.where(group8 == j, rolled[(j - part) % PARTS], ids)
            inside = (chip - 1) * (2 * BLOCK) + start + key_place >= 0
            keys_ids = seg_rows[pl.ds(pl.multiple_of(start, PART), WINDOW)]
            allowed = (keys_ids == ids[0:1]) & causal & inside
            bias[late * PARTS + part] = jnp.where(allowed, 0.0, -1e30)

    lane_wide = lax.broadcasted_iota(jnp.int32, (1, LANES), 1)

    def back_copy(a, place):
        return remote(
            ret_send.at[a, place], ret.at[2 * core + a],
            back_send.at[a], back_recv.at[2 * core + a], 2 * last_chip + place,
        )

    def back_whole(a):
        return remote(ret_send.at[a], ret_send.at[a], back_send.at[a], back_recv.at[a], 2 * last_chip)

    def back_from(head):
        return remote(ret.at[head], ret.at[head], back_send.at[0], back_recv.at[head], 2 * last_chip)

    def mate_back(a):
        return remote(
            mate_send.at[a], mate_in.at[a], mate_back_send.at[a], mate_back_recv.at[a], mate
        )

    def dkv_out(head, which):
        target = (dk_hbm, dv_hbm)[which]
        return pltpu.make_async_copy(
            dkv_buf.at[head, which], target.at[:, thin(head)], dkv_sem.at[head, which]
        )

    def finish(a):
        mine = 2 * core + a
        theirs = 2 * other + a
        back_from(mine).wait_recv()
        for which in range(2):
            total = acc[a, which, block(2 + core)] + ret[mine, which].astype(F32)
            dkv_buf[mine, which] = total.astype(BF16)
            dkv_out(mine, which).start()
        mate_back(a).wait_recv()
        back_from(theirs).wait_recv()
        for which in range(2):
            total = mate_in[a, which].astype(F32) + ret[theirs, which].astype(F32)
            dkv_buf[theirs, which] = total.astype(BF16)
            dkv_out(theirs, which).start()

    def dq_own(a):
        return pltpu.make_async_copy(dq_buf.at[a, 0], dq_hbm.at[:, wide(2 * core + a)], dq_sem.at[a])

    def dq_mate(a):
        return remote(
            dq_buf.at[a, 1], dq_hbm.at[:, wide(2 * core + a)], mate_dq_send.at[a], mate_dq_recv.at[a], mate
        )

    def dq_from(a):
        part = dq_hbm.at[:, wide(2 * other + a)]
        return remote(part, part, mate_dq_send.at[a], mate_dq_recv.at[a], mate)

    def gain_copy1(source):
        return remote(g_part, g_in1.at[source], gain1_send.at[0], gain1_recv.at[source], LEADER)

    def gain_copy3(target):
        return remote(g_total.at[0], g_total.at[1], gain3_sem.at[0], gain3_sem.at[1], target)

    def key_rows(late, part):
        return pl.ds(pl.multiple_of(block_of(late) * BLOCK + part * PART, PART), WINDOW)

    def stack(a, late, which, part):
        rows = pl.ds(late * BLOCK + part * PART, PART)
        return jnp.concatenate(
            [qg[a, which, rows, pl.ds(h * HEAD_SIZE, HEAD_SIZE)] for h in range(GROUP)], axis=0
        )

    def scores(late, a):
        gain = jnp.full((1, LANES), gain_ref[(2 * core + a) * GROUP], F32)
        for h in range(1, GROUP):
            gain = jnp.where(lane_wide >= h * PART, gain_ref[(2 * core + a) * GROUP + h], gain)
        to_score = gain * (SCALE * LOG2E)
        to_grad = gain * SCALE

        def product(target, which, u):
            target[u] = lax.dot_general(
                kv[a, which, key_rows(late, u)], stack(a, late, which, u), NT,
                preferred_element_type=F32,
            )

        def middle(u):
            chunks = [pl.ds(i, CHUNK) for i in range(0, WINDOW, CHUNK)]
            top = jnp.full((8, LANES), -3e38, F32)
            for rows in chunks:
                shade = bias[late * PARTS + u, rows]
                y = s_buf[u, rows] * to_score + jnp.concatenate([shade, shade], axis=1)
                y_buf[u, rows] = y
                top = jnp.maximum(top, jnp.max(y.reshape(CHUNK // 8, 8, LANES), axis=0))
            top = jnp.max(top, axis=0, keepdims=True)
            total = jnp.zeros((8, LANES), F32)
            dot = jnp.zeros((8, LANES), F32)
            for rows in chunks:
                e = jnp.exp2(y_buf[u, rows] - top)
                y_buf[u, rows] = e
                total = total + fold_rows(e)
                dot = dot + fold_rows(e * dp_buf[u, rows])
            inverse = 1.0 / jnp.sum(total, axis=0, keepdims=True)
            delta = jnp.sum(dot, axis=0, keepdims=True) * inverse
            spread = jnp.zeros((8, LANES), F32)
            for rows in chunks:
                p = y_buf[u, rows] * inverse
                dscore = p * (dp_buf[u, rows] - delta)
                spread = spread + fold_rows(dscore * s_buf[u, rows])
                p_buf[2 * a + late, u, rows] = p.astype(BF16)
                ds_buf[2 * a + late, u, rows] = (dscore * to_grad).astype(BF16)
            return jnp.sum(spread, axis=0, keepdims=True) * (SCALE * factor)

        if late:
            mate_qg(a).wait_recv()
        else:
            own = kv.at[a, :, block(2 + core)]
            pltpu.make_async_copy(own, own, own_sem.at[a]).wait()
            held = qg.at[a, :, pl.ds(0, BLOCK)]
            pltpu.make_async_copy(held, held, in_sem.at[a]).wait()
            mate_kv(a, 0).wait_recv()
            halo_whole(a, 0).wait_recv()
        for u in range(PARTS):
            product(s_buf, 0, u)
        if not late:
            mate_kv(a, 1).wait_recv()
            halo_whole(a, 1).wait_recv()

            @pl.when(a == 0)
            def _():
                mate_queries_start(1)

        product(dp_buf, 1, 0)
        terms = jnp.zeros((1, LANES), F32)
        for u in range(PARTS):
            if u + 1 < PARTS:
                product(dp_buf, 1, u + 1)
            terms = terms + middle(u)
        for side in range(2):
            g_part[pl.ds(2 * a + side, 1), :] += terms[:, side * SIDE:(side + 1) * SIDE]

    def own_scores(a, carry):
        scores(0, a)
        return carry

    def mate_scores(a, carry):
        scores(1, a)
        return carry

    g_part[...] = jnp.zeros(g_part.shape, F32)
    lax.fori_loop(0, 2, own_scores, 0)
    lax.fori_loop(0, 2, mate_scores, 0)

    @pl.when(me != LEADER)
    def _():
        gain_copy1(me).start()

    def gain_arrive(i, carry):
        @pl.when(i != LEADER)
        def _():
            gain_copy1(i).wait_recv()

        return carry

    def gain_send2(target, carry):
        offset = lax.rem(target - row + dp_size, dp_size)

        @pl.when(offset != 0)
        def _():
            pltpu.make_async_remote_copy(
                src_ref=g_sum.at[0],
                dst_ref=g_in2.at[offset - 1],
                send_sem=gain2_sem.at[0],
                recv_sem=gain2_sem.at[1],
                device_id={"dp": target},
                device_id_type=pl.DeviceIdType.MESH,
            ).start()

        return carry

    @pl.when(me == LEADER)
    def _():
        g_in1[LEADER] = g_part[...]
        lax.fori_loop(0, seq_size, gain_arrive, 0)
        row_of = lax.broadcasted_iota(jnp.int32, (chips, SIDE), 0)
        lanes = lax.broadcasted_iota(jnp.int32, (chips, SIDE), 1)
        sums = jnp.zeros((chips, SIDE), F32)
        for side in range(2):
            held = g_in1[side]
            for i in range(1, chips):
                held = held + g_in1[2 * i + side]
            for h in range(PARTS):
                head_sum = jnp.sum(jnp.where(lanes // PART == h, held, 0.0), axis=1, keepdims=True)
                place = (QUERY_HEADS // 2) * side + PARTS * row_of + h
                sums = sums + jnp.where((lanes == place) & (row_of < PARTS), head_sum, 0.0)
        g_sum[0] = jnp.sum(sums, axis=0, keepdims=True)
        pl.semaphore_wait(barrier, dp_size - 1)
        lax.fori_loop(0, dp_size, gain_send2, 0)

    def key_side(a, carry):
        for late in range(2):
            for part in range(PARTS):
                rows = key_rows(late, part)
                acc[a, 0, rows] += jnp.dot(
                    ds_buf[2 * a + late, part], stack(a, late, 0, part), preferred_element_type=F32
                )
                acc[a, 1, rows] += jnp.dot(
                    p_buf[2 * a + late, part], stack(a, late, 1, part), preferred_element_type=F32
                )
        for place in range(2):
            for which in range(2):
                ret_send[a, place, which] = acc[a, which, pl.ds(place * BLOCK, BLOCK)].astype(BF16)
            back_copy(a, place).start()
        for which in range(2):
            mate_send[a, which] = acc[a, which, block(2 + other)].astype(BF16)
        mate_back(a).start()
        return carry

    lax.fori_loop(0, 2, key_side, 0)

    def query_side(a, carry):
        for late in (1, 0):
            for part in range(PARTS):
                turned_keys = jnp.transpose(kv[a, 0, key_rows(late, part)])
                dq = jnp.dot(turned_keys, ds_buf[2 * a + late, part], preferred_element_type=F32)
                dq = jnp.transpose(dq.astype(BF16))
                for h in range(GROUP):
                    dq_buf[
                        a, late, pl.ds(part * PART, PART), pl.ds(h * HEAD_SIZE, HEAD_SIZE)
                    ] = dq[h * PART:(h + 1) * PART]
            if late:
                dq_mate(a).start()
            else:
                dq_own(a).start()
        return carry

    lax.fori_loop(0, 2, query_side, 0)
    finish(0)
    finish(1)
    gain2_whole = remote(g_in2, g_in2, gain2_sem.at[0], gain2_sem.at[1], mate)

    def gain_send3(target, carry):
        @pl.when(target != LEADER)
        def _():
            gain_copy3(target).start()

        return carry

    @pl.when(me == LEADER)
    def _():
        gain2_whole.wait_recv()
        g_total[0] = g_sum[0] + jnp.sum(g_in2[...], axis=0)
        lax.fori_loop(0, seq_size, gain_send3, 0)
        g_total[1] = g_total[0]

    @pl.when(me != LEADER)
    def _():
        gain_copy3(mate).wait_recv()

    lane1 = lax.broadcasted_iota(jnp.int32, (1, SIDE), 1)
    for side in range(2):
        gain_out[side] = jnp.sum(jnp.where(lane1 == 2 * me + side, g_total[1], 0.0))

    @pl.when(me == LEADER)
    def _():
        gain2_whole.wait_send()
        sent = g_in2.at[pl.ds(0, seq_size - 1)]
        remote(sent, sent, gain3_sem.at[0], gain3_sem.at[1], mate).wait_send()

    @pl.when(me != LEADER)
    def _():
        gain_copy1(me).wait_send()

    for a in range(2):
        for which in range(2):
            halo_whole(a, which).wait_send()
            mate_kv(a, which).wait_send()
        mate_qg(a).wait_send()
        back_whole(a).wait_send()
        mate_back(a).wait_send()
        dq_own(a).wait()
        dq_mate(a).wait_send()
        dq_from(a).wait_recv()
    for head in range(KEY_VALUE_HEADS):
        for which in range(2):
            dkv_out(head, which).wait()


def hand_over(dq_in, dk_in, dv_in, gain_in, dq_out, dk_out, dv_out, gain_to, dq_buf, dk_buf, dv_buf, gain_buf, sems):
    trips = [
        (dk_in, dk_buf, dk_out),
        (dv_in, dv_buf, dv_out),
        (gain_in, gain_buf, gain_to),
    ]
    for i in range(HAND_PARTS):
        rows = pl.ds(i * (BLOCK // HAND_PARTS), BLOCK // HAND_PARTS)
        trips.append((dq_in.at[rows], dq_buf.at[rows], dq_out.at[rows]))
    there = [pltpu.make_async_copy(x, y, sems.at[0, i]) for i, (x, y, _) in enumerate(trips)]
    back = [pltpu.make_async_copy(y, z, sems.at[1, i]) for i, (_, y, z) in enumerate(trips)]
    for copy in there:
        copy.start()
    for arrive, leave in zip(there, back):
        arrive.wait()
        leave.start()
    for copy in back:
        copy.wait()


def body(queries, keys, values, score_gain, grad, segment_ids):
    seq_size = lax.axis_size("seq")
    dp_size = lax.axis_size("dp")
    tokens = queries.shape[1]
    factor = 1.0 / (dp_size * tokens * seq_size)
    hbm = pl.BlockSpec(memory_space=pltpu.HBM)
    heads = KEY_VALUE_HEADS
    pair = pltpu.SemaphoreType.DMA((2,))
    four = pltpu.SemaphoreType.DMA((2, 2))
    wide = GROUP * HEAD_SIZE
    dq, dk, dv, gain = pl.pallas_call(
        functools.partial(kernel, seq_size, dp_size, factor),
        out_shape=(
            jax.ShapeDtypeStruct((BLOCK, QUERY_HEADS * HEAD_SIZE), BF16),
            jax.ShapeDtypeStruct((BLOCK, heads * HEAD_SIZE), BF16),
            jax.ShapeDtypeStruct((BLOCK, heads * HEAD_SIZE), BF16),
            jax.ShapeDtypeStruct((2,), F32),
        ),
        in_specs=[hbm] * 6,
        out_specs=(hbm, hbm, hbm, pl.BlockSpec(memory_space=pltpu.SMEM)),
        scratch_shapes=[
            pltpu.VMEM((2, 2, 2 * BLOCK, wide), BF16),
            pltpu.VMEM((2, 2, 4 * BLOCK, HEAD_SIZE), BF16),
            pltpu.VMEM((2, 2, 2, BLOCK, HEAD_SIZE), BF16),
            pltpu.VMEM((heads, 2, BLOCK, HEAD_SIZE), BF16),
            pltpu.VMEM((2, 2, BLOCK, HEAD_SIZE), BF16),
            pltpu.VMEM((2, 2, BLOCK, HEAD_SIZE), BF16),
            pltpu.VMEM((2, 2, 4 * BLOCK, HEAD_SIZE), F32),
            pltpu.VMEM((2, 2, BLOCK, wide), BF16),
            pltpu.VMEM((heads, 2, BLOCK, HEAD_SIZE), BF16),
            pltpu.VMEM((4 * BLOCK, BLOCK), F32),
            pltpu.VMEM((2 * PARTS, WINDOW, BLOCK), F32),
            pltpu.VMEM((PARTS, WINDOW, LANES), F32),
            pltpu.VMEM((PARTS, WINDOW, LANES), F32),
            pltpu.VMEM((PARTS, WINDOW, LANES), F32),
            pltpu.VMEM((4, PARTS, WINDOW, LANES), BF16),
            pltpu.VMEM((4, PARTS, WINDOW, LANES), BF16),
            pltpu.VMEM((1, tokens * seq_size), jnp.int32),
            pltpu.SMEM((QUERY_HEADS,), F32),
            pltpu.VMEM((seq_size // 2, SIDE), F32),
            pltpu.VMEM((seq_size, seq_size // 2, SIDE), F32),
            pltpu.VMEM((1, 1, SIDE), F32),
            pltpu.VMEM((dp_size - 1, 1, SIDE), F32),
            pltpu.VMEM((2, 1, SIDE), F32),
            pair, pair, four, four, four, four, pair, pair,
            pair,
            pltpu.SemaphoreType.DMA((heads,)),
            pair, pair, pair, pair, pair,
            pltpu.SemaphoreType.DMA((heads, 2)),
            pair,
            pltpu.SemaphoreType.DMA((seq_size,)),
            pair, pair, pair,
            pltpu.SemaphoreType.REGULAR,
        ],
        compiler_params=pltpu.CompilerParams(
            collective_id=0, has_side_effects=True, vmem_limit_bytes=VMEM_BYTES
        ),
        cost_estimate=pl.CostEstimate(
            flops=2 * 5 * BLOCK * WINDOW * HEAD_SIZE * QUERY_HEADS,
            bytes_accessed=4 * 1024 * 1024,
            transcendentals=BLOCK * WINDOW * QUERY_HEADS,
        ),
    )(queries[0], keys[0], values[0], score_gain, grad[0], segment_ids)
    results = (dq, dk, dv, gain)
    dq, dk, dv, gain = pl.pallas_call(
        hand_over,
        out_shape=tuple(jax.ShapeDtypeStruct(x.shape, x.dtype) for x in results),
        in_specs=[hbm] * 4,
        out_specs=(hbm,) * 4,
        scratch_shapes=[
            *[pltpu.VMEM(x.shape, x.dtype) for x in results[:3]],
            pltpu.SMEM(gain.shape, gain.dtype),
            pltpu.SemaphoreType.DMA((2, HAND_PARTS + 3)),
        ],
        compiler_params=pltpu.CompilerParams(vmem_limit_bytes=VMEM_BYTES),
    )(*results)
    return dq[None], dk[None], dv[None], gain


def solution(mesh):
    return jax.shard_map(
        body,
        mesh=mesh,
        in_specs=(
            P("dp", "seq", None),
            P("dp", "seq", None),
            P("dp", "seq", None),
            P(),
            P("dp", "seq", None),
            P("dp", None),
        ),
        out_specs=(P("dp", "seq", None), P("dp", "seq", None), P("dp", "seq", None), P("seq")),
        check_vma=False,
    )
```

```python
import functools
import math

import jax
import jax.numpy as jnp
from jax import lax
from jax.experimental import pallas as pl
from jax.experimental.pallas import tpu as pltpu
from jax.sharding import PartitionSpec as P

QUERY_HEADS = 32
KEY_VALUE_HEADS = 4
HEAD_SIZE = 128
GROUP = QUERY_HEADS // KEY_VALUE_HEADS
BLOCK = 128
PART = 32
PARTS = BLOCK // PART
WINDOW = 288
LANES = GROUP * PART
SIDE = 128
CHUNK = 32
HAND_PARTS = 8
LEADER = 7
VMEM_BYTES = 64 * 1024 * 1024
LOG2E = math.log2(math.e)
SCALE = HEAD_SIZE ** -0.5
BF16 = jnp.bfloat16
F32 = jnp.float32
NT = (((1,), (1,)), ((), ()))
TN = (((0,), (0,)), ((), ()))


def fold_rows(x):
    return jnp.sum(x.reshape(x.shape[0] // 8, 8, x.shape[1]), axis=0)


def kernel(
    seq_size, dp_size, factor,
    q_hbm, k_hbm, v_hbm, gain_hbm, g_hbm, seg_hbm,
    dq_hbm, dk_hbm, dv_hbm, gain_out,
    qg, kv, ret_send, ret, mate_send, mate_in, acc, dq_buf, dkv_buf, seg_rows, bias,
    s_buf, dp_buf, y_buf, p_buf, ds_buf, seg_ref, gain_ref,
    g_part, g_in1, g_sum, g_in2, g_total,
    in_sem, own_sem, halo_send, halo_recv, mate_kv_send, mate_kv_recv, mate_qg_send, mate_qg_recv,
    back_send, back_recv, mate_back_send, mate_back_recv, dq_sem, mate_dq_send, mate_dq_recv,
    dkv_sem, gain1_send, gain1_recv, gain2_sem, gain3_sem, small_sem, ready,
):
    me = lax.axis_index("seq")
    row = lax.axis_index("dp")
    chips = seq_size // 2
    chip = lax.div(me, 2)
    core = me - 2 * chip
    other = 1 - core
    mate = 2 * chip + other
    next_chip = lax.rem(chip + 1, chips)
    last_chip = lax.rem(chip + chips - 1, chips)

    def thin(head):
        return pl.ds(pl.multiple_of(head * HEAD_SIZE, HEAD_SIZE), HEAD_SIZE)

    def wide(head):
        return pl.ds(pl.multiple_of(head * (GROUP * HEAD_SIZE), GROUP * HEAD_SIZE), GROUP * HEAD_SIZE)

    def block(index):
        return pl.ds(pl.multiple_of(index * BLOCK, BLOCK), BLOCK)

    def remote(source, target, send, recv, device):
        return pltpu.make_async_remote_copy(
            src_ref=source,
            dst_ref=target,
            send_sem=send,
            recv_sem=recv,
            device_id={"seq": device},
            device_id_type=pl.DeviceIdType.MESH,
        )

    barrier = pltpu.get_barrier_semaphore()

    def greet_seq(i, carry):
        there = lax.rem(me - i + seq_size, seq_size)

        @pl.when(there != LEADER)
        def _():
            pl.semaphore_signal(
                barrier, inc=1, device_id={"seq": there}, device_id_type=pl.DeviceIdType.MESH
            )

        return carry

    def greet_dp(i, carry):
        pl.semaphore_signal(
            barrier, inc=1, device_id={"dp": lax.rem(row + i, dp_size)}, device_id_type=pl.DeviceIdType.MESH
        )
        return carry

    lax.fori_loop(1, seq_size, greet_seq, 0)

    @pl.when(me == LEADER)
    def _():
        lax.fori_loop(1, dp_size, greet_dp, 0)

    for a in range(2):
        head = 2 * core + a
        pltpu.make_async_copy(k_hbm.at[:, thin(head)], kv.at[a, 0, block(2 + core)], own_sem.at[a]).start()
        pltpu.make_async_copy(v_hbm.at[:, thin(head)], kv.at[a, 1, block(2 + core)], own_sem.at[a]).start()
        pltpu.make_async_copy(q_hbm.at[:, wide(head)], qg.at[a, 0, pl.ds(0, BLOCK)], in_sem.at[a]).start()
        pltpu.make_async_copy(g_hbm.at[:, wide(head)], qg.at[a, 1, pl.ds(0, BLOCK)], in_sem.at[a]).start()
    seg_copy = pltpu.make_async_copy(seg_hbm, seg_ref, small_sem.at[0])
    gain_copy = pltpu.make_async_copy(gain_hbm, gain_ref, small_sem.at[1])
    seg_copy.start()
    gain_copy.start()

    @pl.when(me != LEADER)
    def _():
        pl.semaphore_wait(barrier, seq_size - 1)
        pl.semaphore_signal(
            ready, inc=1, device_id={"seq": LEADER}, device_id_type=pl.DeviceIdType.MESH
        )

    @pl.when(me == LEADER)
    def _():
        pl.semaphore_wait(ready, seq_size - 1)

    def halo_start(a):
        for which, source in enumerate((k_hbm, v_hbm)):
            for to_core in range(2):
                remote(
                    source.at[:, thin(2 * to_core + a)],
                    kv.at[a, which, block(core)],
                    halo_send.at[a, which],
                    halo_recv.at[a, which],
                    2 * next_chip + to_core,
                ).start()

    def halo_whole(a, which):
        part = kv.at[a, which, pl.ds(0, 2 * BLOCK)]
        return remote(part, part, halo_send.at[a, which], halo_recv.at[a, which], 2 * next_chip)

    def mate_start(a):
        head = 2 * other + a
        for which, source in enumerate((k_hbm, v_hbm)):
            remote(
                source.at[:, thin(head)], kv.at[a, which, block(2 + core)],
                mate_kv_send.at[a, which], mate_kv_recv.at[a, which], mate,
            ).start()

    def mate_queries_start(a):
        head = 2 * other + a
        for which, source in enumerate((q_hbm, g_hbm)):
            remote(
                source.at[:, wide(head)], qg.at[a, which, pl.ds(BLOCK, BLOCK)],
                mate_qg_send.at[a], mate_qg_recv.at[a], mate,
            ).start()

    def mate_kv(a, which):
        part = kv.at[a, which, block(2 + other)]
        return remote(part, part, mate_kv_send.at[a, which], mate_kv_recv.at[a, which], mate)

    def mate_qg(a):
        part = qg.at[a, :, pl.ds(BLOCK, BLOCK)]
        return remote(part, part, mate_qg_send.at[a], mate_qg_recv.at[a], mate)

    halo_start(0)
    mate_start(0)
    mate_queries_start(0)
    mate_start(1)
    acc[...] = jnp.zeros(acc.shape, F32)
    seg_copy.wait()
    gain_copy.wait()

    def ids_of(index):
        place = pl.multiple_of(lax.rem(2 * chip + index + seq_size, seq_size) * BLOCK, BLOCK)
        return seg_ref[:, pl.ds(place, BLOCK)].astype(F32)

    for b in range(4):
        seg_rows[pl.ds(b * BLOCK, BLOCK)] = jnp.transpose(
            jnp.broadcast_to(ids_of(b - 2), (BLOCK, BLOCK))
        )
    def block_of(late):
        return other if late else core

    group8 = lax.broadcasted_iota(jnp.int32, (8, BLOCK), 1) // PART
    key_place = lax.broadcasted_iota(jnp.int32, (WINDOW, BLOCK), 0)
    lane = lax.broadcasted_iota(jnp.int32, (WINDOW, BLOCK), 1)
    causal = key_place <= 2 * BLOCK + lane % PART
    for late in range(2):
        x = block_of(late)
        query_ids = jnp.broadcast_to(ids_of(x), (8, BLOCK))
        rolled = [query_ids] + [pltpu.roll(query_ids, PART * k, 1) for k in range(1, PARTS)]
        for part in range(PARTS):
            start = x * BLOCK + part * PART
            ids = rolled[-part % PARTS]
            for j in range(1, PARTS):
                ids = jnp.where(group8 == j, rolled[(j - part) % PARTS], ids)
            inside = (chip - 1) * (2 * BLOCK) + start + key_place >= 0
            keys_ids = seg_rows[pl.ds(pl.multiple_of(start, PART), WINDOW)]
            allowed = (keys_ids == ids[0:1]) & causal & inside
            bias[late * PARTS + part] = jnp.where(allowed, 0.0, -1e30)

    lane_wide = lax.broadcasted_iota(jnp.int32, (1, LANES), 1)

    def back_copy(a, place):
        return remote(
            ret_send.at[a, place], ret.at[2 * core + a],
            back_send.at[a], back_recv.at[2 * core + a], 2 * last_chip + place,
        )

    def back_whole(a):
        return remote(ret_send.at[a], ret_send.at[a], back_send.at[a], back_recv.at[a], 2 * last_chip)

    def back_from(head):
        return remote(ret.at[head], ret.at[head], back_send.at[0], back_recv.at[head], 2 * last_chip)

    def mate_back(a):
        return remote(
            mate_send.at[a], mate_in.at[a], mate_back_send.at[a], mate_back_recv.at[a], mate
        )

    def dkv_out(head, which):
        target = (dk_hbm, dv_hbm)[which]
        return pltpu.make_async_copy(
            dkv_buf.at[head, which], target.at[:, thin(head)], dkv_sem.at[head, which]
        )

    def finish(a):
        mine = 2 * core + a
        theirs = 2 * other + a
        back_from(mine).wait_recv()
        for which in range(2):
            total = acc[a, which, block(2 + core)] + ret[mine, which].astype(F32)
            dkv_buf[mine, which] = total.astype(BF16)
            dkv_out(mine, which).start()
        mate_back(a).wait_recv()
        back_from(theirs).wait_recv()
        for which in range(2):
            total = mate_in[a, which].astype(F32) + ret[theirs, which].astype(F32)
            dkv_buf[theirs, which] = total.astype(BF16)
            dkv_out(theirs, which).start()

    def dq_own(a):
        return pltpu.make_async_copy(dq_buf.at[a, 0], dq_hbm.at[:, wide(2 * core + a)], dq_sem.at[a])

    def dq_mate(a):
        return remote(
            dq_buf.at[a, 1], dq_hbm.at[:, wide(2 * core + a)], mate_dq_send.at[a], mate_dq_recv.at[a], mate
        )

    def dq_from(a):
        part = dq_hbm.at[:, wide(2 * other + a)]
        return remote(part, part, mate_dq_send.at[a], mate_dq_recv.at[a], mate)

    def gain_copy1(source):
        return remote(g_part, g_in1.at[source], gain1_send.at[0], gain1_recv.at[source], LEADER)

    def gain_copy3(target):
        return remote(g_total.at[0], g_total.at[1], gain3_sem.at[0], gain3_sem.at[1], target)

    def key_rows(late, part):
        return pl.ds(pl.multiple_of(block_of(late) * BLOCK + part * PART, PART), WINDOW)

    def stack(a, late, which, part):
        rows = pl.ds(late * BLOCK + part * PART, PART)
        return jnp.concatenate(
            [qg[a, which, rows, pl.ds(h * HEAD_SIZE, HEAD_SIZE)] for h in range(GROUP)], axis=0
        )

    def scores(late, a):
        gain = jnp.full((1, LANES), gain_ref[(2 * core + a) * GROUP], F32)
        for h in range(1, GROUP):
            gain = jnp.where(lane_wide >= h * PART, gain_ref[(2 * core + a) * GROUP + h], gain)
        to_score = gain * (SCALE * LOG2E)
        to_grad = gain * SCALE

        def product(target, which, u):
            target[u] = lax.dot_general(
                kv[a, which, key_rows(late, u)], stack(a, late, which, u), NT,
                preferred_element_type=F32,
            )

        def middle(u):
            chunks = [pl.ds(i, CHUNK) for i in range(0, WINDOW, CHUNK)]
            top = jnp.full((8, LANES), -3e38, F32)
            for rows in chunks:
                shade = bias[late * PARTS + u, rows]
                y = s_buf[u, rows] * to_score + jnp.concatenate([shade, shade], axis=1)
                y_buf[u, rows] = y
                top = jnp.maximum(top, jnp.max(y.reshape(CHUNK // 8, 8, LANES), axis=0))
            top = jnp.max(top, axis=0, keepdims=True)
            total = jnp.zeros((8, LANES), F32)
            dot = jnp.zeros((8, LANES), F32)
            for rows in chunks:
                e = jnp.exp2(y_buf[u, rows] - top)
                y_buf[u, rows] = e
                total = total + fold_rows(e)
                dot = dot + fold_rows(e * dp_buf[u, rows])
            inverse = 1.0 / jnp.sum(total, axis=0, keepdims=True)
            delta = jnp.sum(dot, axis=0, keepdims=True) * inverse
            spread = jnp.zeros((8, LANES), F32)
            for rows in chunks:
                p = y_buf[u, rows] * inverse
                dscore = p * (dp_buf[u, rows] - delta)
                spread = spread + fold_rows(dscore * s_buf[u, rows])
                p_buf[2 * a + late, u, rows] = p.astype(BF16)
                ds_buf[2 * a + late, u, rows] = (dscore * to_grad).astype(BF16)
            return jnp.sum(spread, axis=0, keepdims=True) * (SCALE * factor)

        if late:
            mate_qg(a).wait_recv()
        else:
            own = kv.at[a, :, block(2 + core)]
            pltpu.make_async_copy(own, own, own_sem.at[a]).wait()
            held = qg.at[a, :, pl.ds(0, BLOCK)]
            pltpu.make_async_copy(held, held, in_sem.at[a]).wait()
            mate_kv(a, 0).wait_recv()
            halo_whole(a, 0).wait_recv()

            @pl.when(a == 0)
            def _():
                halo_start(1)

        for u in range(PARTS):
            product(s_buf, 0, u)
        if not late:
            mate_kv(a, 1).wait_recv()
            halo_whole(a, 1).wait_recv()

            @pl.when(a == 0)
            def _():
                mate_queries_start(1)

        product(dp_buf, 1, 0)
        terms = jnp.zeros((1, LANES), F32)
        for u in range(PARTS):
            if u + 1 < PARTS:
                product(dp_buf, 1, u + 1)
            terms = terms + middle(u)
        for side in range(2):
            g_part[pl.ds(2 * a + side, 1), :] += terms[:, side * SIDE:(side + 1) * SIDE]

    def own_scores(a, carry):
        scores(0, a)
        return carry

    def mate_scores(a, carry):
        scores(1, a)
        return carry

    g_part[...] = jnp.zeros(g_part.shape, F32)
    lax.fori_loop(0, 2, own_scores, 0)
    lax.fori_loop(0, 2, mate_scores, 0)

    @pl.when(me != LEADER)
    def _():
        gain_copy1(me).start()

    def gain_arrive(i, carry):
        @pl.when(i != LEADER)
        def _():
            gain_copy1(i).wait_recv()

        return carry

    def gain_send2(target, carry):
        offset = lax.rem(target - row + dp_size, dp_size)

        @pl.when(offset != 0)
        def _():
            pltpu.make_async_remote_copy(
                src_ref=g_sum.at[0],
                dst_ref=g_in2.at[offset - 1],
                send_sem=gain2_sem.at[0],
                recv_sem=gain2_sem.at[1],
                device_id={"dp": target},
                device_id_type=pl.DeviceIdType.MESH,
            ).start()

        return carry

    @pl.when(me == LEADER)
    def _():
        g_in1[LEADER] = g_part[...]
        lax.fori_loop(0, seq_size, gain_arrive, 0)
        row_of = lax.broadcasted_iota(jnp.int32, (chips, SIDE), 0)
        lanes = lax.broadcasted_iota(jnp.int32, (chips, SIDE), 1)
        sums = jnp.zeros((chips, SIDE), F32)
        for side in range(2):
            held = g_in1[side]
            for i in range(1, chips):
                held = held + g_in1[2 * i + side]
            for h in range(PARTS):
                head_sum = jnp.sum(jnp.where(lanes // PART == h, held, 0.0), axis=1, keepdims=True)
                place = (QUERY_HEADS // 2) * side + PARTS * row_of + h
                sums = sums + jnp.where((lanes == place) & (row_of < PARTS), head_sum, 0.0)
        g_sum[0] = jnp.sum(sums, axis=0, keepdims=True)
        pl.semaphore_wait(barrier, dp_size - 1)
        lax.fori_loop(0, dp_size, gain_send2, 0)

    def key_side(a, carry):
        for late in range(2):
            for part in range(PARTS):
                rows = key_rows(late, part)
                acc[a, 0, rows] += jnp.dot(
                    ds_buf[2 * a + late, part], stack(a, late, 0, part), preferred_element_type=F32
                )
                acc[a, 1, rows] += jnp.dot(
                    p_buf[2 * a + late, part], stack(a, late, 1, part), preferred_element_type=F32
                )
        for place in range(2):
            for which in range(2):
                ret_send[a, place, which] = acc[a, which, pl.ds(place * BLOCK, BLOCK)].astype(BF16)
            back_copy(a, place).start()
        for which in range(2):
            mate_send[a, which] = acc[a, which, block(2 + other)].astype(BF16)
        mate_back(a).start()
        return carry

    lax.fori_loop(0, 2, key_side, 0)

    def query_side(a, carry):
        for late in (1, 0):
            for part in range(PARTS):
                turned_keys = jnp.transpose(kv[a, 0, key_rows(late, part)])
                dq = jnp.dot(turned_keys, ds_buf[2 * a + late, part], preferred_element_type=F32)
                dq = jnp.transpose(dq.astype(BF16))
                for h in range(GROUP):
                    dq_buf[
                        a, late, pl.ds(part * PART, PART), pl.ds(h * HEAD_SIZE, HEAD_SIZE)
                    ] = dq[h * PART:(h + 1) * PART]
            if late:
                dq_mate(a).start()
            else:
                dq_own(a).start()
        return carry

    lax.fori_loop(0, 2, query_side, 0)
    finish(0)
    finish(1)
    gain2_whole = remote(g_in2, g_in2, gain2_sem.at[0], gain2_sem.at[1], mate)

    def gain_send3(target, carry):
        @pl.when(target != LEADER)
        def _():
            gain_copy3(target).start()

        return carry

    @pl.when(me == LEADER)
    def _():
        gain2_whole.wait_recv()
        g_total[0] = g_sum[0] + jnp.sum(g_in2[...], axis=0)
        lax.fori_loop(0, seq_size, gain_send3, 0)
        g_total[1] = g_total[0]

    @pl.when(me != LEADER)
    def _():
        gain_copy3(mate).wait_recv()

    lane1 = lax.broadcasted_iota(jnp.int32, (1, SIDE), 1)
    for side in range(2):
        gain_out[side] = jnp.sum(jnp.where(lane1 == 2 * me + side, g_total[1], 0.0))

    @pl.when(me == LEADER)
    def _():
        gain2_whole.wait_send()
        sent = g_in2.at[pl.ds(0, seq_size - 1)]
        remote(sent, sent, gain3_sem.at[0], gain3_sem.at[1], mate).wait_send()

    @pl.when(me != LEADER)
    def _():
        gain_copy1(me).wait_send()

    for a in range(2):
        for which in range(2):
            halo_whole(a, which).wait_send()
            mate_kv(a, which).wait_send()
        mate_qg(a).wait_send()
        back_whole(a).wait_send()
        mate_back(a).wait_send()
        dq_own(a).wait()
        dq_mate(a).wait_send()
        dq_from(a).wait_recv()
    for head in range(KEY_VALUE_HEADS):
        for which in range(2):
            dkv_out(head, which).wait()


def hand_over(dq_in, dk_in, dv_in, gain_in, dq_out, dk_out, dv_out, gain_to, dq_buf, dk_buf, dv_buf, gain_buf, sems):
    trips = [
        (dk_in, dk_buf, dk_out),
        (dv_in, dv_buf, dv_out),
        (gain_in, gain_buf, gain_to),
    ]
    for i in range(HAND_PARTS):
        rows = pl.ds(i * (BLOCK // HAND_PARTS), BLOCK // HAND_PARTS)
        trips.append((dq_in.at[rows], dq_buf.at[rows], dq_out.at[rows]))
    there = [pltpu.make_async_copy(x, y, sems.at[0, i]) for i, (x, y, _) in enumerate(trips)]
    back = [pltpu.make_async_copy(y, z, sems.at[1, i]) for i, (_, y, z) in enumerate(trips)]
    for copy in there:
        copy.start()
    for arrive, leave in zip(there, back):
        arrive.wait()
        leave.start()
    for copy in back:
        copy.wait()


def body(queries, keys, values, score_gain, grad, segment_ids):
    seq_size = lax.axis_size("seq")
    dp_size = lax.axis_size("dp")
    tokens = queries.shape[1]
    factor = 1.0 / (dp_size * tokens * seq_size)
    hbm = pl.BlockSpec(memory_space=pltpu.HBM)
    heads = KEY_VALUE_HEADS
    pair = pltpu.SemaphoreType.DMA((2,))
    four = pltpu.SemaphoreType.DMA((2, 2))
    wide = GROUP * HEAD_SIZE
    dq, dk, dv, gain = pl.pallas_call(
        functools.partial(kernel, seq_size, dp_size, factor),
        out_shape=(
            jax.ShapeDtypeStruct((BLOCK, QUERY_HEADS * HEAD_SIZE), BF16),
            jax.ShapeDtypeStruct((BLOCK, heads * HEAD_SIZE), BF16),
            jax.ShapeDtypeStruct((BLOCK, heads * HEAD_SIZE), BF16),
            jax.ShapeDtypeStruct((2,), F32),
        ),
        in_specs=[hbm] * 6,
        out_specs=(hbm, hbm, hbm, pl.BlockSpec(memory_space=pltpu.SMEM)),
        scratch_shapes=[
            pltpu.VMEM((2, 2, 2 * BLOCK, wide), BF16),
            pltpu.VMEM((2, 2, 4 * BLOCK, HEAD_SIZE), BF16),
            pltpu.VMEM((2, 2, 2, BLOCK, HEAD_SIZE), BF16),
            pltpu.VMEM((heads, 2, BLOCK, HEAD_SIZE), BF16),
            pltpu.VMEM((2, 2, BLOCK, HEAD_SIZE), BF16),
            pltpu.VMEM((2, 2, BLOCK, HEAD_SIZE), BF16),
            pltpu.VMEM((2, 2, 4 * BLOCK, HEAD_SIZE), F32),
            pltpu.VMEM((2, 2, BLOCK, wide), BF16),
            pltpu.VMEM((heads, 2, BLOCK, HEAD_SIZE), BF16),
            pltpu.VMEM((4 * BLOCK, BLOCK), F32),
            pltpu.VMEM((2 * PARTS, WINDOW, BLOCK), F32),
            pltpu.VMEM((PARTS, WINDOW, LANES), F32),
            pltpu.VMEM((PARTS, WINDOW, LANES), F32),
            pltpu.VMEM((PARTS, WINDOW, LANES), F32),
            pltpu.VMEM((4, PARTS, WINDOW, LANES), BF16),
            pltpu.VMEM((4, PARTS, WINDOW, LANES), BF16),
            pltpu.VMEM((1, tokens * seq_size), jnp.int32),
            pltpu.SMEM((QUERY_HEADS,), F32),
            pltpu.VMEM((seq_size // 2, SIDE), F32),
            pltpu.VMEM((seq_size, seq_size // 2, SIDE), F32),
            pltpu.VMEM((1, 1, SIDE), F32),
            pltpu.VMEM((dp_size - 1, 1, SIDE), F32),
            pltpu.VMEM((2, 1, SIDE), F32),
            pair, pair, four, four, four, four, pair, pair,
            pair,
            pltpu.SemaphoreType.DMA((heads,)),
            pair, pair, pair, pair, pair,
            pltpu.SemaphoreType.DMA((heads, 2)),
            pair,
            pltpu.SemaphoreType.DMA((seq_size,)),
            pair, pair, pair,
            pltpu.SemaphoreType.REGULAR,
        ],
        compiler_params=pltpu.CompilerParams(
            collective_id=0, has_side_effects=True, vmem_limit_bytes=VMEM_BYTES
        ),
        cost_estimate=pl.CostEstimate(
            flops=2 * 5 * BLOCK * WINDOW * HEAD_SIZE * QUERY_HEADS,
            bytes_accessed=4 * 1024 * 1024,
            transcendentals=BLOCK * WINDOW * QUERY_HEADS,
        ),
    )(queries[0], keys[0], values[0], score_gain, grad[0], segment_ids)
    results = (dq, dk, dv, gain)
    dq, dk, dv, gain = pl.pallas_call(
        hand_over,
        out_shape=tuple(jax.ShapeDtypeStruct(x.shape, x.dtype) for x in results),
        in_specs=[hbm] * 4,
        out_specs=(hbm,) * 4,
        scratch_shapes=[
            *[pltpu.VMEM(x.shape, x.dtype) for x in results[:3]],
            pltpu.SMEM(gain.shape, gain.dtype),
            pltpu.SemaphoreType.DMA((2, HAND_PARTS + 3)),
        ],
        compiler_params=pltpu.CompilerParams(vmem_limit_bytes=VMEM_BYTES),
    )(*results)
    return dq[None], dk[None], dv[None], gain


def solution(mesh):
    return jax.shard_map(
        body,
        mesh=mesh,
        in_specs=(
            P("dp", "seq", None),
            P("dp", "seq", None),
            P("dp", "seq", None),
            P(),
            P("dp", "seq", None),
            P("dp", None),
        ),
        out_specs=(P("dp", "seq", None), P("dp", "seq", None), P("dp", "seq", None), P("seq")),
        check_vma=False,
    )
```
